128 devices in a mesh: seq: 16 (over z, y_lo, core), head: 8 (over x, y_hi).
Axes of the slice: x: 4, y: 4 (y_hi: 2, y_lo: 2; y = y_hi * 2 + y_lo), z: 4, core: 2. Of those that a mesh axis runs over, the one named last changes fastest.
Arguments:
- inputs: bfloat16 [2, 2048, 2048], P(None, 'seq'), may hold values from -6 to 6
- cotangent: bfloat16 [2, 2048, 2048], P(None, 'seq'), may hold values from -6 to 6
- lengths: int32 [2], replicated, may hold values from 1024 to 2048, as said below
- attn_gain: bfloat16 [2048], P('seq'), may hold values from 0.5 to 1.5
- w_query: bfloat16 [2048, 2048], P('seq', 'head'), may hold values from -0.0625 to 0.0625
- w_key: bfloat16 [2048, 2048], P('seq', 'head'), may hold values from -0.0625 to 0.0625
- w_value: bfloat16 [2048, 2048], P('seq', 'head'), may hold values from -0.125 to 0.125
- w_out: bfloat16 [2048, 2048], P('head', 'seq'), may hold values from -0.5 to 0.5
- bias_table: bfloat16 [32, 32], P('seq', 'head'), may hold values from -4 to 4
- ffn_gain: bfloat16 [2048], P('seq'), may hold values from 0.5 to 1.5
- w_gate: bfloat16 [2048, 5120], P('seq', 'head'), may hold values from -0.125 to 0.125
- w_up: bfloat16 [2048, 5120], P('seq', 'head'), may hold values from -0.125 to 0.125
- w_down: bfloat16 [5120, 2048], P('head', 'seq'), may hold values from -0.078125 to 0.078125
Outputs:
- layer_out: bfloat16 [2, 2048, 2048], P(None, 'seq')
- input_grad: float32 [2, 2048, 2048], P(None, 'seq')
- attn_gain_grad: float32 [2048], P('seq')
- query_weight_grad: float32 [2048, 2048], P('seq', 'head')
- key_weight_grad: float32 [2048, 2048], P('seq', 'head')
- value_weight_grad: float32 [2048, 2048], P('seq', 'head')
- out_weight_grad: float32 [2048, 2048], P('head', 'seq')
- table_grad: float32 [32, 32], P('seq', 'head')
- ffn_gain_grad: float32 [2048], P('seq')
- gate_weight_grad: float32 [2048, 5120], P('seq', 'head')
- up_weight_grad: float32 [2048, 5120], P('seq', 'head')
- down_weight_grad: float32 [5120, 2048], P('head', 'seq')
The draws below stay inside these ranges and needn't reach their ends.
Inputs may be any that keep to these rules, and one draw needn't show every extreme that they name: `lengths`: each length lies between 1024 and 2048; one sequence of every draw has all 2048 slots live.
All inputs are finite; a program needn't handle non-finite values.
Results may differ from the reference program's by a relative error of at most 0.039.
Values may be sent and summed in bfloat16 or wider, within the bound.
No kernel may reach another device: no remote copies, remote signals or barrier semaphores. Data moves between devices by JAX's collectives and lax.ppermute only.
A program may use at most 192 MiB of HBM per device.

```python
from functools import partial
import jax
import jax.numpy as jnp
from jax import lax

D = 2048
HEADS = 32
HEAD = 64
FF = 5120
BUCKETS = 32
SEQS = 2
LEN = 2048


def draw_lengths(key, part):
    key = jax.random.fold_in(key, 7)
    first_key, second_key = jax.random.split(key)
    drawn = jax.random.randint(first_key, (SEQS,), LEN // 2, LEN + 1)
    chosen = jax.random.randint(second_key, (), 0, SEQS)
    return jnp.where(jnp.arange(SEQS) == chosen, LEN, drawn).astype(jnp.int32)


def levels(own_key, extent, cuts, least, largest):
    gain = 1.0
    for axis_at, parts in cuts:
        draws = jax.random.uniform(jax.random.fold_in(jax.random.fold_in(own_key, 6), axis_at), (parts,), jnp.float32, least / len(cuts), largest / len(cuts))
        gain = gain * jnp.repeat(jnp.exp(draws), extent[axis_at] // parts).reshape((-1,) + (1,) * (len(extent) - 1 - axis_at))
    return gain


def scatter_about(stream_key, shape, scale, most, cuts=(), held_as=jnp.bfloat16):
    values = scale * jax.random.normal(stream_key, shape, jnp.float32)
    if cuts:
        values = values * levels(stream_key, shape, cuts, -0.22, 0.18)
    return jnp.clip(values, -most, most).astype(held_as)


def setup_inputs(seed: int = 0) -> dict:
    arg_keys = jax.random.split(jax.random.key(seed), 14)
    inputs = scatter_about(arg_keys[0], (SEQS, LEN, D), 1.0, 6.0, ((1, 16),))
    cotangent = scatter_about(arg_keys[1], (SEQS, LEN, D), 1.0, 6.0, ((1, 16),))
    lengths = draw_lengths(jax.random.fold_in(arg_keys[13], 71), 0)
    attn_gain = jnp.clip(1.0 + 0.1 * jax.random.normal(arg_keys[3], (D,), jnp.float32), 0.5, 1.5).astype(jnp.bfloat16)
    w_query = scatter_about(arg_keys[4], (D, HEADS * HEAD), (4 * D) ** -0.5, 0.0625, ((0, 16), (1, 8)))
    w_key = scatter_about(arg_keys[5], (D, HEADS * HEAD), (4 * D) ** -0.5, 0.0625, ((0, 16), (1, 8)))
    w_value = scatter_about(arg_keys[6], (D, HEADS * HEAD), D ** -0.5, 0.125, ((0, 16), (1, 8)))
    w_out = scatter_about(arg_keys[7], (HEADS * HEAD, D), (HEADS * HEAD // 16) ** -0.5, 0.5, ((0, 8), (1, 16)))
    bias_table = scatter_about(arg_keys[8], (BUCKETS, HEADS), 1.0, 4.0, ((0, 16), (1, 8)))
    ffn_gain = jnp.clip(1.0 + 0.1 * jax.random.normal(arg_keys[9], (D,), jnp.float32), 0.5, 1.5).astype(jnp.bfloat16)
    w_gate = scatter_about(arg_keys[10], (D, FF), D ** -0.5, 0.125, ((0, 16), (1, 8)))
    w_up = scatter_about(arg_keys[11], (D, FF), D ** -0.5, 0.125, ((0, 16), (1, 8)))
    w_down = scatter_about(arg_keys[12], (FF, D), FF ** -0.5, 0.078125, ((0, 8), (1, 16)))
    return {"inputs": inputs, "cotangent": cotangent, "lengths": lengths, "attn_gain": attn_gain, "w_query": w_query, "w_key": w_key, "w_value": w_value, "w_out": w_out, "bias_table": bias_table, "ffn_gain": ffn_gain, "w_gate": w_gate, "w_up": w_up, "w_down": w_down}


@jax.custom_vjp
def low(v):
    return lax.optimization_barrier(v.astype(jnp.bfloat16)).astype(jnp.float32)

@jax.custom_vjp
def low_back(v):
    return v

def low_keep(v):
    return (low(v), None)

def low_pass(kept, grad):
    return (grad,)

def back_keep(v):
    return (v, None)

def back_low(kept, grad):
    return (low(grad),)
low.defvjp(low_keep, low_pass)
low_back.defvjp(back_keep, back_low)
epsilon = 1e-06
limits = (8, 12, 16, 23, 32, 46, 64, 91)
masked_score = -1000000000.0

def bucket_ids(offset):
    distance = jnp.where(offset < 0, -offset, offset)
    coarse = 7 + sum(((distance >= threshold).astype(jnp.int32) for threshold in limits))
    within = jnp.where(distance < 8, distance, coarse)
    return within + jnp.where(offset > 0, 16, 0).astype(jnp.int32)

def rms_scale(row_block, scale_gain):
    return row_block * lax.rsqrt(lax.optimization_barrier(jnp.mean(row_block * row_block, axis=-1, keepdims=True)) + epsilon) * scale_gain

def gated_gelu(gate_rows, up_rows):
    return jax.nn.gelu(gate_rows, approximate=True) * up_rows

def highest(former, latter):
    return jnp.dot(former, latter, precision=lax.Precision.HIGHEST)

def attend(queries, all_keys, all_values, bias_table, length):
    block_rows = min(512, LEN)
    key_places = jnp.arange(LEN, dtype=jnp.int32)

    def one_block(first_row, queries, all_keys, all_values, bias_table, length):
        query_block = lax.dynamic_slice_in_dim(queries, first_row, block_rows, 0)
        query_places = first_row + jnp.arange(block_rows, dtype=jnp.int32)
        rel_bias = jnp.moveaxis(bias_table[bucket_ids(key_places[None, :] - query_places[:, None])], 2, 0)
        raw_scores = jnp.einsum('qhd,khd->hqk', query_block, all_keys, precision=lax.Precision.HIGHEST) + rel_bias
        raw_scores = low_back(raw_scores)
        scores = jnp.where(key_places[None, None, :] < length, raw_scores, masked_score)
        row_max = lax.optimization_barrier(jnp.max(scores, axis=2, keepdims=True))
        weights_exp = jnp.exp(scores - row_max)
        probabilities = low(weights_exp / lax.optimization_barrier(jnp.sum(weights_exp, axis=2, keepdims=True)))
        return jnp.einsum('hqk,khd->qhd', probabilities, all_values, precision=lax.Precision.HIGHEST)
    checked = jax.checkpoint(one_block)
    starts = jnp.arange(LEN // block_rows, dtype=jnp.int32) * block_rows
    pieces = lax.map(lambda first_row: checked(first_row, queries, all_keys, all_values, bias_table, length), starts)
    return pieces.reshape(LEN, HEADS * HEAD)

def forward(lengths, inputs, attn_gain, w_query, w_key, w_value, w_out, bias_table, ffn_gain, w_gate, w_up, w_down):
    rows_in = inputs.reshape(SEQS * LEN, D)
    normed_one = low(rms_scale(rows_in, attn_gain))
    queries = low_back(low(highest(normed_one, w_query)))
    all_keys = low_back(low(highest(normed_one, w_key)))
    all_values = low_back(low(highest(normed_one, w_value)))
    head_shape = (SEQS, LEN, HEADS, HEAD)

    def per_sequence(members):
        return jax.checkpoint(attend)(members[0], members[1], members[2], bias_table, members[3])
    mixed_rows = lax.map(per_sequence, (queries.reshape(head_shape), all_keys.reshape(head_shape), all_values.reshape(head_shape), lengths))
    mixed_rows = low_back(low(mixed_rows.reshape(SEQS * LEN, HEADS * HEAD)))
    attn_rows = low_back(highest(mixed_rows, w_out))
    hidden_in = rows_in + attn_rows
    normed_two = low(rms_scale(hidden_in, ffn_gain))
    gate_rows = low_back(highest(normed_two, w_gate))
    up_rows = low_back(highest(normed_two, w_up))
    hidden = low(gated_gelu(gate_rows, up_rows))
    ffn_rows = low_back(highest(hidden, w_down))
    return (hidden_in + ffn_rows).reshape(SEQS, LEN, D)

def reference(inputs, cotangent, lengths, attn_gain, w_query, w_key, w_value, w_out, bias_table, ffn_gain, w_gate, w_up, w_down):
    floats = tuple((member.astype(jnp.float32) for member in (inputs, attn_gain, w_query, w_key, w_value, w_out, bias_table, ffn_gain, w_gate, w_up, w_down)))
    result, pull_back = jax.vjp(partial(forward, lengths), *floats)
    live = jnp.arange(LEN, dtype=jnp.int32)[None, :] < lengths[:, None]
    seed_grad = jnp.where(live[:, :, None], cotangent.astype(jnp.float32), 0.0)
    gradients = pull_back(seed_grad)
    return (result.astype(jnp.bfloat16), gradients[0], gradients[1], gradients[2], gradients[3], gradients[4], gradients[5], gradients[6], gradients[7], gradients[8], gradients[9], gradients[10])
```

```python
import functools

import jax
import jax.numpy as jnp
from jax import lax
from jax.experimental import pallas as pl
from jax.experimental.pallas import tpu as pltpu
from jax.sharding import PartitionSpec as P


D = 2048
HEAD = 64
BUCKETS = 32
FFC = 320
epsilon = 1e-06
limits = (8, 12, 16, 23, 32, 46, 64, 91)
masked_score = -1000000000.0

f32, bf16, i32 = jnp.float32, jnp.bfloat16, jnp.int32
VMEM_LIMIT = 52 * 1024 * 1024

CHIP_GROUPS = [[s for s in range(16) if s % 2 == c] for c in range(2)]
RELATIVE = ((0, 0), (0, 1), (1, 0), (3, 0), (1, 1), (3, 1), (2, 0), (2, 1))
SC = {"c": 0, "sc": 1, "h": 2, "len": 3, "idx": 5}


def seq_perm(f):
    return [
        (z * 4 + y * 2 + c, (lambda t: t[0] * 4 + t[1] * 2 + t[2])(f(z, y, c)))
        for z in range(4)
        for y in range(2)
        for c in range(2)
    ]


def head_perm(f):
    return [
        (x * 2 + y, (lambda t: t[0] * 2 + t[1])(f(x, y))) for x in range(4) for y in range(2)
    ]


CORE = seq_perm(lambda z, y, c: (z, y, 1 - c))
FORWARD = [seq_perm(lambda z, y, c, a=dz, b=dy: ((z + a) % 4, y ^ b, c)) for dz, dy in RELATIVE]
BACKWARD = [seq_perm(lambda z, y, c, a=dz, b=dy: ((z - a) % 4, y ^ b, c)) for dz, dy in RELATIVE]
HEAD_PAIRS = [
    head_perm(lambda x, y: (x ^ 1, y)),
    head_perm(lambda x, y: (x ^ 2, y)),
    head_perm(lambda x, y: (x, 1 - y)),
]


def nn(a, b):
    return jnp.dot(a, b, preferred_element_type=f32)


def nt(a, b):
    return lax.dot_general(a, b, (((1,), (1,)), ((), ())), preferred_element_type=f32)


def tn(a, b):
    return lax.dot_general(a, b, (((0,), (0,)), ((), ())), preferred_element_type=f32)


def call(kernel, outs, *args, smem=1, scratch=(), flops=0, name=None):
    specs = [pl.BlockSpec(memory_space=pltpu.SMEM)] * smem + [
        pl.BlockSpec(memory_space=pltpu.VMEM)
    ] * (len(args) - smem)
    moved = sum(a.size * a.dtype.itemsize for a in args) + sum(
        o.size * o.dtype.itemsize for o in outs
    )
    return pl.pallas_call(
        kernel,
        out_shape=tuple(outs),
        in_specs=specs,
        out_specs=tuple(pl.BlockSpec(memory_space=pltpu.VMEM) for _ in outs),
        scratch_shapes=list(scratch),
        compiler_params=pltpu.CompilerParams(vmem_limit_bytes=VMEM_LIMIT),
        cost_estimate=pl.CostEstimate(flops=flops, bytes_accessed=moved, transcendentals=0),
        name=name,
    )(*args)


def out(shape, dtype):
    return jax.ShapeDtypeStruct(shape, dtype)


def lane_at(chip, core):
    return pl.multiple_of(chip * 256 + core * 128, 128)


def chunk_p(ref, rows, chip, c):
    return jnp.concatenate(
        [ref[rows, pl.ds(lane_at(chip, c), 128)], ref[rows, pl.ds(lane_at(chip, 1 - c), 128)]],
        axis=1,
    )


def rows_of(half):
    return slice(half * 256, (half + 1) * 256)


def qkv_kernel(scal, x_own, x_sib, w, n1, q, kv, gains):
    c = scal[SC["c"]]

    def w_at(k, p, first, size):
        return pl.ds(pl.multiple_of((2 * k + p) * 144 + first, 16), size)

    for k in range(8):
        for core, p in ((0, c), (1, 1 - c)):
            row = w[w_at(k, p, 128, 16), 0:256].astype(f32)[0:1]
            gains[0:1, k * 256 + core * 128 : k * 256 + core * 128 + 128] = row[:, 0:128]
            gains[1:2, k * 256 + core * 128 : k * 256 + core * 128 + 128] = row[:, 128:256]
    for half, x in ((0, x_own), (1, x_sib)):
        rows = rows_of(half)
        total = jnp.zeros((256, 1), f32)
        for k in range(8):
            v = x[:, k * 256 : (k + 1) * 256].astype(f32)
            total = total + jnp.sum(v * v, axis=1, keepdims=True)
        rinv = lax.rsqrt(total * (1.0 / D) + epsilon)
        acc = jnp.zeros((256, 384), f32)
        for k in range(8):
            lanes = slice(k * 256, (k + 1) * 256)
            v = x[:, lanes].astype(f32)
            normed = (v * rinv * gains[0:1, lanes]).astype(bf16)
            n1[rows, lanes] = normed
            wk = jnp.concatenate(
                [w[w_at(k, c, 0, 128), :], w[w_at(k, 1 - c, 0, 128), :]], axis=0
            )
            acc = acc + nn(normed, wk)
        q[rows, :] = acc[:, 0:128].astype(bf16)
        low = acc[:, 128:384].astype(bf16)
        for chip in range(8):
            kv[chip * 512 + half * 256 : chip * 512 + (half + 1) * 256, :] = low


def out_kernel(scal, mixed, *refs, half, added):
    blocks, rest = refs[:8], refs[8:]
    recv = rest[0] if added else None
    res = rest[-1]
    c = scal[SC["c"]]
    rows = mixed[rows_of(half), :]
    for k in range(8):
        part = nn(rows, blocks[k][0:128, :])
        chip = scal[SC["idx"] + k]
        for p, core in ((0, c), (1, 1 - c)):
            lanes = pl.ds(lane_at(chip, core), 128)
            piece = part[:, p * 128 : (p + 1) * 128]
            if added:
                piece = piece + recv[:, lanes].astype(f32)
            res[:, lanes] = piece.astype(bf16)


def bucket_ids(offset):
    distance = jnp.abs(offset)
    coarse = 7 + sum(((distance >= threshold).astype(i32) for threshold in limits))
    within = jnp.where(distance < 8, distance, coarse)
    return within + jnp.where(offset > 0, 16, 0).astype(i32)


def band_buckets():
    return bucket_ids(
        lax.broadcasted_iota(i32, (128, 384), 1)
        - 128
        - lax.broadcasted_iota(i32, (128, 384), 0)
    )


def key_places(c):
    lane = lax.broadcasted_iota(i32, (1, D), 1)
    stored = lane // 128
    tile = (stored // 2) * 2 + jnp.where(stored % 2 == 1, 1 - c, c)
    return tile, tile * 128 + lane % 128


def band_tiles(scal, half):
    c = scal[SC["c"]]
    tile = scal[SC["sc"]] * 2 + (c if half == 0 else 1 - c)
    lanes = []
    for step in (-1, 0, 1):
        near = tile + step
        stored = (near // 2) * 2 + jnp.where(near % 2 == 1, 1 - c, c)
        inside = jnp.logical_and(near >= 0, near < 16)
        lanes.append(pl.multiple_of(jnp.where(inside, stored, 16) * 128, 128))
    return tile, lanes


def attend_kernel(scal, table, q, kv, e, rl, mixed, s_ref, band):
    c = scal[SC["c"]]
    ids = band_buckets()
    for j in range(2):
        value = jnp.zeros((128, 384), f32)
        for b in range(BUCKETS):
            value = jnp.where(ids == b, table[b, j], value)
        band[j] = value
    tile_of, place_of = key_places(c)
    head_lane = lax.broadcasted_iota(i32, (256, 128), 1) // HEAD
    for b in range(2):
        length = scal[SC["len"] + b]
        keys = kv[:, b, :, 0:128].reshape(D, 128)
        values = jnp.concatenate(
            [kv[:, b, :, 128:256].reshape(D, 128), jnp.ones((D, 128), bf16)], axis=1
        )
        queries = q[:, b].reshape(256, 128)
        together = jnp.zeros((256, 128), f32)
        for j in range(2):
            mine = jnp.where(head_lane == j, queries, jnp.zeros_like(queries))
            s_ref[:, 0:D] = nt(mine, keys)
            for half in range(2):
                tile, lanes = band_tiles(scal, half)
                rows = slice(half * 128, (half + 1) * 128)
                for t in range(3):
                    at = pl.ds(lanes[t], 128)
                    s_ref[rows, at] = s_ref[rows, at] + band[j, :, t * 128 : (t + 1) * 128]
                added = jnp.where(place_of >= length, masked_score, 0.0) + jnp.where(
                    tile_of < tile - 1,
                    table[15, j],
                    jnp.where(tile_of > tile + 1, table[31, j], 0.0),
                )

                def some_rows(i, carry, half=half, added=added, b=b, j=j):
                    at = pl.ds(pl.multiple_of(half * 128 + i * 16, 16), 16)
                    s = s_ref[at, 0:D] + added
                    e[b * 2 + j, at, :] = jnp.exp(s - jnp.max(s, axis=1, keepdims=True)).astype(
                        bf16
                    )
                    return carry

                lax.fori_loop(0, 8, some_rows, 0, unroll=2)
            wide = nn(e[b * 2 + j], values)
            inverse = 1.0 / wide[:, 128:129]
            rl[b * 2 + j] = inverse
            together = jnp.where(head_lane == j, wide[:, 0:128] * inverse, together)
        mixed[:, b] = together.astype(bf16).reshape(2, 128, 128)


def attend_back_kernel(scal, q, kv, e, rl, al_own, al_sib, *refs):
    blocks, (dq, dkv, tab), (d_ref, ds_ref, band, mg) = refs[:8], refs[8:11], refs[11:]
    c = scal[SC["c"]]
    for half, al in ((0, al_own), (1, al_sib)):
        acc = jnp.zeros((256, 128), f32)
        for k in range(8):
            acc = acc + nt(
                chunk_p(al, slice(None), scal[SC["idx"] + k], c), blocks[k][0:128, :]
            )
        mg[half] = acc.astype(bf16).reshape(2, 128, 128)
    tile_of, _ = key_places(c)
    head_lane = lax.broadcasted_iota(i32, (256, 128), 1) // HEAD
    ds_ref[:, D : D + 128] = jnp.zeros((256, 128), bf16)
    band[...] = jnp.zeros_like(band)
    far = [[jnp.zeros((1, D), f32) for _ in range(2)] for _ in range(2)]
    row16 = lax.broadcasted_iota(i32, (16, 256), 0)
    lane256 = lax.broadcasted_iota(i32, (16, 256), 1)
    marks = (row16 == lane256 // 128).astype(f32).astype(bf16)
    for b in range(2):
        keys = kv[:, b, :, 0:128].reshape(D, 128)
        values = kv[:, b, :, 128:256].reshape(D, 128)
        queries = q[:, b].reshape(256, 128)
        turned = queries.astype(f32).T.astype(bf16)
        grads = mg[:, b].reshape(256, 128).astype(f32)
        together = jnp.zeros((256, 128), f32)
        for j in range(2):
            inverse = rl[b * 2 + j]
            scaled = jnp.where(head_lane == j, grads * inverse, 0.0)
            mine = scaled.astype(bf16)
            d_ref[...] = nt(mine, values)

            def some_rows(i, carry, b=b, j=j):
                at = pl.ds(pl.multiple_of(i * 16, 16), 16)
                p = e[b * 2 + j, at, :].astype(f32)
                d = d_ref[at, :]
                inner = jnp.sum(p * d, axis=1, keepdims=True) * rl[b * 2 + j, at, :]
                ds_ref[at, 0:D] = (p * (d - inner)).astype(bf16)
                return carry

            lax.fori_loop(0, 16, some_rows, 0, unroll=2)
            score_grad = ds_ref[:, 0:D]
            together = jnp.where(head_lane == j, nn(score_grad, keys), together)
            left = jnp.concatenate([turned[j * HEAD : (j + 1) * HEAD, :], marks], axis=0)
            key_t = nn(left, score_grad)
            value_t = nn(scaled.T[j * HEAD : (j + 1) * HEAD, :].astype(bf16), e[b * 2 + j])
            for chip in range(8):
                lanes = slice(chip * 256, (chip + 1) * 256)
                at = chip * 256 + j * HEAD
                dkv[at : at + HEAD, b * 256 : (b + 1) * 256] = key_t[0:HEAD, lanes].astype(bf16)
                dkv[at + 128 : at + 128 + HEAD, b * 256 : (b + 1) * 256] = value_t[
                    :, lanes
                ].astype(bf16)
            for half in range(2):
                tile, lanes = band_tiles(scal, half)
                rows = slice(half * 128, (half + 1) * 128)
                for t in range(3):
                    cols = slice(t * 128, (t + 1) * 128)
                    band[j, :, cols] = band[j, :, cols] + ds_ref[
                        rows, pl.ds(lanes[t], 128)
                    ].astype(f32)
                line = key_t[HEAD + half : HEAD + half + 1, :]
                far[j][0] = far[j][0] + jnp.where(tile_of < tile - 1, line, 0.0)
                far[j][1] = far[j][1] + jnp.where(tile_of > tile + 1, line, 0.0)
        dq[:, b] = together.astype(bf16).reshape(2, 128, 128)
    ids = band_buckets()
    lane = lax.broadcasted_iota(i32, (BUCKETS, 128), 1)
    bucket = lax.broadcasted_iota(i32, (BUCKETS, 1), 0)
    result = jnp.zeros((BUCKETS, 128), f32)
    for j in range(2):
        near = band[j]
        lines = [
            jnp.sum(jnp.where(ids == b, near, 0.0), axis=0, keepdims=True) for b in range(BUCKETS)
        ]
        column = jnp.sum(jnp.concatenate(lines, axis=0), axis=1, keepdims=True)
        column = column + jnp.where(bucket == 15, jnp.sum(far[j][0]), 0.0)
        column = column + jnp.where(bucket == 31, jnp.sum(far[j][1]), 0.0)
        result = jnp.where(lane == j, column, result)
    tab[...] = result


def summed(parts):
    total = parts[0:32, :].astype(f32)
    for k in range(1, 8):
        total = total + parts[k * 32 : (k + 1) * 32, :].astype(f32)
    return total


def own_rows(scal, ref):
    return ref[pl.ds(pl.multiple_of(scal[SC["h"]] * 32, 32), 32), :]


def spread(ref, value):
    for k in range(8):
        ref[k * 32 : (k + 1) * 32, :] = value


def norm_two_kernel(scal, parts, x, gains, hid, normed):
    hidden_in = own_rows(scal, x).astype(f32) + summed(parts)
    hid[...] = hidden_in
    rinv = lax.rsqrt(jnp.mean(hidden_in * hidden_in, axis=1, keepdims=True) + epsilon)
    spread(normed, (hidden_in * rinv * gains[1:2, :]).astype(bf16))


def norm_back(value, grad, gain):
    rinv = lax.rsqrt(jnp.mean(value * value, axis=1, keepdims=True) + epsilon)
    u = grad * gain
    return rinv * u - (rinv * rinv * rinv) * value * jnp.mean(u * value, axis=1, keepdims=True)


def live_rows(scal, half, b, first, count):
    c = scal[SC["c"]]
    core = c if half == 0 else 1 - c
    place = (scal[SC["sc"]] * 2 + core) * 128 + first + lax.broadcasted_iota(i32, (count, 1), 0)
    return place < scal[SC["len"] + b]


def norm_two_back_kernel(scal, parts, hid, cot, gains, hig, low):
    h = scal[SC["h"]]
    b = h // 4
    place = (
        (scal[SC["sc"]] * 2 + scal[SC["c"]]) * 128
        + (h - b * 4) * 32
        + lax.broadcasted_iota(i32, (32, 1), 0)
    )
    live = place < scal[SC["len"] + b]
    out_grad = jnp.where(live, own_rows(scal, cot).astype(f32), 0.0)
    grad = out_grad + norm_back(hid[...], summed(parts), gains[1:2, :])
    hig[...] = grad
    spread(low, grad.astype(bf16))


def norm_one_back_kernel(scal, parts, x, hig, gains, res):
    grad = hig[...] + norm_back(own_rows(scal, x).astype(f32), summed(parts), gains[0:1, :])
    spread(res, grad.astype(bf16))


def gelu_pair(g):
    k0, k1 = 0.7978845608028654, 0.044715
    g2 = g * g
    t = jnp.tanh(k0 * g * (1.0 + k1 * g2))
    value = 0.5 * g * (1.0 + t)
    slope = 0.5 * (1.0 + t) + 0.5 * g * (1.0 - t * t) * k0 * (1.0 + 3.0 * k1 * g2)
    return value, slope


def ffn_kernel(scal, n_own, n_sib, cot_own, cot_sib, *refs):
    blocks, (hidden, gu_low, out_low) = refs[:8], refs[8:]
    c = scal[SC["c"]]
    for half, n, cot in ((0, n_own, cot_own), (1, n_sib, cot_sib)):
        rows = rows_of(half)
        live = jnp.concatenate(
            [live_rows(scal, half, b, 0, 128) for b in range(2)], axis=0
        )
        out_low[rows, :] = jnp.where(live, cot[...], jnp.zeros((), bf16))
        gate_a = jnp.zeros((256, 256), f32)
        up_a = jnp.zeros((256, 256), f32)
        rest = jnp.zeros((256, 128), f32)
        back = jnp.zeros((256, FFC), f32)
        for k in range(8):
            chip = scal[SC["idx"] + k]
            v = chunk_p(n, slice(None), chip, c)
            w = blocks[k]
            gate_a = gate_a + nn(v, w[448:704, :])
            up_a = up_a + nn(v, w[704:960, :])
            rest = rest + nn(v[:, 0:128], w[960:1088, 0:128])
            rest = rest + nn(v[:, 128:256], w[960:1088, 128:256])
            back = back + nt(chunk_p(out_low, rows, chip, c), w[128:448, :])
        for gate, up, dh, at, size in (
            (gate_a, up_a, back[:, 0:256], 0, 256),
            (rest[:, 0:64], rest[:, 64:128], back[:, 256:FFC], 256, 64),
        ):
            value, slope = gelu_pair(gate)
            hidden[rows, at : at + size] = (value * up).astype(bf16)
            gate_low = (dh * up * slope).astype(bf16)
            up_low = (dh * value).astype(bf16)
            first = 0 if at == 0 else 512
            gu_low[rows, first : first + size] = gate_low
            gu_low[rows, first + size : first + 2 * size] = up_low


def ffn_back_kernel(scal, gu_low, n, gains, *refs, half, added):
    blocks, rest = refs[:8], refs[8:]
    recv = rest[0] if added else None
    res, gain_sum = rest[-2:]
    c = scal[SC["c"]]
    low = gu_low[rows_of(half), :]
    for k in range(8):
        chip = scal[SC["idx"] + k]
        w = blocks[k]
        part = nt(low[:, 0:256], w[448:704, :]) + nt(low[:, 256:512], w[704:960, :])
        for p, core in ((0, c), (1, 1 - c)):
            lanes = pl.ds(lane_at(chip, core), 128)
            cols = slice(p * 128, (p + 1) * 128)
            piece = part[:, cols] + nt(low[:, 512:640], w[960:1088, cols])
            gain_sum[0:1, lanes] = (
                jnp.sum(piece * n[:, lanes].astype(f32), axis=0, keepdims=True)
                / gains[1:2, lanes]
            )
            if added:
                piece = piece + recv[:, lanes].astype(f32)
            res[:, lanes] = piece.astype(bf16)


def ffn_weights_kernel(scal, n_own, n_sib, gu_low, hidden, out_low, *results):
    c = scal[SC["c"]]
    for k in range(8):
        chip = scal[SC["idx"] + k]
        res = results[k]
        res[0:320, :] = tn(hidden[...], chunk_p(out_low, slice(None), chip, c)).astype(bf16)
        v = jnp.concatenate(
            [chunk_p(n_own, slice(None), chip, c), chunk_p(n_sib, slice(None), chip, c)], axis=0
        )
        part = tn(v, gu_low[...]).astype(bf16)
        res[320:576, :] = part[:, 0:256]
        res[576:832, :] = part[:, 256:512]
        res[832:960, 0:128] = part[0:128, 512:640]
        res[832:960, 128:256] = part[128:256, 512:640]


def ffn_out_kernel(scal, hidden, *refs, half, added):
    blocks, rest = refs[:8], refs[8:]
    res = rest[-1]
    c = scal[SC["c"]]
    low = hidden[rows_of(half), :]
    for k in range(8):
        chip = scal[SC["idx"] + k]
        part = nn(low, blocks[k][128:448, :])
        for p, core in ((0, c), (1, 1 - c)):
            lanes = pl.ds(lane_at(chip, core), 128)
            piece = part[:, p * 128 : (p + 1) * 128]
            if added:
                recv, hid = rest[0], rest[1]
                whole = piece + recv[:, lanes].astype(f32)
                res[:, lanes] = whole.astype(bf16)
                at = pl.ds(pl.multiple_of(scal[SC["h"]] * 32, 32), 32)
                res[at, lanes] = (res[at, lanes].astype(f32) + hid[:, lanes]).astype(bf16)
            else:
                res[:, lanes] = piece.astype(bf16)


def key_value_sum_kernel(scal, parts, kv_low):
    total = parts[0:256, :].astype(f32)
    for k in range(1, 8):
        total = total + parts[k * 256 : (k + 1) * 256, :].astype(f32)
    for b in range(2):
        for half in range(2):
            lanes = slice(b * 256 + half * 128, b * 256 + (half + 1) * 128)
            kv_low[half * 256 + b * 128 : half * 256 + (b + 1) * 128, :] = total[:, lanes].T.astype(
                bf16
            )


def qkv_back_kernel(scal, q_low, kv_low, n1, w, gains, *rest, half, added):
    recv = rest[0] if added else None
    res, gain_sum = rest[-2:]
    c = scal[SC["c"]]
    rows = rows_of(half)
    low = jnp.concatenate([q_low[rows, :], kv_low[rows, :]], axis=1)
    for k in range(8):
        wk = jnp.concatenate(
            [w[pl.ds(pl.multiple_of((2 * k + p) * 144, 16), 128), :] for p in (c, 1 - c)], axis=0
        )
        lanes = slice(k * 256, (k + 1) * 256)
        part = nt(low, wk)
        gain_sum[0:1, lanes] = (
            jnp.sum(part * n1[rows, lanes].astype(f32), axis=0, keepdims=True) / gains[0:1, lanes]
        )
        if added:
            part = part + recv[:, lanes].astype(f32)
        res[:, lanes] = part.astype(bf16)


def last_weights_kernel(
    scal, n1, q_low, kv_low, mixed, al_own, al_sib, g1a, g1b, g2a, g2b, tab, *results
):
    c = scal[SC["c"]]
    low = jnp.concatenate([q_low[...], kv_low[...]], axis=1)
    for k in range(8):
        chip = scal[SC["idx"] + k]
        res = results[k]
        al = jnp.concatenate(
            [chunk_p(al_own, slice(None), chip, c), chunk_p(al_sib, slice(None), chip, c)], axis=0
        )
        res[0:128, :] = tn(mixed[...], al).astype(bf16)
        part = tn(chunk_p(n1, slice(None), chip, c), low).astype(bf16)
        res[128:384, :] = part[:, 0:256]
        res[384:512, 0:128] = part[0:128, 256:384]
        res[384:512, 128:256] = part[128:256, 256:384]
        one = slice(0, 1)
        misc = jnp.concatenate(
            [
                chunk_p(g1a, one, chip, c) + chunk_p(g1b, one, chip, c),
                chunk_p(g2a, one, chip, c) + chunk_p(g2b, one, chip, c),
                tab[pl.ds(chip, 1), :],
                jnp.zeros((13, 256), f32),
            ],
            axis=0,
        )
        res[512:528, :] = misc.astype(bf16)


def to_sibling(a):
    return lax.ppermute(a, "seq", CORE)


def over_head(a):
    return lax.all_to_all(a, "head", 0, 0, tiled=True)


def over_chips(a):
    return lax.all_to_all(a, "seq", 0, 0, axis_index_groups=CHIP_GROUPS, tiled=True)


def body(
    inputs,
    cotangent,
    lengths,
    attn_gain,
    w_query,
    w_key,
    w_value,
    w_out,
    bias_table,
    ffn_gain,
    w_gate,
    w_up,
    w_down,
):
    s = lax.axis_index("seq").astype(i32)
    h = lax.axis_index("head").astype(i32)
    c, sc = s % 2, s // 2
    z, y = sc // 2, sc % 2
    first = c == 0
    idx = [((z - dz) % 4) * 2 + (y ^ dy) for dz, dy in RELATIVE]
    scal = jnp.stack([c, sc, h, lengths[0], lengths[1], *idx]).astype(i32)

    def halves(a, axis):
        low, high = jnp.split(a, 2, axis=axis)
        return jnp.where(first, low, high), jnp.where(first, high, low)

    def in_order(own, sib, axis):
        return jnp.where(
            first,
            jnp.concatenate([own, sib], axis=axis),
            jnp.concatenate([sib, own], axis=axis),
        )

    misc = jnp.concatenate(
        [
            jnp.pad(
                jnp.concatenate([attn_gain, ffn_gain])[None, :], ((0, 0), (0, 128))
            ),
            jnp.pad(bias_table, ((0, 13), (0, 380))),
        ],
        axis=0,
    )
    pairs = [halves(w, 1) for w in (w_query, w_key, w_value)]
    mine = jnp.concatenate([jnp.concatenate([a for a, _ in pairs], axis=1), misc], axis=0)
    theirs = jnp.concatenate([jnp.concatenate([a for _, a in pairs], axis=1), misc], axis=0)
    block = jnp.concatenate([mine, to_sibling(theirs)], axis=0)
    w_qkv = over_chips(jnp.broadcast_to(block[None], (8, 288, 384)).reshape(8 * 288, 384))

    x_own = inputs.reshape(256, D)
    x_sib = to_sibling(x_own)
    cot_own = cotangent.reshape(256, D)
    cot_sib = to_sibling(cot_own)

    out_mine, out_theirs = halves(w_out, 0)
    down_mine, down_theirs = halves(w_down, 0)
    gate_mine, gate_theirs = halves(w_gate, 1)
    up_mine, up_theirs = halves(w_up, 1)

    def joined(gate, up):
        return jnp.concatenate(
            [gate[:, 0:256], up[:, 0:256], gate[:, 256:FFC], up[:, 256:FFC]], axis=1
        )

    rows_mine = jnp.concatenate([out_mine, down_mine], axis=0)
    gu_mine = joined(gate_mine, up_mine)
    rows_recv = to_sibling(jnp.concatenate([out_theirs, down_theirs], axis=0))
    gu_recv = to_sibling(joined(gate_theirs, up_theirs))
    block = jnp.concatenate(
        [
            jnp.concatenate([rows_mine, rows_recv], axis=1),
            jnp.concatenate([gu_mine[:, 0:256], gu_recv[:, 0:256]], axis=0),
            jnp.concatenate([gu_mine[:, 256:512], gu_recv[:, 256:512]], axis=0),
            jnp.concatenate([gu_mine[:, 512:640], gu_recv[:, 512:640]], axis=1),
        ],
        axis=0,
    )
    blocks = [block] + [lax.ppermute(block, "seq", FORWARD[k]) for k in range(1, 8)]

    n1, q, kv, gains = call(
        qkv_kernel,
        [out((512, D), bf16), out((512, 128), bf16), out((8 * 512, 256), bf16), out((2, D), f32)],
        scal,
        x_own,
        x_sib,
        w_qkv,
        flops=2 * 512 * D * 384,
        name="qkv",
    )
    q = q.reshape(2, 2, 128, 128)
    kv = over_chips(kv).reshape(16, 2, 128, 256)
    rows = w_qkv.reshape(8, 2, 144, 384)[:, :, 129:131, 0:4].astype(f32)
    rows = jnp.where(first, rows, rows[:, ::-1]).reshape(BUCKETS, 4)
    table = jnp.where(first, rows[:, 0:2], rows[:, 2:4])
    e, rl, mixed = call(
        attend_kernel,
        [out((4, 256, D), bf16), out((4, 256, 1), f32), out((2, 2, 128, 128), bf16)],
        scal,
        table,
        q,
        kv,
        smem=2,
        scratch=[pltpu.VMEM((256, D + 128), f32), pltpu.VMEM((2, 128, 384), f32)],
        flops=20 * 10**9,
        name="attend",
    )
    mixed = mixed.reshape(512, 128)

    def both_halves(kernel, args, outs, flops, extra=(), name=None):
        args_sib, args_own = args
        sib = call(
            functools.partial(kernel, half=1, added=False), outs, *args_sib, flops=flops, name=name + "_sib"
        )
        recv = to_sibling(sib[0])
        own = call(
            functools.partial(kernel, half=0, added=True),
            outs,
            *args_own,
            recv,
            *extra,
            flops=flops,
            name=name + "_own",
        )
        return sib, own

    part = [out((256, D), bf16)]
    part_gain = [out((256, D), bf16), out((1, D), f32)]
    args = (scal, mixed, *blocks)
    _, (attn_part,) = both_halves(out_kernel, (args, args), part, 2 * 256 * D * 128, name="out")
    hid, n2 = call(
        norm_two_kernel,
        [out((32, D), f32), out((256, D), bf16)],
        scal,
        over_head(attn_part),
        x_own,
        gains,
        name="norm_two",
    )
    n_own = over_head(n2)
    n_sib = to_sibling(n_own)

    hidden, gu_low, out_low = call(
        ffn_kernel,
        [out((512, FFC), bf16), out((512, 640), bf16), out((512, D), bf16)],
        scal,
        n_own,
        n_sib,
        cot_own,
        cot_sib,
        *blocks,
        flops=2 * 512 * D * 960,
        name="ffn",
    )
    (_, g2a), (ffn_part, g2b) = both_halves(
        ffn_back_kernel,
        ((scal, gu_low, n_sib, gains, *blocks), (scal, gu_low, n_own, gains, *blocks)),
        part_gain,
        2 * 256 * D * 640,
        name="ffn_back",
    )
    ffn_grads = call(
        ffn_weights_kernel,
        [out((960, 256), bf16)] * 8,
        scal,
        n_own,
        n_sib,
        gu_low,
        hidden,
        out_low,
        flops=2 * 512 * D * 960,
        name="ffn_weights",
    )
    args = (scal, hidden, *blocks)
    _, (out_part,) = both_halves(
        ffn_out_kernel, (args, args), part, 2 * 256 * D * FFC, extra=(hid,), name="ffn_out"
    )
    layer_out = lax.psum(out_part, "head").reshape(2, 128, D)
    hig, low = call(
        norm_two_back_kernel,
        [out((32, D), f32), out((256, D), bf16)],
        scal,
        over_head(ffn_part),
        hid,
        cot_own,
        gains,
        name="norm_two_back",
    )
    al_own = over_head(low)
    al_sib = to_sibling(al_own)

    q_low, dkv, tab = call(
        attend_back_kernel,
        [out((2, 2, 128, 128), bf16), out((8 * 256, 512), bf16), out((BUCKETS, 128), f32)],
        scal,
        q,
        kv,
        e,
        rl,
        al_own,
        al_sib,
        *blocks,
        scratch=[
            pltpu.VMEM((256, D), f32),
            pltpu.VMEM((256, D + 128), bf16),
            pltpu.VMEM((2, 128, 384), f32),
            pltpu.VMEM((2, 2, 128, 128), bf16),
        ],
        flops=40 * 10**9,
        name="attend_back",
    )
    q_low = q_low.reshape(512, 128)
    (kv_low,) = call(
        key_value_sum_kernel, [out((512, 256), bf16)], scal, over_chips(dkv), name="key_value_sum"
    )
    args = (scal, q_low, kv_low, n1, w_qkv, gains)
    (_, g1a), (one_part, g1b) = both_halves(
        qkv_back_kernel, (args, args), part_gain, 2 * 256 * D * 384, name="qkv_back"
    )
    (low,) = call(
        norm_one_back_kernel,
        [out((256, D), bf16)],
        scal,
        over_head(one_part),
        x_own,
        hig,
        gains,
        name="norm_one_back",
    )
    input_grad = over_head(low).astype(f32).reshape(2, 128, D)

    rows = tab[:, 0:2].reshape(8, 2, 4)
    rows = jnp.where(first, rows, rows[:, ::-1])
    rows = jnp.pad(rows, ((0, 0), (0, 0), (0, 124))).reshape(8, 256)
    last_grads = call(
        last_weights_kernel,
        [out((528, 256), bf16)] * 8,
        scal,
        n1,
        q_low,
        kv_low,
        mixed,
        al_own,
        al_sib,
        g1a,
        g1b,
        g2a,
        g2b,
        rows,
        flops=2 * 512 * D * 512,
        name="last_weights",
    )

    def gathered(pieces):
        total = pieces[0].astype(f32)
        for k in range(1, 8):
            total = total + lax.ppermute(pieces[k], "seq", BACKWARD[k]).astype(f32)
        return total

    def apart(total, first_row):
        a = total[first_row : first_row + 256]
        b = total[first_row + 256 : first_row + 512]
        rest = total[first_row + 512 : first_row + 640]
        res = []
        for p in range(2):
            at = slice(p * 128, (p + 1) * 128)
            res.append(
                (
                    jnp.concatenate([a[at], rest[:, p * 128 : p * 128 + 64]], axis=1),
                    jnp.concatenate([b[at], rest[:, p * 128 + 64 : (p + 1) * 128]], axis=1),
                )
            )
        return res

    total = gathered(ffn_grads)
    (gate_own, up_own), (gate_sib, up_sib) = apart(total, 320)
    down_recv = to_sibling(total[0:320, 128:256].astype(bf16)).astype(f32)
    gu_recv = to_sibling(jnp.concatenate([gate_sib, up_sib], axis=1).astype(bf16)).astype(f32)
    down_grad = in_order(total[0:320, 0:128], down_recv, 0)
    gate_grad = in_order(gate_own, gu_recv[:, 0:FFC], 1)
    up_grad = in_order(up_own, gu_recv[:, FFC : 2 * FFC], 1)

    total = gathered(last_grads)
    sent = jnp.concatenate(
        [
            total[0:128, 128:256],
            total[256:384, 0:256],
            total[384:512, 128:256],
        ],
        axis=1,
    ).astype(bf16)
    recv = to_sibling(sent).astype(f32)
    out_grad = in_order(total[0:128, 0:128], recv[:, 0:128], 0)
    query_grad = in_order(total[128:256, 0:128], recv[:, 128:256], 1)
    key_grad = in_order(total[128:256, 128:256], recv[:, 256:384], 1)
    value_grad = in_order(total[384:512, 0:128], recv[:, 384:512], 1)
    small = to_sibling(total[512:528, 128:256])
    gain_sums = total[512:514, 0:128] + small[0:2, :]
    for pairs in HEAD_PAIRS:
        gain_sums = gain_sums + lax.ppermute(gain_sums, "head", pairs)
    table_grad = in_order(
        total[514, 0:4].reshape(2, 2), small[2, 0:4].reshape(2, 2), 1
    )
    return (
        layer_out,
        input_grad,
        gain_sums[0],
        query_grad,
        key_grad,
        value_grad,
        out_grad,
        table_grad,
        gain_sums[1],
        gate_grad,
        up_grad,
        down_grad,
    )


def solution(mesh):
    seq_head, head_seq = P("seq", "head"), P("head", "seq")
    in_specs = (
        P(None, "seq", None),
        P(None, "seq", None),
        P(),
        P("seq"),
        seq_head,
        seq_head,
        seq_head,
        head_seq,
        seq_head,
        P("seq"),
        seq_head,
        seq_head,
        head_seq,
    )
    out_specs = (
        P(None, "seq", None),
        P(None, "seq", None),
        P("seq"),
        seq_head,
        seq_head,
        seq_head,
        head_seq,
        seq_head,
        P("seq"),
        seq_head,
        seq_head,
        head_seq,
    )
    return jax.shard_map(body, mesh=mesh, in_specs=in_specs, out_specs=out_specs, check_vma=False)
```

```python
import functools

import jax
import jax.numpy as jnp
from jax import lax
from jax.experimental import pallas as pl
from jax.experimental.pallas import tpu as pltpu
from jax.sharding import PartitionSpec as P


D = 2048
HEAD = 64
BUCKETS = 32
FFC = 320
epsilon = 1e-06
limits = (8, 12, 16, 23, 32, 46, 64, 91)
masked_score = -1000000000.0

f32, bf16, i32 = jnp.float32, jnp.bfloat16, jnp.int32
MIB = 1024 * 1024

CHIP_GROUPS = [[s for s in range(16) if s % 2 == c] for c in range(2)]
RELATIVE = ((0, 0), (0, 1), (1, 0), (1, 1), (3, 0), (3, 1), (2, 0), (2, 1))
def seq_perm(f):
    return [
        (z * 4 + y * 2 + c, (lambda t: t[0] * 4 + t[1] * 2 + t[2])(f(z, y, c)))
        for z in range(4)
        for y in range(2)
        for c in range(2)
    ]


def head_perm(f):
    return [
        (x * 2 + y, (lambda t: t[0] * 2 + t[1])(f(x, y))) for x in range(4) for y in range(2)
    ]


CORE = seq_perm(lambda z, y, c: (z, y, 1 - c))
OTHER_Y = seq_perm(lambda z, y, c: (z, 1 - y, c))
ALONG_Z = {d: seq_perm(lambda z, y, c, d=d: ((z + d) % 4, y, c)) for d in (1, 2, 3)}
HEAD_PAIRS = [
    head_perm(lambda x, y: (x ^ 1, y)),
    head_perm(lambda x, y: (x ^ 2, y)),
    head_perm(lambda x, y: (x, 1 - y)),
]


def nn(a, b):
    return jnp.dot(a, b, preferred_element_type=f32)


def nt(a, b):
    return lax.dot_general(a, b, (((1,), (1,)), ((), ())), preferred_element_type=f32)


def tn(a, b):
    return lax.dot_general(a, b, (((0,), (0,)), ((), ())), preferred_element_type=f32)


class Loaded:
    def __init__(self, copy, ref):
        self.copy, self.ref, self.here = copy, ref, False

    def ready(self):
        if not self.here:
            self.copy.wait()
            self.here = True
        return self.ref

    def __getitem__(self, at):
        return self.ready()[at]

    @property
    def at(self):
        return self.ready().at


class Stored:
    def __init__(self, ref, there, sems, times):
        self.ref, self.there, self.sems, self.times = ref, there, sems, times
        self.copies, self.whole = [], True

    def start(self, source, target):
        copy = pltpu.make_async_copy(source, target, self.sems.at[len(self.copies)])
        copy.start()
        self.copies.append(copy)

    def send(self):
        rows = self.ref.shape[0]
        for t in range(self.times):
            there = self.there if self.times == 1 else self.there.at[pl.ds(t * rows, rows)]
            self.start(self.ref, there)

    def send_part(self, at):
        self.start(self.ref.at[at], self.there.at[at])

    def __getitem__(self, at):
        return self.ref[at]

    def __setitem__(self, at, value):
        self.ref[at] = value

    @property
    def at(self):
        return self.ref.at


class Place:
    def __init__(self, scalars):
        self.c, self.sc, self.h = scalars[0], scalars[1], scalars[2]
        self.lengths = {0: scalars[3], 1: scalars[4]}
        self.idx = [scalars[5 + k] for k in range(8)]


def place_scalars(lengths):
    s, h = lax.axis_index("seq"), lax.axis_index("head")
    c, sc = s % 2, s // 2
    z, y = sc // 2, sc % 2
    idx = [((z + 4 - dz) % 4) * 2 + (y if dy == 0 else 1 - y) for dz, dy in RELATIVE]
    return jnp.stack([c, sc, h, lengths[0], lengths[1], *idx]).astype(i32)


class Far:
    def __init__(self, value, at=None):
        self.value, self.at = value, at

    def shape(self):
        return jax.eval_shape(lambda v: v if self.at is None else v[self.at], self.value).shape


class Rows(Far):
    def shape(self):
        return (32, self.value.shape[1])


def call(kernel, outs, lengths, *args, smem=(), scratch=(), vmem=8, name=None):
    n, m, fixed = len(args), len(outs), 1 + len(smem)
    far_in = [i for i, a in enumerate(args) if isinstance(a, Far)]
    far_out = [k for k, o in enumerate(outs) if len(o) == 3]

    def whole(*refs):
        lens, scalars, refs = refs[0], refs[1:fixed], refs[fixed:]
        inputs, outputs, refs = list(refs[:n]), list(refs[n : n + m]), list(refs[n + m :])
        for i in far_in:
            buf, sem = refs.pop(0), refs.pop(0)
            there = inputs[i]
            if isinstance(args[i], Rows):
                first = pl.multiple_of(lens[2] * 32, 32)
                there = there.at[pl.ds(first, 32)]
            elif args[i].at is not None:
                there = there.at[args[i].at]
            copy = pltpu.make_async_copy(there, buf, sem)
            copy.start()
            inputs[i] = Loaded(copy, buf)
        for k in far_out:
            buf, sems = refs.pop(0), refs.pop(0)
            outputs[k] = Stored(buf, outputs[k], sems, outs[k][2])
        kernel(Place(lens), *scalars, *inputs, *outputs, *refs)
        for i in far_in:
            inputs[i].ready()
        for k in far_out:
            if not outputs[k].copies:
                outputs[k].send()
        for k in far_out:
            for copy in outputs[k].copies:
                copy.wait()

    buffers = []
    for i in far_in:
        buffers += [pltpu.VMEM(args[i].shape(), args[i].value.dtype), pltpu.SemaphoreType.DMA]
    for k in far_out:
        shape, dtype, _ = outs[k]
        buffers += [pltpu.VMEM(shape, dtype), pltpu.SemaphoreType.DMA((24,))]
    placed = [
        pltpu.with_memory_space_constraint(a.value, pltpu.HBM)
        if isinstance(a, Far)
        else a
        for a in args
    ]
    shapes = [
        pltpu.HBM((o[0][0] * o[2], *o[0][1:]), o[1])
        if len(o) == 3
        else jax.ShapeDtypeStruct(o[0], o[1])
        for o in outs
    ]
    return pl.pallas_call(
        whole,
        out_shape=tuple(shapes),
        in_specs=[pl.BlockSpec(memory_space=pltpu.SMEM)] * fixed
        + [pl.BlockSpec(memory_space=pl.ANY if i in far_in else pltpu.VMEM) for i in range(n)],
        out_specs=tuple(
            pl.BlockSpec(memory_space=pl.ANY if k in far_out else pltpu.VMEM) for k in range(m)
        ),
        scratch_shapes=buffers + list(scratch),
        compiler_params=pltpu.CompilerParams(vmem_limit_bytes=vmem * MIB),
        cost_estimate=pl.CostEstimate(flops=1000, bytes_accessed=1000, transcendentals=0),
        name=name,
    )(lengths, *smem, *placed)


def lane_at(chip, core):
    return pl.multiple_of(chip * 256 + core * 128, 128)


def chunk_p(ref, rows, chip, c):
    return jnp.concatenate(
        [ref[rows, pl.ds(lane_at(chip, c), 128)], ref[rows, pl.ds(lane_at(chip, 1 - c), 128)]],
        axis=1,
    )


def rows_of(half):
    return slice(half * 256, (half + 1) * 256)


def pack_kernel(me, wq, wk, wv, wo, ga, gf, bias, mine, theirs, misc):
    misc[...] = jnp.zeros_like(misc)
    misc[0:1, 0:128] = ga[...].astype(f32)
    misc[0:1, 128:256] = gf[...].astype(f32)
    misc[1:3, 0:4] = bias[...].astype(f32)
    low = jnp.concatenate([wq[:, 0:128], wk[:, 0:128], wv[:, 0:128], wo[0:128, :]], axis=1)
    high = jnp.concatenate(
        [wq[:, 128:256], wk[:, 128:256], wv[:, 128:256], wo[128:256, :]], axis=1
    )
    theirs[0:128, :] = jnp.where(me.c == 0, high, low)
    mine[0:128, :] = jnp.where(me.c == 0, low, high)
    for res in (mine, theirs):
        res[128:144, :] = misc[...].astype(bf16)


def qkv_kernel(me, x_own, x_sib, w, n1, q, kv, gains):
    c = me.c
    rinvs = []
    for x in (x_own, x_sib):
        total = jnp.zeros((256, 1), f32)
        for k in range(8):
            v = x[:, k * 256 : (k + 1) * 256].astype(f32)
            total = total + jnp.sum(v * v, axis=1, keepdims=True)
        rinvs.append(lax.rsqrt(total * (1.0 / D) + epsilon))
    for k in range(8):
        for core, p in ((0, c), (1, 1 - c)):
            row = w[2 * k + p, 128:144, 0:256].astype(f32)[0:1]
            gains[0:1, k * 256 + core * 128 : k * 256 + core * 128 + 128] = row[:, 0:128]
            gains[1:2, k * 256 + core * 128 : k * 256 + core * 128 + 128] = row[:, 128:256]
    gains.send()
    for half, x, rinv in ((0, x_own, rinvs[0]), (1, x_sib, rinvs[1])):
        rows = rows_of(half)
        acc = jnp.zeros((256, 384), f32)
        for k in range(8):
            lanes = slice(k * 256, (k + 1) * 256)
            v = x[:, lanes].astype(f32)
            normed = (v * rinv * gains[0:1, lanes]).astype(bf16)
            n1[rows, lanes] = normed
            wk = jnp.concatenate(
                [w[2 * k + c, 0:128, 0:384], w[2 * k + 1 - c, 0:128, 0:384]], axis=0
            )
            acc = acc + nn(normed, wk)
        q[rows, :] = acc[:, 0:128].astype(bf16)
        kv[rows, :] = acc[:, 128:384].astype(bf16)
        for chip in range(8):
            kv.start(kv.ref.at[rows], kv.there.at[pl.ds(chip * 512 + half * 256, 256)])
        n1.send_part(rows)


def out_weights(me, w, k):
    return jnp.concatenate([w[2 * k + p] for p in (me.c, 1 - me.c)], axis=1)


def bucket_ids(offset):
    distance = jnp.abs(offset)
    coarse = 7 + sum(((distance >= threshold).astype(i32) for threshold in limits))
    within = jnp.where(distance < 8, distance, coarse)
    return within + jnp.where(offset > 0, 16, 0).astype(i32)


def band_buckets():
    return bucket_ids(
        lax.broadcasted_iota(i32, (128, 384), 1)
        - 128
        - lax.broadcasted_iota(i32, (128, 384), 0)
    )


def key_places(c):
    lane = lax.broadcasted_iota(i32, (1, D), 1)
    stored = lane // 128
    tile = (stored // 2) * 2 + jnp.where(stored % 2 == 1, 1 - c, c)
    return tile, tile * 128 + lane % 128


def band_tiles(me, half):
    c = me.c
    tile = me.sc * 2 + (c if half == 0 else 1 - c)
    lanes = []
    for step in (-1, 0, 1):
        near = tile + step
        stored = (near // 2) * 2 + jnp.where(near % 2 == 1, 1 - c, c)
        inside = jnp.logical_and(near >= 0, near < 16)
        lanes.append(pl.multiple_of(jnp.where(inside, stored, 16) * 128, 128))
    return tile, lanes


def attend_kernel(me, table, q, kv, w, e0, e1, e2, e3, rl, mixed, own, sib, s_ref, band):
    exps = (e0, e1, e2, e3)
    c = me.c
    ids = band_buckets()
    for j in range(2):
        value = jnp.zeros((128, 384), f32)
        for b in range(BUCKETS):
            value = jnp.where(ids == b, table[b, j], value)
        band[j] = value
    tile_of, place_of = key_places(c)
    head_lane = lax.broadcasted_iota(i32, (256, 128), 1) // HEAD
    for b in range(2):
        length = me.lengths[b]
        keys = kv[:, b, :, 0:128].reshape(D, 128)
        values = jnp.concatenate(
            [kv[:, b, :, 128:256].reshape(D, 128), jnp.ones((D, 128), bf16)], axis=1
        )
        queries = q[:, b].reshape(256, 128)
        together = jnp.zeros((256, 128), f32)
        for j in range(2):
            mine = jnp.where(head_lane == j, queries, jnp.zeros_like(queries))
            s_ref[:, 0:D] = nt(mine, keys)
            for half in range(2):
                tile, lanes = band_tiles(me, half)
                rows = slice(half * 128, (half + 1) * 128)
                for t in range(3):
                    at = pl.ds(lanes[t], 128)
                    s_ref[rows, at] = s_ref[rows, at] + band[j, :, t * 128 : (t + 1) * 128]
                added = jnp.where(place_of >= length, masked_score, 0.0) + jnp.where(
                    tile_of < tile - 1,
                    table[15, j],
                    jnp.where(tile_of > tile + 1, table[31, j], 0.0),
                )

                def some_rows(i, carry, half=half, added=added, b=b, j=j):
                    at = pl.ds(pl.multiple_of(half * 128 + i * 16, 16), 16)
                    s = s_ref[at, 0:D] + added
                    exps[b * 2 + j][at, :] = jnp.exp(
                        s - jnp.max(s, axis=1, keepdims=True)
                    ).astype(bf16)
                    return carry

                lax.fori_loop(0, 8, some_rows, 0, unroll=2)
            exps[b * 2 + j].send()
            wide = nn(exps[b * 2 + j][...], values)
            inverse = 1.0 / wide[:, 128:129]
            rl[b * 2 + j] = inverse
            together = jnp.where(head_lane == j, wide[:, 0:128] * inverse, together)
        mixed[:, b] = together.astype(bf16).reshape(2, 128, 128)
    rl.send()
    mixed.send()
    for half, res in ((1, sib), (0, own)):
        for k in range(8):
            res[:, k * 256 : (k + 1) * 256] = nn(
                mixed[half].reshape(256, 128), out_weights(me, w, k)
            ).astype(bf16)


def attend_back_kernel(
    me, w, al_own, al_sib, q, kv, rl, e0, e1, e2, e3, dq, dkv, tab, d_ref, ds_ref, band, mg
):
    exps = (e0, e1, e2, e3)
    c = me.c
    for half, al in ((0, al_own), (1, al_sib)):
        acc = jnp.zeros((256, 128), f32)
        for k in range(8):
            acc = acc + nt(al[:, k * 256 : (k + 1) * 256], out_weights(me, w, k))
        mg[half] = acc.astype(bf16).reshape(2, 128, 128)
    tile_of, _ = key_places(c)
    head_lane = lax.broadcasted_iota(i32, (256, 128), 1) // HEAD
    ds_ref[:, D : D + 128] = jnp.zeros((256, 128), bf16)
    band[...] = jnp.zeros_like(band)
    far = [[jnp.zeros((1, D), f32) for _ in range(2)] for _ in range(2)]
    row16 = lax.broadcasted_iota(i32, (16, 256), 0)
    lane256 = lax.broadcasted_iota(i32, (16, 256), 1)
    marks = (row16 == lane256 // 128).astype(f32).astype(bf16)
    for b in range(2):
        keys = kv[:, b, :, 0:128].reshape(D, 128)
        values = kv[:, b, :, 128:256].reshape(D, 128)
        queries = q[:, b].reshape(256, 128)
        turned = queries.astype(f32).T.astype(bf16)
        grads = mg[:, b].reshape(256, 128).astype(f32)
        together = jnp.zeros((256, 128), f32)
        for j in range(2):
            inverse = rl[b * 2 + j]
            e = exps[b * 2 + j].ready()
            scaled = jnp.where(head_lane == j, grads * inverse, 0.0)
            mine = scaled.astype(bf16)
            d_ref[...] = nt(mine, values)

            def some_rows(i, carry, b=b, j=j, e=e):
                at = pl.ds(pl.multiple_of(i * 16, 16), 16)
                p = e[at, :].astype(f32)
                d = d_ref[at, :]
                inner = jnp.sum(p * d, axis=1, keepdims=True) * rl[b * 2 + j, at, :]
                ds_ref[at, 0:D] = (p * (d - inner)).astype(bf16)
                return carry

            lax.fori_loop(0, 16, some_rows, 0, unroll=2)
            score_grad = ds_ref[:, 0:D]
            together = jnp.where(head_lane == j, nn(score_grad, keys), together)
            left = jnp.concatenate([turned[j * HEAD : (j + 1) * HEAD, :], marks], axis=0)
            key_t = nn(left, score_grad)
            value_t = nn(scaled.T[j * HEAD : (j + 1) * HEAD, :].astype(bf16), e[...])
            for chip in range(8):
                lanes = slice(chip * 256, (chip + 1) * 256)
                at = chip * 256 + j * HEAD
                dkv[at : at + HEAD, b * 256 : (b + 1) * 256] = key_t[0:HEAD, lanes].astype(bf16)
                dkv[at + 128 : at + 128 + HEAD, b * 256 : (b + 1) * 256] = value_t[
                    :, lanes
                ].astype(bf16)
            for half in range(2):
                tile, lanes = band_tiles(me, half)
                rows = slice(half * 128, (half + 1) * 128)
                for t in range(3):
                    cols = slice(t * 128, (t + 1) * 128)
                    band[j, :, cols] = band[j, :, cols] + ds_ref[
                        rows, pl.ds(lanes[t], 128)
                    ].astype(f32)
                line = key_t[HEAD + half : HEAD + half + 1, :]
                far[j][0] = far[j][0] + jnp.where(tile_of < tile - 1, line, 0.0)
                far[j][1] = far[j][1] + jnp.where(tile_of > tile + 1, line, 0.0)
        dq[:, b] = together.astype(bf16).reshape(2, 128, 128)
        dkv.send_part((slice(None), pl.ds(b * 256, 256)))
    ids = band_buckets()
    lane = lax.broadcasted_iota(i32, (BUCKETS, 128), 1)
    bucket = lax.broadcasted_iota(i32, (BUCKETS, 1), 0)
    result = jnp.zeros((BUCKETS, 128), f32)
    for j in range(2):
        near = band[j]
        lines = [
            jnp.sum(jnp.where(ids == b, near, 0.0), axis=0, keepdims=True) for b in range(BUCKETS)
        ]
        column = jnp.sum(jnp.concatenate(lines, axis=0), axis=1, keepdims=True)
        column = column + jnp.where(bucket == 15, jnp.sum(far[j][0]), 0.0)
        column = column + jnp.where(bucket == 31, jnp.sum(far[j][1]), 0.0)
        result = jnp.where(lane == j, column, result)
    tab[...] = result


def summed(parts, first, rows):
    total = parts[first : first + rows, :].astype(f32)
    for k in range(1, 8):
        total = total + parts[k * 32 + first : k * 32 + first + rows, :].astype(f32)
    return total


def spread_rows(res, first, rows, value):
    at = pl.ds(first, rows)
    res[at, :] = value.astype(bf16)
    size = res.ref.shape[0]
    for t in range(res.times):
        res.start(res.ref.at[at], res.there.at[pl.ds(t * size + first, rows)])


def norm_two_kernel(me, parts, x, gains, hid, normed):
    for first in (0, 16):
        rows = slice(first, first + 16)
        hidden_in = summed(parts, first, 16) + x[rows, :].astype(f32)
        rinv = lax.rsqrt(jnp.mean(hidden_in * hidden_in, axis=1, keepdims=True) + epsilon)
        spread_rows(normed, first, 16, hidden_in * rinv * gains[1:2, :])
        hid[rows, :] = hidden_in


def norm_back(value, grad, gain):
    rinv = lax.rsqrt(jnp.mean(value * value, axis=1, keepdims=True) + epsilon)
    u = grad * gain
    return rinv * u - (rinv * rinv * rinv) * value * jnp.mean(u * value, axis=1, keepdims=True)


def live_rows(me, half, b, first, count):
    c = me.c
    core = c if half == 0 else 1 - c
    place = (me.sc * 2 + core) * 128 + first + lax.broadcasted_iota(i32, (count, 1), 0)
    return place < me.lengths[b]


def norm_two_back_kernel(me, parts, hid, cot, gains, hig, low):
    b = me.h // 4
    for first in (0, 16):
        rows = slice(first, first + 16)
        place = (
            (me.sc * 2 + me.c) * 128
            + (me.h - b * 4) * 32
            + first
            + lax.broadcasted_iota(i32, (16, 1), 0)
        )
        total = summed(parts, first, 16)
        grad = norm_back(hid[rows, :], total, gains[1:2, :])
        grad = grad + jnp.where(place < jnp.where(b == 0, me.lengths[0], me.lengths[1]), cot[rows, :].astype(f32), 0.0)
        spread_rows(low, first, 16, grad)
        hig[rows, :] = grad


def norm_one_back_kernel(me, parts, layer, x, gains, hig, res):
    spread_rows(res, 32, 32, layer[...])
    for first in (0, 16):
        rows = slice(first, first + 16)
        total = summed(parts, first, 16)
        grad = norm_back(x[rows, :].astype(f32), total, gains[0:1, :]) + hig[rows, :]
        spread_rows(res, first, 16, grad)


def gelu_pair(g):
    k0, k1 = 0.7978845608028654, 0.044715
    g2 = g * g
    t = jnp.tanh(k0 * g * (1.0 + k1 * g2))
    value = 0.5 * g * (1.0 + t)
    slope = 0.5 * (1.0 + t) + 0.5 * g * (1.0 - t * t) * k0 * (1.0 + 3.0 * k1 * g2)
    return value, slope


def ffn_kernel(me, n_own, cot_own, cot_sib, gains, first, n_sib, *refs):
    blocks = (first, *refs[:7])
    hidden, gu_low, out_low, own, sib, out_own, out_sib, gain_sum = refs[7:]
    c = me.c
    for half, n, cot in ((0, n_own, cot_own), (1, n_sib, cot_sib)):
        rows = rows_of(half)
        live = jnp.concatenate(
            [live_rows(me, half, b, 0, 128) for b in range(2)], axis=0
        )
        out_low[rows, :] = jnp.where(live, cot[...], jnp.zeros((), bf16))
        gate_a = jnp.zeros((256, 256), f32)
        up_a = jnp.zeros((256, 256), f32)
        rest = jnp.zeros((256, 128), f32)
        back = jnp.zeros((256, FFC), f32)
        for k in range(8):
            chip = me.idx[k]
            v = chunk_p(n, slice(None), chip, c)
            w = blocks[k]
            gate_a = gate_a + nn(v, w[320:576, :])
            up_a = up_a + nn(v, w[576:832, :])
            rest = rest + nn(v[:, 0:128], w[832:960, 0:128])
            rest = rest + nn(v[:, 128:256], w[832:960, 128:256])
            back = back + nt(chunk_p(out_low, rows, chip, c), w[0:320, :])
        for gate, up, dh, at, size in (
            (gate_a, up_a, back[:, 0:256], 0, 256),
            (rest[:, 0:64], rest[:, 64:128], back[:, 256:FFC], 256, 64),
        ):
            value, slope = gelu_pair(gate)
            hidden[rows, at : at + size] = (value * up).astype(bf16)
            gate_low = (dh * up * slope).astype(bf16)
            up_low = (dh * value).astype(bf16)
            first = 0 if at == 0 else 512
            gu_low[rows, first : first + size] = gate_low
            gu_low[rows, first + size : first + 2 * size] = up_low

    hidden.send()
    gu_low.send()
    out_low.send()
    for k in range(8):
        chip = me.idx[k]
        w = blocks[k]
        wide = jnp.concatenate(
            [
                w[320:576, :],
                w[576:832, :],
            ],
            axis=1,
        )
        sums = []
        for half, n, res in ((0, n_own, own), (1, n_sib, sib)):
            low = gu_low[rows_of(half), :]
            part = nt(low[:, 0:512], wide)
            for p, core in ((0, c), (1, 1 - c)):
                lanes = pl.ds(lane_at(chip, core), 128)
                cols = slice(p * 128, (p + 1) * 128)
                piece = part[:, cols] + nt(low[:, 512:640], w[832:960, cols])
                sums.append(
                    jnp.sum(piece * n[:, lanes].astype(f32), axis=0, keepdims=True)
                )
                res[:, lanes] = piece.astype(bf16)
        for p, core in ((0, c), (1, 1 - c)):
            lanes = pl.ds(lane_at(chip, core), 128)
            gain_sum[0:1, lanes] = (sums[p] + sums[2 + p]) / gains[1:2, lanes]
        for half, res in ((0, out_own), (1, out_sib)):
            part = nn(hidden[rows_of(half), :], w[0:320, :]).astype(bf16)
            for p, core in ((0, c), (1, 1 - c)):
                res[:, pl.ds(lane_at(chip, core), 128)] = part[:, p * 128 : (p + 1) * 128]


def ffn_weights_kernel(me, hidden, out_low, n_own, n_sib, gu_low, *results, ranks):
    c = me.c
    for k, res in zip(ranks, results):
        chip = me.idx[k]
        res[0:320, :] = tn(hidden[...], chunk_p(out_low, slice(None), chip, c)).astype(bf16)
        v = jnp.concatenate(
            [chunk_p(n_own, slice(None), chip, c), chunk_p(n_sib, slice(None), chip, c)], axis=0
        )
        part = tn(v, gu_low[...]).astype(bf16)
        res[320:576, :] = part[:, 0:256]
        res[576:832, :] = part[:, 256:512]
        res[832:960, 0:128] = part[0:128, 512:640]
        res[832:960, 128:256] = part[128:256, 512:640]
        res.send()


def layer_join_kernel(me, own, recv, hid, res):
    res[...] = (own[...].astype(f32) + recv[...].astype(f32)).astype(bf16)
    at = pl.ds(pl.multiple_of(me.h * 32, 32), 32)
    res[at, :] = (own[at, :].astype(f32) + recv[at, :].astype(f32) + hid[...]).astype(bf16)


def qkv_back_kernel(me, parts, q_low, w, n1, gains, kv_low, own, sib, gain_sum):
    c = me.c
    total = parts[0:256, :].astype(f32)
    for k in range(1, 8):
        total = total + parts[k * 256 : (k + 1) * 256, :].astype(f32)
    for b in range(2):
        for half in range(2):
            lanes = slice(b * 256 + half * 128, b * 256 + (half + 1) * 128)
            kv_low[half * 256 + b * 128 : half * 256 + (b + 1) * 128, :] = total[:, lanes].T.astype(
                bf16
            )
    for k in range(8):
        wk = jnp.concatenate(
            [
                w[2 * k + p, 0:128, 0:384]
                for p in (c, 1 - c)
            ],
            axis=0,
        )
        lanes = slice(k * 256, (k + 1) * 256)
        line = jnp.zeros((1, 256), f32)
        for half, res in ((0, own), (1, sib)):
            rows = rows_of(half)
            part = nt(q_low[rows, :], wk[:, 0:128]) + nt(kv_low[rows, :], wk[:, 128:384])
            line = line + jnp.sum(part * n1[rows, lanes].astype(f32), axis=0, keepdims=True)
            res[:, lanes] = part.astype(bf16)
        gain_sum[0:1, lanes] = line / gains[0:1, lanes]


def early_weights_kernel(me, n1, q_low, mixed, al_own, al_sib, *results):
    c = me.c
    for k in range(8):
        chip = me.idx[k]
        res = results[k // 2].at[k % 2]
        al = jnp.concatenate(
            [chunk_p(al_own, slice(None), chip, c), chunk_p(al_sib, slice(None), chip, c)], axis=0
        )
        res[0:128, :] = tn(mixed[...], al).astype(bf16)
        part = tn(chunk_p(n1, slice(None), chip, c), q_low[...]).astype(bf16)
        res[128:256, 0:128] = part[0:128]
        res[128:256, 128:256] = part[128:256]
        if k % 2:
            results[k // 2].send()


def last_weights_kernel(me, n1, kv_low, g1, g2, tab, *results):
    c = me.c
    for k in range(8):
        chip = me.idx[k]
        res = results[k // 2].at[k % 2]
        part = tn(chunk_p(n1, slice(None), chip, c), kv_low[...]).astype(bf16)
        for p in range(2):
            rows, lanes = slice(p * 128, (p + 1) * 128), slice(p * 128, (p + 1) * 128)
            res[0:128, lanes] = part[rows, 0:128]
            res[128:256, lanes] = part[rows, 128:256]
        one = slice(0, 1)
        misc = jnp.concatenate(
            [
                chunk_p(g1, one, chip, c),
                chunk_p(g2, one, chip, c),
                tab[pl.ds(chip, 1), :],
                jnp.zeros((13, 256), f32),
            ],
            axis=0,
        )
        res[256:272, :] = misc.astype(bf16)
        if k % 2:
            results[k // 2].send()


def layer_sum_kernel(me, parts, res):
    res[...] = summed(parts, 0, 32).astype(bf16)


def ffn_sum_kernel(me, *refs):
    parts, results = refs[:6], refs[6:]
    for y, res in enumerate(results):
        value = parts[y][...].astype(f32)
        for a in parts[2 + y :: 2]:
            value = value + a[...].astype(f32)
        res[...] = value.astype(res.ref.dtype)
        res.send()


def last_sum_kernel(me, *refs):
    early, late, (own, other, misc) = refs[:4], refs[4:8], refs[8:]
    for y, res in ((1, other), (0, own)):
        for parts, rows in ((early, slice(0, 256)), (late, slice(256, 528))):
            value = parts[0][y].astype(f32)
            for a in parts[1:]:
                value = value + a[y].astype(f32)
            res[rows, :] = value.astype(f32 if y == 0 else bf16)
        misc[y] = value[256:272]


def last_split_kernel(me, own, recv, mine, theirs):
    total = own[...] + recv[...].astype(f32)
    mine[...] = jnp.concatenate([total[k * 128 : (k + 1) * 128, 0:128] for k in range(4)], axis=1)
    theirs[...] = jnp.concatenate(
        [total[k * 128 : (k + 1) * 128, 128:256] for k in range(4)], axis=1
    ).astype(bf16)


def ffn_split_kernel(me, own, recv, mine, theirs):
    for p, res in ((1, theirs), (0, mine)):
        lanes = slice(p * 128, (p + 1) * 128)
        rows = [(0, 320, lanes)]
        for first in (320, 576):
            rows += [(first + p * 128, 128, slice(0, 128)), (first + p * 128, 128, slice(128, 256))]
        rows.append((832, 128, lanes))
        at = 0
        for first, size, cols in rows:
            value = own[first : first + size, cols] + recv[first : first + size, cols].astype(f32)
            res[at : at + size, :] = value.astype(bf16 if p else f32)
            at += size


def ffn_order_kernel(me, mine, recv, gate_grad, up_grad, down_grad):
    first = me.c == 0
    a, b = mine[0:320, :], recv[0:320, :].astype(f32)
    down_grad[0:320, :] = jnp.where(first, a, b)
    down_grad[320:640, :] = jnp.where(first, b, a)
    down_grad.send()
    for at, lane, res in ((320, 0, gate_grad), (576, 64, up_grad)):
        sides = []
        for ref in (mine, recv):
            rest = ref[832:960, lane : lane + 64]
            sides.append(
                jnp.concatenate([ref[at : at + 128, :], ref[at + 128 : at + 256, :], rest], axis=1)
            )
        a, b = sides[0], sides[1].astype(f32)
        res[...] = jnp.concatenate([jnp.where(first, a, b), jnp.where(first, b, a)], axis=1)
        res.send()


def last_order_kernel(me, mine, recv, out_grad, query_grad, key_grad, value_grad):
    a, b = mine[...], recv[...].astype(f32)
    low, high = jnp.where(me.c == 0, a, b), jnp.where(me.c == 0, b, a)
    out_grad[0:128, :] = low[:, 0:128]
    out_grad[128:256, :] = high[:, 0:128]
    for k, res in ((1, query_grad), (2, key_grad), (3, value_grad)):
        cols = slice(k * 128, (k + 1) * 128)
        res[:, 0:128] = low[:, cols]
        res[:, 128:256] = high[:, cols]


def to_sibling(a):
    return lax.ppermute(a, "seq", CORE)


def over_head(a):
    return lax.all_to_all(a, "head", 0, 0, tiled=True)


def over_chips(a):
    return lax.all_to_all(a, "seq", 0, 0, axis_index_groups=CHIP_GROUPS, tiled=True)


def body(
    inputs,
    cotangent,
    lengths,
    attn_gain,
    w_query,
    w_key,
    w_value,
    w_out,
    bias_table,
    ffn_gain,
    w_gate,
    w_up,
    w_down,
):
    s = lax.axis_index("seq")
    first = s % 2 == 0
    scalars = place_scalars(lengths)

    def halves(a, axis):
        low, high = jnp.split(a, 2, axis=axis)
        return jnp.where(first, low, high), jnp.where(first, high, low)

    def in_order(own, sib, axis):
        return jnp.where(
            first,
            jnp.concatenate([own, sib], axis=axis),
            jnp.concatenate([sib, own], axis=axis),
        )

    def on(kernel, outs, *args, **more):
        return call(kernel, outs, scalars, *args, **more)

    mine, theirs = on(
        pack_kernel,
        [((144, 512), bf16)] * 2,
        Far(w_query),
        Far(w_key),
        Far(w_value),
        Far(w_out),
        Far(attn_gain.reshape(1, 128)),
        Far(ffn_gain.reshape(1, 128)),
        Far(bias_table),
        scratch=[pltpu.VMEM((16, 512), f32)],
        name="pack",
    )
    block = jnp.concatenate([mine, to_sibling(theirs)], axis=0)
    w_attn = over_chips(jnp.broadcast_to(block[None], (8, 288, 512)).reshape(8 * 288, 512))
    w_attn = w_attn.reshape(16, 144, 512)

    x_own = inputs.reshape(256, D)
    x_sib = to_sibling(x_own)
    cot_own = cotangent.reshape(256, D)
    cot_sib = to_sibling(cot_own)

    down_mine, down_theirs = halves(w_down, 0)
    gate_mine, gate_theirs = halves(w_gate, 1)
    up_mine, up_theirs = halves(w_up, 1)

    def joined(gate, up):
        return jnp.concatenate(
            [gate[:, 0:256], up[:, 0:256], gate[:, 256:FFC], up[:, 256:FFC]], axis=1
        )

    gu_mine = joined(gate_mine, up_mine)
    down_recv = to_sibling(down_theirs)
    gu_recv = to_sibling(joined(gate_theirs, up_theirs))
    block = jnp.concatenate(
        [
            jnp.concatenate([down_mine, down_recv], axis=1),
            jnp.concatenate([gu_mine[:, 0:256], gu_recv[:, 0:256]], axis=0),
            jnp.concatenate([gu_mine[:, 256:512], gu_recv[:, 256:512]], axis=0),
            jnp.concatenate([gu_mine[:, 512:640], gu_recv[:, 512:640]], axis=1),
        ],
        axis=0,
    )

    def with_sibling(own, sib):
        return (own.astype(f32) + to_sibling(sib).astype(f32)).astype(bf16)

    def along_z(a, steps):
        return lax.ppermute(a, "seq", ALONG_Z[steps % 4])

    def other_y(a):
        return lax.ppermute(a, "seq", OTHER_Y)

    tie = lax.optimization_barrier
    half, part, line = ((256, D), bf16), ((256, D), bf16), ((1, D), f32)

    n1, q, kv, gains = on(
        qkv_kernel,
        [((512, D), bf16, 1), ((512, 128), bf16, 1), ((512, 256), bf16, 8), ((2, D), f32, 1)],
        x_own,
        Far(x_sib),
        Far(w_attn),
        vmem=16,
        name="qkv",
    )
    q = q.reshape(2, 2, 128, 128)
    kv, block = tie((over_chips(kv), block))
    kv = kv.reshape(16, 2, 128, 256)
    w_parts = Far(w_attn, (slice(None), pl.ds(0, 128), pl.ds(384, 128)))
    rows = w_attn.reshape(8, 2, 144, 512)[:, :, 129:131, 0:4].astype(f32)
    rows = jnp.where(first, rows, rows[:, ::-1]).reshape(BUCKETS, 4)
    table = jnp.where(first, rows[:, 0:2], rows[:, 2:4])
    *exps, rl, mixed, own, sib = on(
        attend_kernel,
        [((256, D), bf16, 1)] * 4 + [((4, 256, 1), f32, 1), ((2, 2, 128, 128), bf16, 1), half, half],
        Far(q),
        Far(kv),
        w_parts,
        smem=(table,),
        scratch=[pltpu.VMEM((256, D + 128), f32), pltpu.VMEM((2, 128, 384), f32)],
        vmem=24, name="attend",
    )
    mixed = mixed.reshape(512, 128)
    flipped = other_y(block)
    sib, flipped = tie((sib, flipped))
    attn, block, flipped = tie((with_sibling(own, sib), block, flipped))
    attn, up_a, up_b, down_a, down_b = tie(
        (
            over_head(attn),
            along_z(block, 1),
            along_z(flipped, 1),
            along_z(block, 3),
            along_z(flipped, 3),
        )
    )
    hid, n2 = on(
        norm_two_kernel,
        [((32, D), f32, 1), ((32, D), bf16, 8)],
        attn,
        Rows(x_own),
        Far(gains),
        name="norm_two",
    )
    n2, up_a, down_b = tie((n2, up_a, down_b))
    n_own, far_a, far_b = tie((over_head(n2), along_z(up_a, 1), along_z(down_b, 3)))
    blocks = [block, flipped, up_a, up_b, down_a, down_b, far_a, far_b]
    n_sib = to_sibling(n_own)

    hidden, gu_low, out_low, own, sib, out_own, out_sib, g2 = on(
        ffn_kernel,
        [
            ((512, FFC), bf16, 1),
            ((512, 640), bf16, 1),
            ((512, D), bf16, 1),
            part,
            part,
            part,
            part,
            line,
        ],
        n_own,
        Far(cot_own),
        Far(cot_sib),
        Far(gains),
        Far(blocks[0]),
        n_sib,
        *[Far(a) for a in blocks[1:]],
        vmem=26,
        name="ffn",
    )
    def weight_grads(name, ranks):
        return on(
            functools.partial(ffn_weights_kernel, ranks=ranks),
            [((960, 256), bf16, 1)] * len(ranks),
            Far(hidden),
            Far(out_low),
            Far(n_own),
            Far(n_sib),
            Far(gu_low),
            vmem=18,
            name=name,
        )

    far_a, far_b = weight_grads("ffn_weights_far", (6, 7))
    fore_a, back_b = weight_grads("ffn_weights_next", (4, 3))
    (out_own,) = on(
        layer_join_kernel, [part], out_own, to_sibling(out_sib), Far(hid), name="layer_join"
    )
    ffn_sum, fore_recv, back_recv, fore_a, back_b, out_own = tie(
        (
            over_head(with_sibling(own, sib)),
            along_z(far_a, 1),
            along_z(far_b, 3),
            fore_a,
            back_b,
            out_own,
        )
    )
    hig, low = on(
        norm_two_back_kernel,
        [((32, D), f32, 1), ((32, D), bf16, 8)],
        ffn_sum,
        Far(hid),
        Rows(cot_own),
        Far(gains),
        name="norm_two_back",
    )
    low, fore_recv, back_recv = tie((low, fore_recv, back_recv))
    fore_a = (fore_a.astype(f32) + fore_recv.astype(f32)).astype(bf16)
    back_b = (back_b.astype(f32) + back_recv.astype(f32)).astype(bf16)
    fore_b, back_a = weight_grads("ffn_weights_last", (5, 2))
    al_own, fore_a, back_b, fore_b, back_a, out_own = tie(
        (over_head(low), along_z(fore_a, 1), along_z(back_b, 3), fore_b, back_a, out_own)
    )
    al_sib = to_sibling(al_own)

    out_parts = over_head(out_own)
    q_low, dkv, tab = on(
        attend_back_kernel,
        [((2, 2, 128, 128), bf16, 1), ((8 * 256, 512), bf16, 1), ((BUCKETS, 128), f32)],
        w_parts,
        al_own,
        al_sib,
        Far(q),
        Far(kv),
        Far(rl),
        *[Far(e) for e in exps],
        scratch=[
            pltpu.VMEM((256, D), f32),
            pltpu.VMEM((256, D + 128), bf16),
            pltpu.VMEM((2, 128, 384), f32),
            pltpu.VMEM((2, 2, 128, 128), bf16),
        ],
        vmem=28, name="attend_back",
    )
    dkv, out_parts, fore_b, back_a = tie(
        (dkv, out_parts, along_z(fore_b, 1), along_z(back_a, 3))
    )
    q_low = q_low.reshape(512, 128)

    (layer_out,) = on(layer_sum_kernel, [((32, D), bf16)], out_parts, name="layer_sum")
    early = on(
        early_weights_kernel,
        [((2, 256, 256), bf16, 1)] * 4,
        Far(n1),
        Far(q_low),
        Far(mixed),
        Far(al_own),
        Far(al_sib),
        vmem=14,
        name="early_weights",
    )
    near_a, near_b = weight_grads("ffn_weights_near", (0, 1))
    ffn_own, ffn_other = on(
        ffn_sum_kernel,
        [((960, 256), f32, 1), ((960, 256), bf16, 1)],
        *[Far(a) for a in (near_a, near_b, fore_a, fore_b, back_a, back_b)],
        vmem=12,
        name="ffn_sum",
    )
    kv_parts, layer_out, ffn_own, ffn_other, *early = tie(
        (over_chips(dkv), layer_out, ffn_own, ffn_other, *early)
    )
    kv_low, own, sib, g1 = on(
        qkv_back_kernel,
        [((512, 256), bf16, 1), part, part, line],
        kv_parts,
        Far(q_low),
        Far(w_attn),
        Far(n1),
        Far(gains),
        vmem=16,
        name="qkv_back",
    )

    rows = tab[:, 0:2].reshape(8, 2, 4)
    rows = jnp.where(first, rows, rows[:, ::-1])
    rows = jnp.pad(rows, ((0, 0), (0, 0), (0, 124))).reshape(8, 256)
    late = on(
        last_weights_kernel,
        [((2, 272, 256), bf16, 1)] * 4,
        Far(n1),
        Far(kv_low),
        g1,
        g2,
        rows,
        vmem=14,
        name="last_weights",
    )

    def gathered(near, back, fore, far):
        return near, along_z(fore, 1), along_z(back, 3), along_z(far, 2)

    one_sum, ffn_recv, *early = tie(
        (over_head(with_sibling(own, sib)), other_y(ffn_other), *gathered(*early))
    )
    (low,) = on(
        norm_one_back_kernel,
        [((64, D), bf16, 8)],
        one_sum,
        layer_out,
        Rows(x_own),
        Far(gains),
        Far(hig),
        name="norm_one_back",
    )
    low, *late = tie((low, *gathered(*late)))
    both = over_head(low).reshape(8, 64, D)
    input_grad = both[:, 0:32].astype(f32).reshape(2, 128, D)
    layer_out = both[:, 32:64].reshape(2, 128, D)
    last_own, last_other, misc = on(
        last_sum_kernel,
        [((528, 256), f32), ((528, 256), bf16), ((2, 16, 256), f32)],
        *[Far(a) for a in (*early, *late)],
        name="last_sum",
    )
    mine, theirs = on(
        last_split_kernel,
        [((128, 512), f32), ((128, 512), bf16)],
        last_own,
        other_y(last_other),
        name="last_split",
    )
    out_grad, query_grad, key_grad, value_grad = on(
        last_order_kernel,
        [((256, 128), f32, 1)] + [((128, 256), f32, 1)] * 3,
        mine,
        to_sibling(theirs),
        name="last_order",
    )
    misc = misc[0] + other_y(misc[1])
    small = to_sibling(misc[:, 128:256])
    gain_sums = misc[0:2, 0:128] + small[0:2, :]
    for swap in HEAD_PAIRS:
        gain_sums = gain_sums + lax.ppermute(gain_sums, "head", swap)
    table_grad = in_order(misc[2, 0:4].reshape(2, 2), small[2, 0:4].reshape(2, 2), 1)

    mine, theirs = on(
        ffn_split_kernel,
        [((960, 128), f32), ((960, 128), bf16)],
        Far(ffn_own),
        ffn_recv,
        name="ffn_split",
    )
    gate_grad, up_grad, down_grad = on(
        ffn_order_kernel,
        [((128, 640), f32, 1), ((128, 640), f32, 1), ((640, 128), f32, 1)],
        mine,
        to_sibling(theirs),
        name="ffn_order",
    )
    return (
        layer_out,
        input_grad,
        gain_sums[0],
        query_grad,
        key_grad,
        value_grad,
        out_grad,
        table_grad,
        gain_sums[1],
        gate_grad,
        up_grad,
        down_grad,
    )


def solution(mesh):
    seq_head, head_seq = P("seq", "head"), P("head", "seq")
    in_specs = (
        P(None, "seq", None),
        P(None, "seq", None),
        P(),
        P("seq"),
        seq_head,
        seq_head,
        seq_head,
        head_seq,
        seq_head,
        P("seq"),
        seq_head,
        seq_head,
        head_seq,
    )
    out_specs = (
        P(None, "seq", None),
        P(None, "seq", None),
        P("seq"),
        seq_head,
        seq_head,
        seq_head,
        head_seq,
        seq_head,
        P("seq"),
        seq_head,
        seq_head,
        head_seq,
    )
    return jax.shard_map(body, mesh=mesh, in_specs=in_specs, out_specs=out_specs, check_vma=False)
```

```python
import functools

import jax
import jax.numpy as jnp
from jax import lax
from jax.experimental import pallas as pl
from jax.experimental.pallas import tpu as pltpu
from jax.sharding import PartitionSpec as P


D = 2048
HEAD = 64
BUCKETS = 32
FFC = 320
epsilon = 1e-06
limits = (8, 12, 16, 23, 32, 46, 64, 91)
masked_score = -1000000000.0

f32, bf16, i32 = jnp.float32, jnp.bfloat16, jnp.int32
MIB = 1024 * 1024

CHIP_GROUPS = [[s for s in range(16) if s % 2 == c] for c in range(2)]
RELATIVE = ((0, 0), (0, 1), (1, 0), (1, 1), (3, 0), (3, 1), (2, 0), (2, 1))
def seq_perm(f):
    return [
        (z * 4 + y * 2 + c, (lambda t: t[0] * 4 + t[1] * 2 + t[2])(f(z, y, c)))
        for z in range(4)
        for y in range(2)
        for c in range(2)
    ]


def head_perm(f):
    return [
        (x * 2 + y, (lambda t: t[0] * 2 + t[1])(f(x, y))) for x in range(4) for y in range(2)
    ]


CORE = seq_perm(lambda z, y, c: (z, y, 1 - c))
OTHER_Y = seq_perm(lambda z, y, c: (z, 1 - y, c))
ALONG_Z = {d: seq_perm(lambda z, y, c, d=d: ((z + d) % 4, y, c)) for d in (1, 2, 3)}
HEAD_PAIRS = [
    head_perm(lambda x, y: (x ^ 1, y)),
    head_perm(lambda x, y: (x ^ 2, y)),
    head_perm(lambda x, y: (x, 1 - y)),
]


def nn(a, b):
    return jnp.dot(a, b, preferred_element_type=f32)


def nt(a, b):
    return lax.dot_general(a, b, (((1,), (1,)), ((), ())), preferred_element_type=f32)


def tn(a, b):
    return lax.dot_general(a, b, (((0,), (0,)), ((), ())), preferred_element_type=f32)


class Loaded:
    def __init__(self, copy, ref, queue):
        self.copy, self.ref, self.queue, self.here = copy, ref, queue, False

    def ready(self):
        if not self.here:
            while self in self.queue:
                self.queue.pop(0).copy.start()
            self.copy.wait()
            self.here = True
            if self.queue:
                self.queue.pop(0).copy.start()
        return self.ref

    def __getitem__(self, at):
        return self.ready()[at]

    @property
    def at(self):
        return self.ready().at


class Stored:
    def __init__(self, ref, there, sems, times):
        self.ref, self.there, self.sems, self.times = ref, there, sems, times
        self.copies, self.whole = [], True

    def start(self, source, target):
        copy = pltpu.make_async_copy(source, target, self.sems.at[len(self.copies)])
        copy.start()
        self.copies.append(copy)

    def send(self):
        rows = self.ref.shape[0]
        for t in range(self.times):
            there = self.there if self.times == 1 else self.there.at[pl.ds(t * rows, rows)]
            self.start(self.ref, there)

    def send_part(self, at):
        self.start(self.ref.at[at], self.there.at[at])

    def __getitem__(self, at):
        return self.ref[at]

    def __setitem__(self, at, value):
        self.ref[at] = value

    @property
    def at(self):
        return self.ref.at


class Place:
    def __init__(self, scalars):
        self.c, self.sc, self.h = scalars[0], scalars[1], scalars[2]
        self.lengths = {0: scalars[3], 1: scalars[4]}
        self.idx = [scalars[5 + k] for k in range(8)]


def place_scalars(lengths):
    s, h = lax.axis_index("seq"), lax.axis_index("head")
    c, sc = s % 2, s // 2
    z, y = sc // 2, sc % 2
    idx = [((z + 4 - dz) % 4) * 2 + (y if dy == 0 else 1 - y) for dz, dy in RELATIVE]
    return jnp.stack([c, sc, h, lengths[0], lengths[1], *idx]).astype(i32)


class Far:
    def __init__(self, value, at=None):
        self.value, self.at = value, at

    def shape(self):
        return jax.eval_shape(lambda v: v if self.at is None else v[self.at], self.value).shape


class Rows(Far):
    def shape(self):
        return (32, self.value.shape[1])


def call(kernel, outs, lengths, *args, smem=(), scratch=(), vmem=8, ahead=16, name=None):
    n, m, fixed = len(args), len(outs), 1 + len(smem)
    far_in = [i for i, a in enumerate(args) if isinstance(a, Far)]
    far_out = [k for k, o in enumerate(outs) if len(o) == 3]

    def whole(*refs):
        lens, scalars, refs = refs[0], refs[1:fixed], refs[fixed:]
        inputs, outputs, refs = list(refs[:n]), list(refs[n : n + m]), list(refs[n + m :])
        queue = []
        for i in far_in:
            buf, sem = refs.pop(0), refs.pop(0)
            there = inputs[i]
            if isinstance(args[i], Rows):
                first = pl.multiple_of(lens[2] * 32, 32)
                there = there.at[pl.ds(first, 32)]
            elif args[i].at is not None:
                there = there.at[args[i].at]
            inputs[i] = Loaded(pltpu.make_async_copy(there, buf, sem), buf, queue)
            queue.append(inputs[i])
        for _ in range(min(ahead, len(queue))):
            queue.pop(0).copy.start()
        for k in far_out:
            buf, sems = refs.pop(0), refs.pop(0)
            outputs[k] = Stored(buf, outputs[k], sems, outs[k][2])
        kernel(Place(lens), *scalars, *inputs, *outputs, *refs)
        for i in far_in:
            inputs[i].ready()
        for k in far_out:
            if not outputs[k].copies:
                outputs[k].send()
        for k in far_out:
            for copy in outputs[k].copies:
                copy.wait()

    buffers = []
    for i in far_in:
        buffers += [pltpu.VMEM(args[i].shape(), args[i].value.dtype), pltpu.SemaphoreType.DMA]
    for k in far_out:
        shape, dtype, _ = outs[k]
        buffers += [pltpu.VMEM(shape, dtype), pltpu.SemaphoreType.DMA((24,))]
    placed = [
        pltpu.with_memory_space_constraint(a.value, pltpu.HBM)
        if isinstance(a, Far)
        else pltpu.with_memory_space_constraint(a, pltpu.VMEM)
        for a in args
    ]
    shapes = [
        pltpu.HBM((o[0][0] * o[2], *o[0][1:]), o[1])
        if len(o) == 3
        else pltpu.VMEM(o[0], o[1])
        for o in outs
    ]
    return pl.pallas_call(
        whole,
        out_shape=tuple(shapes),
        in_specs=[pl.BlockSpec(memory_space=pltpu.SMEM)] * fixed
        + [pl.BlockSpec(memory_space=pl.ANY if i in far_in else pltpu.VMEM) for i in range(n)],
        out_specs=tuple(
            pl.BlockSpec(memory_space=pl.ANY if k in far_out else pltpu.VMEM) for k in range(m)
        ),
        scratch_shapes=buffers + list(scratch),
        compiler_params=pltpu.CompilerParams(vmem_limit_bytes=vmem * MIB),
        cost_estimate=pl.CostEstimate(flops=1000, bytes_accessed=1000, transcendentals=0),
        name=name,
    )(lengths, *smem, *placed)


def lane_at(chip, core):
    return pl.multiple_of(chip * 256 + core * 128, 128)


def chunk_p(ref, rows, chip, c):
    return jnp.concatenate(
        [ref[rows, pl.ds(lane_at(chip, c), 128)], ref[rows, pl.ds(lane_at(chip, 1 - c), 128)]],
        axis=1,
    )


def rows_of(half):
    return slice(half * 256, (half + 1) * 256)


def pack_kernel(me, wq, wk, wv, wo, ga, gf, bias, mine, theirs, misc):
    misc[...] = jnp.zeros_like(misc)
    misc[0:1, 0:128] = ga[...].astype(f32)
    misc[0:1, 128:256] = gf[...].astype(f32)
    misc[1:3, 0:4] = bias[...].astype(f32)
    low = jnp.concatenate([wq[:, 0:128], wk[:, 0:128], wv[:, 0:128], wo[0:128, :]], axis=1)
    high = jnp.concatenate(
        [wq[:, 128:256], wk[:, 128:256], wv[:, 128:256], wo[128:256, :]], axis=1
    )
    theirs[0:128, :] = jnp.where(me.c == 0, high, low)
    mine[0:128, :] = jnp.where(me.c == 0, low, high)
    for res in (mine, theirs):
        res[128:144, :] = misc[...].astype(bf16)


def qkv_kernel(me, x_own, x_sib, w, n1, q, kv, gains):
    c = me.c
    rinvs = []
    for x in (x_own, x_sib):
        total = jnp.zeros((256, 1), f32)
        for k in range(8):
            v = x[:, k * 256 : (k + 1) * 256].astype(f32)
            total = total + jnp.sum(v * v, axis=1, keepdims=True)
        rinvs.append(lax.rsqrt(total * (1.0 / D) + epsilon))
    for k in range(8):
        for core, p in ((0, c), (1, 1 - c)):
            row = w[2 * k + p, 128:144, 0:256].astype(f32)[0:1]
            gains[0:1, k * 256 + core * 128 : k * 256 + core * 128 + 128] = row[:, 0:128]
            gains[1:2, k * 256 + core * 128 : k * 256 + core * 128 + 128] = row[:, 128:256]
    gains.send()
    for half, x, rinv in ((0, x_own, rinvs[0]), (1, x_sib, rinvs[1])):
        rows = rows_of(half)
        acc = jnp.zeros((256, 384), f32)
        for k in range(8):
            lanes = slice(k * 256, (k + 1) * 256)
            v = x[:, lanes].astype(f32)
            normed = (v * rinv * gains[0:1, lanes]).astype(bf16)
            n1[rows, lanes] = normed
            wk = jnp.concatenate(
                [w[2 * k + c, 0:128, 0:384], w[2 * k + 1 - c, 0:128, 0:384]], axis=0
            )
            acc = acc + nn(normed, wk)
        q[rows, :] = acc[:, 0:128].astype(bf16)
        kv[rows, :] = acc[:, 128:384].astype(bf16)
        for chip in range(8):
            kv.start(kv.ref.at[rows], kv.there.at[pl.ds(chip * 512 + half * 256, 256)])
        n1.send_part(rows)


def out_weights(me, w, k):
    return jnp.concatenate([w[2 * k + p] for p in (me.c, 1 - me.c)], axis=1)


def bucket_ids(offset):
    distance = jnp.abs(offset)
    coarse = 7 + sum(((distance >= threshold).astype(i32) for threshold in limits))
    within = jnp.where(distance < 8, distance, coarse)
    return within + jnp.where(offset > 0, 16, 0).astype(i32)


def band_buckets():
    return bucket_ids(
        lax.broadcasted_iota(i32, (128, 384), 1)
        - 128
        - lax.broadcasted_iota(i32, (128, 384), 0)
    )


def key_places(c):
    lane = lax.broadcasted_iota(i32, (1, D), 1)
    stored = lane // 128
    tile = (stored // 2) * 2 + jnp.where(stored % 2 == 1, 1 - c, c)
    return tile, tile * 128 + lane % 128


def band_tiles(me, half):
    c = me.c
    tile = me.sc * 2 + (c if half == 0 else 1 - c)
    lanes = []
    for step in (-1, 0, 1):
        near = tile + step
        stored = (near // 2) * 2 + jnp.where(near % 2 == 1, 1 - c, c)
        inside = jnp.logical_and(near >= 0, near < 16)
        lanes.append(pl.multiple_of(jnp.where(inside, stored, 16) * 128, 128))
    return tile, lanes


def band_kernel(me, table, band):
    ids = band_buckets()
    for j in range(2):
        value = jnp.zeros((128, 384), f32)
        for b in range(BUCKETS):
            value = jnp.where(ids == b, table[b, j], value)
        band[j] = value


def attend_kernel(me, table, q, kv, band, w, e0, e1, e2, e3, rl, mixed, own, sib, s_ref):
    exps = (e0, e1, e2, e3)
    c = me.c
    tile_of, place_of = key_places(c)
    head_lane = lax.broadcasted_iota(i32, (256, 128), 1) // HEAD
    for b in range(2):
        length = me.lengths[b]
        keys = kv[:, b, :, 0:128].reshape(D, 128)
        values = jnp.concatenate(
            [kv[:, b, :, 128:256].reshape(D, 128), jnp.ones((D, 128), bf16)], axis=1
        )
        queries = q[:, b].reshape(256, 128)
        together = jnp.zeros((256, 128), f32)
        for j in range(2):
            mine = jnp.where(head_lane == j, queries, jnp.zeros_like(queries))
            s_ref[:, 0:D] = nt(mine, keys)
            for half in range(2):
                tile, lanes = band_tiles(me, half)
                rows = slice(half * 128, (half + 1) * 128)
                for t in range(3):
                    at = pl.ds(lanes[t], 128)
                    s_ref[rows, at] = s_ref[rows, at] + band[j, :, t * 128 : (t + 1) * 128]
                added = jnp.where(place_of >= length, masked_score, 0.0) + jnp.where(
                    tile_of < tile - 1,
                    table[15, j],
                    jnp.where(tile_of > tile + 1, table[31, j], 0.0),
                )

                def some_rows(i, carry, half=half, added=added, b=b, j=j):
                    at = pl.ds(pl.multiple_of(half * 128 + i * 16, 16), 16)
                    s = s_ref[at, 0:D] + added
                    exps[b * 2 + j][at, :] = jnp.exp(
                        s - jnp.max(s, axis=1, keepdims=True)
                    ).astype(bf16)
                    return carry

                lax.fori_loop(0, 8, some_rows, 0, unroll=8)
            exps[b * 2 + j].send()
            wide = nn(exps[b * 2 + j][...], values)
            inverse = 1.0 / wide[:, 128:129]
            rl[b * 2 + j] = inverse
            together = jnp.where(head_lane == j, wide[:, 0:128] * inverse, together)
        mixed[:, b] = together.astype(bf16).reshape(2, 128, 128)
    rl.send()
    mixed.send()
    for half, res in ((1, sib), (0, own)):
        for k in range(8):
            res[:, k * 256 : (k + 1) * 256] = nn(
                mixed[half].reshape(256, 128), out_weights(me, w, k)
            ).astype(bf16)


def attend_back_kernel(
    me, w, al_own, al_sib, q, kv, rl, e0, e1, e2, e3, dq, dkv, band, far_out, d_ref, ds_ref, mg
):
    exps = (e0, e1, e2, e3)
    c = me.c
    for half, al in ((0, al_own), (1, al_sib)):
        acc = jnp.zeros((256, 128), f32)
        for k in range(8):
            acc = acc + nt(al[:, k * 256 : (k + 1) * 256], out_weights(me, w, k))
        mg[half] = acc.astype(bf16).reshape(2, 128, 128)
    tile_of, _ = key_places(c)
    head_lane = lax.broadcasted_iota(i32, (256, 128), 1) // HEAD
    ds_ref[:, D : D + 128] = jnp.zeros((256, 128), bf16)
    band[...] = jnp.zeros_like(band)
    far = [[jnp.zeros((1, D), f32) for _ in range(2)] for _ in range(2)]
    row16 = lax.broadcasted_iota(i32, (16, 256), 0)
    lane256 = lax.broadcasted_iota(i32, (16, 256), 1)
    marks = (row16 == lane256 // 128).astype(f32).astype(bf16)
    for b in range(2):
        keys = kv[:, b, :, 0:128].reshape(D, 128)
        values = kv[:, b, :, 128:256].reshape(D, 128)
        queries = q[:, b].reshape(256, 128)
        turned = queries.astype(f32).T.astype(bf16)
        grads = mg[:, b].reshape(256, 128).astype(f32)
        together = jnp.zeros((256, 128), f32)
        for j in range(2):
            inverse = rl[b * 2 + j]
            e = exps[b * 2 + j].ready()
            scaled = jnp.where(head_lane == j, grads * inverse, 0.0)
            mine = scaled.astype(bf16)
            d_ref[...] = nt(mine, values)

            def some_rows(i, carry, b=b, j=j, e=e):
                at = pl.ds(pl.multiple_of(i * 16, 16), 16)
                p = e[at, :].astype(f32)
                d = d_ref[at, :]
                inner = jnp.sum(p * d, axis=1, keepdims=True) * rl[b * 2 + j, at, :]
                ds_ref[at, 0:D] = (p * (d - inner)).astype(bf16)
                return carry

            lax.fori_loop(0, 16, some_rows, 0, unroll=16)
            score_grad = ds_ref[:, 0:D]
            together = jnp.where(head_lane == j, nn(score_grad, keys), together)
            left = jnp.concatenate([turned[j * HEAD : (j + 1) * HEAD, :], marks], axis=0)
            key_t = nn(left, score_grad)
            value_t = nn(scaled.T[j * HEAD : (j + 1) * HEAD, :].astype(bf16), e[...])
            for chip in range(8):
                lanes = slice(chip * 256, (chip + 1) * 256)
                at = chip * 256 + j * HEAD
                dkv[at : at + HEAD, b * 256 : (b + 1) * 256] = key_t[0:HEAD, lanes].astype(bf16)
                dkv[at + 128 : at + 128 + HEAD, b * 256 : (b + 1) * 256] = value_t[
                    :, lanes
                ].astype(bf16)
            for half in range(2):
                tile, lanes = band_tiles(me, half)
                rows = slice(half * 128, (half + 1) * 128)
                for t in range(3):
                    cols = slice(t * 128, (t + 1) * 128)
                    band[j, :, cols] = band[j, :, cols] + ds_ref[
                        rows, pl.ds(lanes[t], 128)
                    ].astype(f32)
                line = key_t[HEAD + half : HEAD + half + 1, :]
                far[j][0] = far[j][0] + jnp.where(tile_of < tile - 1, line, 0.0)
                far[j][1] = far[j][1] + jnp.where(tile_of > tile + 1, line, 0.0)
        dq[:, b] = together.astype(bf16).reshape(2, 128, 128)
        dkv.send_part((slice(None), pl.ds(b * 256, 256)))
    for j in range(2):
        for side in range(2):
            far_out[2 * j + side : 2 * j + side + 1, :] = far[j][side]


def table_kernel(me, band, far, tab):
    ids = band_buckets()
    lane = lax.broadcasted_iota(i32, (BUCKETS, 128), 1)
    bucket = lax.broadcasted_iota(i32, (BUCKETS, 1), 0)
    result = jnp.zeros((BUCKETS, 128), f32)
    for j in range(2):
        near = band[j]
        lines = [
            jnp.sum(jnp.where(ids == b, near, 0.0), axis=0, keepdims=True) for b in range(BUCKETS)
        ]
        column = jnp.sum(jnp.concatenate(lines, axis=0), axis=1, keepdims=True)
        sides = [jnp.sum(far[2 * j + k : 2 * j + k + 1, :], axis=1, keepdims=True) for k in (0, 1)]
        column = column + jnp.where(bucket == 15, sides[0], 0.0)
        column = column + jnp.where(bucket == 31, sides[1], 0.0)
        result = jnp.where(lane == j, column, result)
    tab[...] = result


def summed(parts, first, rows):
    total = parts[first : first + rows, :].astype(f32)
    for k in range(1, 8):
        total = total + parts[k * 32 + first : k * 32 + first + rows, :].astype(f32)
    return total


def spread_rows(res, first, rows, value):
    at = pl.ds(first, rows)
    res[at, :] = value.astype(bf16)
    size = res.ref.shape[0]
    for t in range(res.times):
        res.start(res.ref.at[at], res.there.at[pl.ds(t * size + first, rows)])


def norm_two_kernel(me, parts, x, gains, hid, normed):
    for first in (0, 16):
        rows = slice(first, first + 16)
        hidden_in = summed(parts, first, 16) + x[rows, :].astype(f32)
        rinv = lax.rsqrt(jnp.mean(hidden_in * hidden_in, axis=1, keepdims=True) + epsilon)
        spread_rows(normed, first, 16, hidden_in * rinv * gains[1:2, :])
        hid[rows, :] = hidden_in


def norm_back(value, grad, gain):
    rinv = lax.rsqrt(jnp.mean(value * value, axis=1, keepdims=True) + epsilon)
    u = grad * gain
    return rinv * u - (rinv * rinv * rinv) * value * jnp.mean(u * value, axis=1, keepdims=True)


def live_rows(me, half, b, first, count):
    c = me.c
    core = c if half == 0 else 1 - c
    place = (me.sc * 2 + core) * 128 + first + lax.broadcasted_iota(i32, (count, 1), 0)
    return place < me.lengths[b]


def norm_two_back_kernel(me, parts, hid, cot, gains, hig, low):
    b = me.h // 4
    for first in (0, 16):
        rows = slice(first, first + 16)
        place = (
            (me.sc * 2 + me.c) * 128
            + (me.h - b * 4) * 32
            + first
            + lax.broadcasted_iota(i32, (16, 1), 0)
        )
        total = summed(parts, first, 16)
        grad = norm_back(hid[rows, :], total, gains[1:2, :])
        grad = grad + jnp.where(place < jnp.where(b == 0, me.lengths[0], me.lengths[1]), cot[rows, :].astype(f32), 0.0)
        spread_rows(low, first, 16, grad)
        hig[rows, :] = grad


def norm_one_back_kernel(me, parts, layer, x, gains, hig, res):
    spread_rows(res, 32, 32, layer[...])
    for first in (0, 16):
        rows = slice(first, first + 16)
        total = summed(parts, first, 16)
        grad = norm_back(x[rows, :].astype(f32), total, gains[0:1, :]) + hig[rows, :]
        spread_rows(res, first, 16, grad)


def gelu_pair(g):
    k0, k1 = 0.7978845608028654, 0.044715
    g2 = g * g
    t = jnp.tanh(k0 * g * (1.0 + k1 * g2))
    value = 0.5 * g * (1.0 + t)
    slope = 0.5 * (1.0 + t) + 0.5 * g * (1.0 - t * t) * k0 * (1.0 + 3.0 * k1 * g2)
    return value, slope


def gate_up(w):
    wide = jnp.concatenate([w[320:576, :], w[576:832, :]], axis=1)
    rest = jnp.concatenate([w[832:960, 0:128], w[832:960, 128:256]], axis=0)
    return wide, rest


def weight_grad(me, k, res, hidden, out_low, n_own, n_sib, gu_low):
    chip, c = me.idx[k], me.c
    res[0:320, :] = tn(hidden[...], chunk_p(out_low, slice(None), chip, c)).astype(bf16)
    v = jnp.concatenate(
        [chunk_p(n_own, slice(None), chip, c), chunk_p(n_sib, slice(None), chip, c)], axis=0
    )
    part = tn(v, gu_low[...]).astype(bf16)
    res[320:576, :] = part[:, 0:256]
    res[576:832, :] = part[:, 256:512]
    res[832:960, 0:128] = part[0:128, 512:640]
    res[832:960, 128:256] = part[128:256, 512:640]
    res.send()


def ffn_kernel(me, n_own, cot_own, cot_sib, gains, first, n_sib, *refs):
    blocks = (first, *refs[:7])
    hidden, gu_low, out_low, own, sib, out_own, out_sib, gain_sum, far_a, far_b = refs[7:]
    c = me.c
    all_rows = slice(None)

    def tokens(chip):
        return jnp.concatenate(
            [chunk_p(n_own, all_rows, chip, c), chunk_p(n_sib, all_rows, chip, c)], axis=0
        )

    gu = jnp.zeros((512, 512), f32)
    rest = jnp.zeros((512, 128), f32)
    for k in range(8):
        if k == 2:
            for a in (*blocks[2:], cot_own, cot_sib, gains):
                a.ready()
        v = tokens(me.idx[k])
        wide, last = gate_up(blocks[k])
        gu = gu + nn(v, wide)
        rest = rest + nn(v, last)
    for half, cot in ((0, cot_own), (1, cot_sib)):
        live = jnp.concatenate([live_rows(me, half, b, 0, 128) for b in range(2)], axis=0)
        out_low[rows_of(half), :] = jnp.where(live, cot[...], jnp.zeros((), bf16))
    out_low.send()
    back = jnp.zeros((512, FFC), f32)
    for k in range(8):
        back = back + nt(chunk_p(out_low, all_rows, me.idx[k], c), blocks[k][0:320, :])
    for gate, up, dh, at, size in (
        (gu[:, 0:256], gu[:, 256:512], back[:, 0:256], 0, 256),
        (rest[:, 0:64], rest[:, 64:128], back[:, 256:FFC], 256, 64),
    ):
        value, slope = gelu_pair(gate)
        hidden[:, at : at + size] = (value * up).astype(bf16)
        at = 2 * at
        gu_low[:, at : at + size] = (dh * up * slope).astype(bf16)
        gu_low[:, at + size : at + 2 * size] = (dh * value).astype(bf16)
    hidden.send()
    gu_low.send()
    for k, res in ((6, far_a), (7, far_b)):
        weight_grad(me, k, res, hidden, out_low, n_own, n_sib, gu_low)
    for k in range(8):
        chip = me.idx[k]
        wide, last = gate_up(blocks[k])
        part = nt(gu_low[:, 0:512], wide) + nt(gu_low[:, 512:640], last)
        line = jnp.sum(part * tokens(chip).astype(f32), axis=0, keepdims=True)
        made = nn(hidden[...], blocks[k][0:320, :])
        for p, core in ((0, c), (1, 1 - c)):
            lanes = pl.ds(lane_at(chip, core), 128)
            cols = slice(p * 128, (p + 1) * 128)
            gain_sum[0:1, lanes] = line[:, cols] / gains[1:2, lanes]
            for half, res, out in ((0, own, out_own), (1, sib, out_sib)):
                res[:, lanes] = part[rows_of(half), cols].astype(bf16)
                out[:, lanes] = made[rows_of(half), cols].astype(bf16)


def ffn_weights_kernel(me, hidden, out_low, n_own, n_sib, gu_low, *results, ranks):
    for k, res in zip(ranks, results):
        weight_grad(me, k, res, hidden, out_low, n_own, n_sib, gu_low)


def layer_join_kernel(me, own, recv, hid, res):
    res[...] = (own[...].astype(f32) + recv[...].astype(f32)).astype(bf16)
    at = pl.ds(pl.multiple_of(me.h * 32, 32), 32)
    res[at, :] = (own[at, :].astype(f32) + recv[at, :].astype(f32) + hid[...]).astype(bf16)


def qkv_back_kernel(me, parts, q_low, w, n1, gains, kv_low, own, sib, gain_sum):
    c = me.c
    total = parts[0:256, :].astype(f32)
    for k in range(1, 8):
        total = total + parts[k * 256 : (k + 1) * 256, :].astype(f32)
    for b in range(2):
        for half in range(2):
            lanes = slice(b * 256 + half * 128, b * 256 + (half + 1) * 128)
            kv_low[half * 256 + b * 128 : half * 256 + (b + 1) * 128, :] = total[:, lanes].T.astype(
                bf16
            )
    for k in range(8):
        wk = jnp.concatenate(
            [
                w[2 * k + p, 0:128, 0:384]
                for p in (c, 1 - c)
            ],
            axis=0,
        )
        lanes = slice(k * 256, (k + 1) * 256)
        line = jnp.zeros((1, 256), f32)
        for half, res in ((0, own), (1, sib)):
            rows = rows_of(half)
            part = nt(q_low[rows, :], wk[:, 0:128]) + nt(kv_low[rows, :], wk[:, 128:384])
            line = line + jnp.sum(part * n1[rows, lanes].astype(f32), axis=0, keepdims=True)
            res[:, lanes] = part.astype(bf16)
        gain_sum[0:1, lanes] = line / gains[0:1, lanes]


def early_weights_kernel(me, n1, q_low, mixed, al_own, al_sib, *results):
    c = me.c
    for k in range(8):
        chip = me.idx[k]
        res = results[k // 2].at[k % 2]
        al = jnp.concatenate(
            [chunk_p(al_own, slice(None), chip, c), chunk_p(al_sib, slice(None), chip, c)], axis=0
        )
        res[0:128, :] = tn(mixed[...], al).astype(bf16)
        part = tn(chunk_p(n1, slice(None), chip, c), q_low[...]).astype(bf16)
        res[128:256, 0:128] = part[0:128]
        res[128:256, 128:256] = part[128:256]
        if k % 2:
            results[k // 2].send()


def last_weights_kernel(me, n1, kv_low, g1, g2, tab, *results):
    c = me.c
    for k in (6, 7, 5, 2, 4, 3, 0, 1):
        chip = me.idx[k]
        res = results[k]
        part = tn(chunk_p(n1, slice(None), chip, c), kv_low[...]).astype(bf16)
        for p in range(2):
            rows, lanes = slice(p * 128, (p + 1) * 128), slice(p * 128, (p + 1) * 128)
            res[0:128, lanes] = part[rows, 0:128]
            res[128:256, lanes] = part[rows, 128:256]
        one = slice(0, 1)
        misc = jnp.concatenate(
            [
                chunk_p(g1, one, chip, c),
                chunk_p(g2, one, chip, c),
                tab[pl.ds(chip, 1), :],
                jnp.zeros((13, 256), f32),
            ],
            axis=0,
        )
        res[256:272, :] = misc.astype(bf16)
        res.send()


def unpack_kernel(me, both, input_grad, layer):
    for h in range(8):
        rows = slice(h * 32, (h + 1) * 32)
        layer[rows, :] = both[h * 64 + 32 : (h + 1) * 64, :]
        input_grad[rows, :] = both[h * 64 : h * 64 + 32, :].astype(f32)
        layer.send_part(rows)
        input_grad.send_part(rows)


def layer_sum_kernel(me, parts, res):
    res[...] = summed(parts, 0, 32).astype(bf16)


def ffn_sum_kernel(me, *refs):
    parts, results = refs[:6], refs[6:]
    for y, res in enumerate(results):
        value = parts[y][...].astype(f32)
        for a in parts[2 + y :: 2]:
            value = value + a[...].astype(f32)
        res[...] = value.astype(res.ref.dtype)
        res.send()


def last_sum_kernel(me, *refs):
    early, late, (own, other, misc) = refs[:4], refs[4:10], refs[10:]
    for y, res in ((1, other), (0, own)):
        value = early[0][y].astype(f32)
        for a in early[1:]:
            value = value + a[y].astype(f32)
        res[0:256, :] = value.astype(f32 if y == 0 else bf16)
        value = late[y][...].astype(f32)
        for a in late[2 + y :: 2]:
            value = value + a[...].astype(f32)
        res[256:528, :] = value.astype(f32 if y == 0 else bf16)
        misc[y] = value[256:272]


def last_split_kernel(me, own, recv, mine, theirs):
    total = own[...] + recv[...].astype(f32)
    mine[...] = jnp.concatenate([total[k * 128 : (k + 1) * 128, 0:128] for k in range(4)], axis=1)
    theirs[...] = jnp.concatenate(
        [total[k * 128 : (k + 1) * 128, 128:256] for k in range(4)], axis=1
    ).astype(bf16)


def ffn_split_kernel(me, own, recv, mine, theirs):
    for p, res in ((1, theirs), (0, mine)):
        lanes = slice(p * 128, (p + 1) * 128)
        rows = [(0, 320, lanes)]
        for first in (320, 576):
            rows += [(first + p * 128, 128, slice(0, 128)), (first + p * 128, 128, slice(128, 256))]
        rows.append((832, 128, lanes))
        at = 0
        for first, size, cols in rows:
            value = own[first : first + size, cols] + recv[first : first + size, cols].astype(f32)
            res[at : at + size, :] = value.astype(bf16 if p else f32)
            at += size


def ffn_order_kernel(me, mine, recv, gate_grad, up_grad, down_grad):
    first = me.c == 0
    a, b = mine[0:320, :], recv[0:320, :].astype(f32)
    down_grad[0:320, :] = jnp.where(first, a, b)
    down_grad[320:640, :] = jnp.where(first, b, a)
    down_grad.send()
    for at, lane, res in ((320, 0, gate_grad), (576, 64, up_grad)):
        sides = []
        for ref in (mine, recv):
            rest = ref[832:960, lane : lane + 64]
            sides.append(
                jnp.concatenate([ref[at : at + 128, :], ref[at + 128 : at + 256, :], rest], axis=1)
            )
        a, b = sides[0], sides[1].astype(f32)
        res[...] = jnp.concatenate([jnp.where(first, a, b), jnp.where(first, b, a)], axis=1)
        res.send()


def last_order_kernel(me, mine, recv, out_grad, query_grad, key_grad, value_grad):
    a, b = mine[...], recv[...].astype(f32)
    low, high = jnp.where(me.c == 0, a, b), jnp.where(me.c == 0, b, a)
    out_grad[0:128, :] = low[:, 0:128]
    out_grad[128:256, :] = high[:, 0:128]
    for k, res in ((1, query_grad), (2, key_grad), (3, value_grad)):
        cols = slice(k * 128, (k + 1) * 128)
        res[:, 0:128] = low[:, cols]
        res[:, 128:256] = high[:, cols]


def to_sibling(a):
    return lax.ppermute(a, "seq", CORE)


def over_head(a):
    return lax.all_to_all(a, "head", 0, 0, tiled=True)


def over_chips(a):
    return lax.all_to_all(a, "seq", 0, 0, axis_index_groups=CHIP_GROUPS, tiled=True)


def body(
    inputs,
    cotangent,
    lengths,
    attn_gain,
    w_query,
    w_key,
    w_value,
    w_out,
    bias_table,
    ffn_gain,
    w_gate,
    w_up,
    w_down,
):
    s = lax.axis_index("seq")
    first = s % 2 == 0
    scalars = place_scalars(lengths)

    def halves(a, axis):
        low, high = jnp.split(a, 2, axis=axis)
        return jnp.where(first, low, high), jnp.where(first, high, low)

    def in_order(own, sib, axis):
        return jnp.where(
            first,
            jnp.concatenate([own, sib], axis=axis),
            jnp.concatenate([sib, own], axis=axis),
        )

    def on(kernel, outs, *args, **more):
        return call(kernel, outs, scalars, *args, **more)

    mine, theirs = on(
        pack_kernel,
        [((144, 512), bf16)] * 2,
        Far(w_query),
        Far(w_key),
        Far(w_value),
        Far(w_out),
        Far(attn_gain.reshape(1, 128)),
        Far(ffn_gain.reshape(1, 128)),
        Far(bias_table),
        scratch=[pltpu.VMEM((16, 512), f32)],
        name="pack",
    )
    block = jnp.concatenate([mine, to_sibling(theirs)], axis=0)
    w_attn = over_chips(jnp.broadcast_to(block[None], (8, 288, 512)).reshape(8 * 288, 512))
    w_attn = w_attn.reshape(16, 144, 512)

    x_own = inputs.reshape(256, D)
    x_sib = to_sibling(x_own)
    cot_own = cotangent.reshape(256, D)
    cot_sib = to_sibling(cot_own)

    down_mine, down_theirs = halves(w_down, 0)
    gate_mine, gate_theirs = halves(w_gate, 1)
    up_mine, up_theirs = halves(w_up, 1)

    def joined(gate, up):
        return jnp.concatenate(
            [gate[:, 0:256], up[:, 0:256], gate[:, 256:FFC], up[:, 256:FFC]], axis=1
        )

    gu_mine = joined(gate_mine, up_mine)
    down_recv = to_sibling(down_theirs)
    gu_recv = to_sibling(joined(gate_theirs, up_theirs))
    block = jnp.concatenate(
        [
            jnp.concatenate([down_mine, down_recv], axis=1),
            jnp.concatenate([gu_mine[:, 0:256], gu_recv[:, 0:256]], axis=0),
            jnp.concatenate([gu_mine[:, 256:512], gu_recv[:, 256:512]], axis=0),
            jnp.concatenate([gu_mine[:, 512:640], gu_recv[:, 512:640]], axis=1),
        ],
        axis=0,
    )

    def with_sibling(own, sib):
        return (own.astype(f32) + to_sibling(sib).astype(f32)).astype(bf16)

    def along_z(a, steps):
        return lax.ppermute(a, "seq", ALONG_Z[steps % 4])

    def other_y(a):
        return lax.ppermute(a, "seq", OTHER_Y)

    tie = lax.optimization_barrier
    half, part, line = ((256, D), bf16), ((256, D), bf16), ((1, D), f32)

    n1, q, kv, gains = on(
        qkv_kernel,
        [((512, D), bf16, 1), ((512, 128), bf16, 1), ((512, 256), bf16, 8), ((2, D), f32, 1)],
        x_own,
        Far(x_sib),
        Far(w_attn),
        vmem=16,
        name="qkv",
    )
    q = q.reshape(2, 2, 128, 128)
    rows = w_attn.reshape(8, 2, 144, 512)[:, :, 129:131, 0:4].astype(f32)
    rows = jnp.where(first, rows, rows[:, ::-1]).reshape(BUCKETS, 4)
    table = jnp.where(first, rows[:, 0:2], rows[:, 2:4])
    (band,) = on(band_kernel, [((2, 128, 384), f32)], smem=(table,), name="band")
    kv, block, band = tie((over_chips(kv), block, band))
    kv = kv.reshape(16, 2, 128, 256)
    w_parts = Far(w_attn, (slice(None), pl.ds(0, 128), pl.ds(384, 128)))
    *exps, rl, mixed, own, sib = on(
        attend_kernel,
        [((256, D), bf16, 1)] * 4 + [((4, 256, 1), f32, 1), ((2, 2, 128, 128), bf16, 1), half, half],
        Far(q),
        Far(kv),
        band,
        w_parts,
        smem=(table,),
        scratch=[pltpu.VMEM((256, D + 128), f32)],
        vmem=24, name="attend",
    )
    mixed = mixed.reshape(512, 128)
    flipped = other_y(block)
    sib, flipped, up_a, down_a = tie((sib, flipped, along_z(block, 1), along_z(block, 3)))
    attn, flipped = tie((with_sibling(own, sib), flipped))
    attn, up_b, down_b = tie((over_head(attn), along_z(flipped, 1), along_z(flipped, 3)))
    hid, n2 = on(
        norm_two_kernel,
        [((32, D), f32, 1), ((32, D), bf16, 8)],
        attn,
        Rows(x_own),
        Far(gains),
        name="norm_two",
    )
    n2, up_a, down_b = tie((n2, up_a, down_b))
    n_own, far_a, far_b = tie((over_head(n2), along_z(up_a, 1), along_z(down_b, 3)))
    blocks = [block, flipped, up_a, up_b, down_a, down_b, far_a, far_b]
    n_sib = to_sibling(n_own)

    hidden, gu_low, out_low, own, sib, out_own, out_sib, g2, far_a, far_b = on(
        ffn_kernel,
        [
            ((512, FFC), bf16, 1),
            ((512, 640), bf16, 1),
            ((512, D), bf16, 1),
            part,
            part,
            part,
            part,
            line,
            ((960, 256), bf16, 1),
            ((960, 256), bf16, 1),
        ],
        n_own,
        Far(cot_own),
        Far(cot_sib),
        Far(gains),
        Far(blocks[0]),
        n_sib,
        *[Far(a) for a in blocks[1:]],
        vmem=32,
        name="ffn",
    )
    def weight_grads(name, ranks):
        return on(
            functools.partial(ffn_weights_kernel, ranks=ranks),
            [((960, 256), bf16, 1)] * len(ranks),
            Far(hidden),
            Far(out_low),
            Far(n_own),
            Far(n_sib),
            Far(gu_low),
            vmem=18,
            name=name,
        )

    fore_a, back_b = weight_grads("ffn_weights_next", (4, 3))
    (out_own,) = on(
        layer_join_kernel, [part], out_own, to_sibling(out_sib), Far(hid), name="layer_join"
    )
    ffn_sum, fore_recv, back_recv, fore_a, back_b, out_own = tie(
        (
            over_head(with_sibling(own, sib)),
            along_z(far_a, 1),
            along_z(far_b, 3),
            fore_a,
            back_b,
            out_own,
        )
    )
    hig, low = on(
        norm_two_back_kernel,
        [((32, D), f32, 1), ((32, D), bf16, 8)],
        ffn_sum,
        Far(hid),
        Rows(cot_own),
        Far(gains),
        name="norm_two_back",
    )
    low, fore_recv, back_recv = tie((low, fore_recv, back_recv))
    fore_a = (fore_a.astype(f32) + fore_recv.astype(f32)).astype(bf16)
    back_b = (back_b.astype(f32) + back_recv.astype(f32)).astype(bf16)
    fore_b, back_a = weight_grads("ffn_weights_last", (5, 2))
    al_own, fore_a, back_b, fore_b, back_a, out_own = tie(
        (over_head(low), along_z(fore_a, 1), along_z(back_b, 3), fore_b, back_a, out_own)
    )
    al_sib = to_sibling(al_own)

    out_parts = over_head(out_own)
    q_low, dkv, near_sums, far_sums = on(
        attend_back_kernel,
        [
            ((2, 2, 128, 128), bf16, 1),
            ((8 * 256, 512), bf16, 1),
            ((2, 128, 384), f32),
            ((4, D), f32),
        ],
        w_parts,
        al_own,
        al_sib,
        Far(q),
        Far(kv),
        Far(rl),
        *[Far(e) for e in exps],
        scratch=[
            pltpu.VMEM((256, D), f32),
            pltpu.VMEM((256, D + 128), bf16),
            pltpu.VMEM((2, 2, 128, 128), bf16),
        ],
        vmem=28, name="attend_back",
    )
    dkv, out_parts, fore_b, back_a = tie(
        (dkv, out_parts, along_z(fore_b, 1), along_z(back_a, 3))
    )
    q_low = q_low.reshape(512, 128)

    (layer_out,) = on(layer_sum_kernel, [((32, D), bf16)], out_parts, name="layer_sum")
    (tab,) = on(table_kernel, [((BUCKETS, 128), f32)], near_sums, far_sums, name="table")
    early = on(
        early_weights_kernel,
        [((2, 256, 256), bf16, 1)] * 4,
        Far(n1),
        Far(q_low),
        Far(mixed),
        Far(al_own),
        Far(al_sib),
        vmem=14,
        name="early_weights",
    )
    near_a, near_b = weight_grads("ffn_weights_near", (0, 1))
    ffn_own, ffn_other = on(
        ffn_sum_kernel,
        [((960, 256), f32, 1), ((960, 256), bf16, 1)],
        *[Far(a) for a in (near_a, near_b, fore_a, fore_b, back_a, back_b)],
        vmem=12,
        name="ffn_sum",
    )
    kv_parts, tab, layer_out, ffn_own, ffn_other, *early = tie(
        (over_chips(dkv), tab, layer_out, ffn_own, ffn_other, *early)
    )
    kv_low, own, sib, g1 = on(
        qkv_back_kernel,
        [((512, 256), bf16, 1), part, part, line],
        kv_parts,
        Far(q_low),
        Far(w_attn),
        Far(n1),
        Far(gains),
        vmem=16,
        name="qkv_back",
    )

    rows = tab[:, 0:2].reshape(8, 2, 4)
    rows = jnp.where(first, rows, rows[:, ::-1])
    rows = jnp.pad(rows, ((0, 0), (0, 0), (0, 124))).reshape(8, 256)
    near_a, near_b, back_a, back_b, fore_a, fore_b, far_a, far_b = on(
        last_weights_kernel,
        [((272, 256), bf16, 1)] * 8,
        Far(n1),
        Far(kv_low),
        g1,
        g2,
        rows,
        vmem=14,
        name="last_weights",
    )

    def gathered(near, back, fore, far):
        return near, along_z(fore, 1), along_z(back, 3), along_z(far, 2)

    one_sum, ffn_recv, *early = tie(
        (over_head(with_sibling(own, sib)), other_y(ffn_other), *gathered(*early))
    )
    (low,) = on(
        norm_one_back_kernel,
        [((64, D), bf16, 8)],
        one_sum,
        layer_out,
        Rows(x_own),
        Far(gains),
        Far(hig),
        name="norm_one_back",
    )
    fore_recv, back_recv = along_z(far_a, 1), along_z(far_b, 3)
    low, fore_recv, back_recv, fore_b, back_a = tie(
        (low, fore_recv, back_recv, along_z(fore_b, 1), along_z(back_a, 3))
    )
    fore_a = (fore_a.astype(f32) + fore_recv.astype(f32)).astype(bf16)
    back_b = (back_b.astype(f32) + back_recv.astype(f32)).astype(bf16)
    fore_a, back_b = along_z(fore_a, 1), along_z(back_b, 3)
    both = over_head(low)
    input_grad, layer_out = on(
        unpack_kernel, [((256, D), f32, 1), ((256, D), bf16, 1)], Far(both), name="unpack"
    )
    last_own, last_other, misc = on(
        last_sum_kernel,
        [((528, 256), f32), ((528, 256), bf16), ((2, 16, 256), f32)],
        *[Far(a) for a in (*early, near_a, near_b, fore_a, fore_b, back_a, back_b)],
        name="last_sum",
    )
    mine, theirs = on(
        last_split_kernel,
        [((128, 512), f32), ((128, 512), bf16)],
        last_own,
        other_y(last_other),
        name="last_split",
    )
    out_grad, query_grad, key_grad, value_grad = on(
        last_order_kernel,
        [((256, 128), f32, 1)] + [((128, 256), f32, 1)] * 3,
        mine,
        to_sibling(theirs),
        name="last_order",
    )
    misc = misc[0] + other_y(misc[1])
    small = to_sibling(misc[:, 128:256])
    gain_sums = misc[0:2, 0:128] + small[0:2, :]
    for swap in HEAD_PAIRS:
        gain_sums = gain_sums + lax.ppermute(gain_sums, "head", swap)
    table_grad = in_order(misc[2, 0:4].reshape(2, 2), small[2, 0:4].reshape(2, 2), 1)

    mine, theirs = on(
        ffn_split_kernel,
        [((960, 128), f32), ((960, 128), bf16)],
        Far(ffn_own),
        ffn_recv,
        name="ffn_split",
    )
    gate_grad, up_grad, down_grad = on(
        ffn_order_kernel,
        [((128, 640), f32, 1), ((128, 640), f32, 1), ((640, 128), f32, 1)],
        mine,
        to_sibling(theirs),
        name="ffn_order",
    )
    return (
        layer_out.reshape(2, 128, D),
        input_grad.reshape(2, 128, D),
        gain_sums[0],
        query_grad,
        key_grad,
        value_grad,
        out_grad,
        table_grad,
        gain_sums[1],
        gate_grad,
        up_grad,
        down_grad,
    )


def solution(mesh):
    seq_head, head_seq = P("seq", "head"), P("head", "seq")
    in_specs = (
        P(None, "seq", None),
        P(None, "seq", None),
        P(),
        P("seq"),
        seq_head,
        seq_head,
        seq_head,
        head_seq,
        seq_head,
        P("seq"),
        seq_head,
        seq_head,
        head_seq,
    )
    out_specs = (
        P(None, "seq", None),
        P(None, "seq", None),
        P("seq"),
        seq_head,
        seq_head,
        seq_head,
        head_seq,
        seq_head,
        P("seq"),
        seq_head,
        seq_head,
        head_seq,
    )
    return jax.shard_map(body, mesh=mesh, in_specs=in_specs, out_specs=out_specs, check_vma=False)
```

```python
import functools

import jax
import jax.numpy as jnp
from jax import lax
from jax.experimental import pallas as pl
from jax.experimental.pallas import tpu as pltpu
from jax.sharding import PartitionSpec as P


D = 2048
HEAD = 64
BUCKETS = 32
FFC = 320
epsilon = 1e-06
limits = (8, 12, 16, 23, 32, 46, 64, 91)
masked_score = -1000000000.0

f32, bf16, i32 = jnp.float32, jnp.bfloat16, jnp.int32
MIB = 1024 * 1024

CHIP_GROUPS = [[s for s in range(16) if s % 2 == c] for c in range(2)]
RELATIVE = ((0, 0), (0, 1), (1, 0), (1, 1), (3, 0), (3, 1), (2, 0), (2, 1))
def seq_perm(f):
    return [
        (z * 4 + y * 2 + c, (lambda t: t[0] * 4 + t[1] * 2 + t[2])(f(z, y, c)))
        for z in range(4)
        for y in range(2)
        for c in range(2)
    ]


def head_perm(f):
    return [
        (x * 2 + y, (lambda t: t[0] * 2 + t[1])(f(x, y))) for x in range(4) for y in range(2)
    ]


CORE = seq_perm(lambda z, y, c: (z, y, 1 - c))
OTHER_Y = seq_perm(lambda z, y, c: (z, 1 - y, c))
ALONG_Z = {d: seq_perm(lambda z, y, c, d=d: ((z + d) % 4, y, c)) for d in (1, 2, 3)}
OTHER_HEAD_Y = head_perm(lambda x, y: (x, 1 - y))
ALONG_X = {d: head_perm(lambda x, y, d=d: ((x + d) % 4, y)) for d in (1, 2, 3)}


def nn(a, b):
    return jnp.dot(a, b, preferred_element_type=f32)


def nt(a, b):
    return lax.dot_general(a, b, (((1,), (1,)), ((), ())), preferred_element_type=f32)


def tn(a, b):
    return lax.dot_general(a, b, (((0,), (0,)), ((), ())), preferred_element_type=f32)


class Loaded:
    def __init__(self, copy, ref, queue):
        self.copy, self.ref, self.queue, self.here = copy, ref, queue, False

    def ready(self):
        if not self.here:
            while self in self.queue:
                self.queue.pop(0).copy.start()
            self.copy.wait()
            self.here = True
            if self.queue:
                self.queue.pop(0).copy.start()
        return self.ref

    def __getitem__(self, at):
        return self.ready()[at]

    @property
    def at(self):
        return self.ready().at


class Stored:
    def __init__(self, ref, there, sems, times):
        self.ref, self.there, self.sems, self.times = ref, there, sems, times
        self.copies, self.whole = [], True

    def start(self, source, target):
        copy = pltpu.make_async_copy(source, target, self.sems.at[len(self.copies)])
        copy.start()
        self.copies.append(copy)

    def send(self):
        rows = self.ref.shape[0]
        for t in range(self.times):
            there = self.there if self.times == 1 else self.there.at[pl.ds(t * rows, rows)]
            self.start(self.ref, there)

    def send_part(self, at):
        self.start(self.ref.at[at], self.there.at[at])

    def __getitem__(self, at):
        return self.ref[at]

    def __setitem__(self, at, value):
        self.ref[at] = value

    @property
    def at(self):
        return self.ref.at


class Place:
    def __init__(self, scalars):
        self.c, self.sc, self.h = scalars[0], scalars[1], scalars[2]
        self.lengths = {0: scalars[3], 1: scalars[4]}
        self.idx = [scalars[5 + k] for k in range(8)]


def place_scalars(lengths):
    s, h = lax.axis_index("seq"), lax.axis_index("head")
    c, sc = s % 2, s // 2
    z, y = sc // 2, sc % 2
    idx = [((z + 4 - dz) % 4) * 2 + (y if dy == 0 else 1 - y) for dz, dy in RELATIVE]
    return jnp.stack([c, sc, h, lengths[0], lengths[1], *idx]).astype(i32)


class Far:
    def __init__(self, value, at=None):
        self.value, self.at = value, at

    def shape(self):
        return jax.eval_shape(lambda v: v if self.at is None else v[self.at], self.value).shape


class Rows(Far):
    def shape(self):
        return (32, self.value.shape[1])


def call(kernel, outs, lengths, *args, smem=(), scratch=(), vmem=8, ahead=16, name=None):
    n, m, fixed = len(args), len(outs), 1 + len(smem)
    far_in = [i for i, a in enumerate(args) if isinstance(a, Far)]
    far_out = [k for k, o in enumerate(outs) if len(o) == 3]

    def whole(*refs):
        lens, scalars, refs = refs[0], refs[1:fixed], refs[fixed:]
        inputs, outputs, refs = list(refs[:n]), list(refs[n : n + m]), list(refs[n + m :])
        queue = []
        for i in far_in:
            buf, sem = refs.pop(0), refs.pop(0)
            there = inputs[i]
            if isinstance(args[i], Rows):
                first = pl.multiple_of(lens[2] * 32, 32)
                there = there.at[pl.ds(first, 32)]
            elif args[i].at is not None:
                there = there.at[args[i].at]
            inputs[i] = Loaded(pltpu.make_async_copy(there, buf, sem), buf, queue)
            queue.append(inputs[i])
        for _ in range(min(ahead, len(queue))):
            queue.pop(0).copy.start()
        for k in far_out:
            buf, sems = refs.pop(0), refs.pop(0)
            outputs[k] = Stored(buf, outputs[k], sems, outs[k][2])
        kernel(Place(lens), *scalars, *inputs, *outputs, *refs)
        for i in far_in:
            inputs[i].ready()
        for k in far_out:
            if not outputs[k].copies:
                outputs[k].send()
        for k in far_out:
            for copy in outputs[k].copies:
                copy.wait()

    buffers = []
    for i in far_in:
        buffers += [pltpu.VMEM(args[i].shape(), args[i].value.dtype), pltpu.SemaphoreType.DMA]
    for k in far_out:
        shape, dtype, _ = outs[k]
        buffers += [pltpu.VMEM(shape, dtype), pltpu.SemaphoreType.DMA((24,))]
    placed = [
        pltpu.with_memory_space_constraint(a.value, pltpu.HBM)
        if isinstance(a, Far)
        else pltpu.with_memory_space_constraint(a, pltpu.VMEM)
        for a in args
    ]
    shapes = [
        pltpu.HBM((o[0][0] * o[2], *o[0][1:]), o[1])
        if len(o) == 3
        else pltpu.VMEM(o[0], o[1])
        for o in outs
    ]
    return pl.pallas_call(
        whole,
        out_shape=tuple(shapes),
        in_specs=[pl.BlockSpec(memory_space=pltpu.SMEM)] * fixed
        + [pl.BlockSpec(memory_space=pl.ANY if i in far_in else pltpu.VMEM) for i in range(n)],
        out_specs=tuple(
            pl.BlockSpec(memory_space=pl.ANY if k in far_out else pltpu.VMEM) for k in range(m)
        ),
        scratch_shapes=buffers + list(scratch),
        compiler_params=pltpu.CompilerParams(vmem_limit_bytes=vmem * MIB),
        cost_estimate=pl.CostEstimate(flops=1000, bytes_accessed=1000, transcendentals=0),
        name=name,
    )(lengths, *smem, *placed)


def lane_at(chip, core):
    return pl.multiple_of(chip * 256 + core * 128, 128)


def chunk_p(ref, rows, chip, c):
    return jnp.concatenate(
        [ref[rows, pl.ds(lane_at(chip, c), 128)], ref[rows, pl.ds(lane_at(chip, 1 - c), 128)]],
        axis=1,
    )


def rows_of(half):
    return slice(half * 256, (half + 1) * 256)


def pack_kernel(me, wq, wk, wv, wo, ga, gf, bias, mine, theirs, misc):
    misc[...] = jnp.zeros_like(misc)
    misc[0:1, 0:128] = ga[...].astype(f32)
    misc[0:1, 128:256] = gf[...].astype(f32)
    misc[1:3, 0:4] = bias[...].astype(f32)
    low = jnp.concatenate([wq[:, 0:128], wk[:, 0:128], wv[:, 0:128], wo[0:128, :]], axis=1)
    high = jnp.concatenate(
        [wq[:, 128:256], wk[:, 128:256], wv[:, 128:256], wo[128:256, :]], axis=1
    )
    theirs[0:128, :] = jnp.where(me.c == 0, high, low)
    mine[0:128, :] = jnp.where(me.c == 0, low, high)
    for res in (mine, theirs):
        res[128:144, :] = misc[...].astype(bf16)


def qkv_kernel(me, x_own, x_sib, w, n1, q, kv, gains):
    c = me.c
    rinvs = []
    for x in (x_own, x_sib):
        total = jnp.zeros((256, 1), f32)
        for k in range(8):
            v = x[:, k * 256 : (k + 1) * 256].astype(f32)
            total = total + jnp.sum(v * v, axis=1, keepdims=True)
        rinvs.append(lax.rsqrt(total * (1.0 / D) + epsilon))
    for k in range(8):
        for core, p in ((0, c), (1, 1 - c)):
            rows = w[k, 256:272, 0:256].astype(f32)
            row = jnp.where(p == 0, rows[0:1], rows[8:9])
            gains[0:1, k * 256 + core * 128 : k * 256 + core * 128 + 128] = row[:, 0:128]
            gains[1:2, k * 256 + core * 128 : k * 256 + core * 128 + 128] = row[:, 128:256]
    gains.send()
    for half, x, rinv in ((0, x_own, rinvs[0]), (1, x_sib, rinvs[1])):
        rows = rows_of(half)
        acc = jnp.zeros((256, 384), f32)
        for k in range(8):
            lanes = slice(k * 256, (k + 1) * 256)
            v = x[:, lanes].astype(f32)
            normed = (v * rinv * gains[0:1, lanes]).astype(bf16)
            n1[rows, lanes] = normed
            wk = jnp.concatenate(
                [w[k, rows_p(c), 0:384], w[k, rows_p(1 - c), 0:384]], axis=0
            )
            acc = acc + nn(normed, wk)
        q[rows, :] = acc[:, 0:128].astype(bf16)
        kv[rows, :] = acc[:, 128:384].astype(bf16)
        for chip in range(8):
            kv.start(kv.ref.at[rows], kv.there.at[pl.ds(chip * 512 + half * 256, 256)])
        n1.send_part(rows)


def rows_p(p):
    return pl.ds(pl.multiple_of(p * 128, 128), 128)


def out_weights(me, w, k):
    return jnp.concatenate([w[k, rows_p(p)] for p in (me.c, 1 - me.c)], axis=1)


def bucket_ids(offset):
    distance = jnp.abs(offset)
    coarse = 7 + sum(((distance >= threshold).astype(i32) for threshold in limits))
    within = jnp.where(distance < 8, distance, coarse)
    return within + jnp.where(offset > 0, 16, 0).astype(i32)


def band_buckets():
    return bucket_ids(
        lax.broadcasted_iota(i32, (128, 384), 1)
        - 128
        - lax.broadcasted_iota(i32, (128, 384), 0)
    )


def key_places(c):
    lane = lax.broadcasted_iota(i32, (1, D), 1)
    stored = lane // 128
    tile = (stored // 2) * 2 + jnp.where(stored % 2 == 1, 1 - c, c)
    return tile, tile * 128 + lane % 128


def band_tiles(me, half):
    c = me.c
    tile = me.sc * 2 + (c if half == 0 else 1 - c)
    lanes = []
    for step in (-1, 0, 1):
        near = tile + step
        stored = (near // 2) * 2 + jnp.where(near % 2 == 1, 1 - c, c)
        inside = jnp.logical_and(near >= 0, near < 16)
        lanes.append(pl.multiple_of(jnp.where(inside, stored, 16) * 128, 128))
    return tile, lanes


def band_kernel(me, table, band):
    ids = band_buckets()
    for j in range(2):
        value = jnp.zeros((128, 384), f32)
        for b in range(BUCKETS):
            value = jnp.where(ids == b, table[b, j], value)
        band[j] = value


def attend_kernel(me, table, q, kv, band, w, e0, e1, e2, e3, rl, mixed, own, sib, s_ref):
    exps = (e0, e1, e2, e3)
    c = me.c
    tile_of, place_of = key_places(c)
    head_lane = lax.broadcasted_iota(i32, (256, 128), 1) // HEAD
    for b in range(2):
        length = me.lengths[b]
        keys = kv[:, b, :, 0:128].reshape(D, 128)
        values = jnp.concatenate(
            [kv[:, b, :, 128:256].reshape(D, 128), jnp.ones((D, 128), bf16)], axis=1
        )
        queries = q[:, b].reshape(256, 128)
        together = jnp.zeros((256, 128), f32)
        for j in range(2):
            mine = jnp.where(head_lane == j, queries, jnp.zeros_like(queries))
            s_ref[:, 0:D] = nt(mine, keys)
            for half in range(2):
                tile, lanes = band_tiles(me, half)
                rows = slice(half * 128, (half + 1) * 128)
                for t in range(3):
                    at = pl.ds(lanes[t], 128)
                    s_ref[rows, at] = s_ref[rows, at] + band[j, :, t * 128 : (t + 1) * 128]
                added = jnp.where(place_of >= length, masked_score, 0.0) + jnp.where(
                    tile_of < tile - 1,
                    table[15, j],
                    jnp.where(tile_of > tile + 1, table[31, j], 0.0),
                )

                def some_rows(i, carry, half=half, added=added, b=b, j=j):
                    at = pl.ds(pl.multiple_of(half * 128 + i * 16, 16), 16)
                    s = s_ref[at, 0:D] + added
                    exps[b * 2 + j][at, :] = jnp.exp(
                        s - jnp.max(s, axis=1, keepdims=True)
                    ).astype(bf16)
                    return carry

                lax.fori_loop(0, 8, some_rows, 0, unroll=8)
            exps[b * 2 + j].send()
            wide = nn(exps[b * 2 + j][...], values)
            inverse = 1.0 / wide[:, 128:129]
            rl[b * 2 + j] = inverse
            together = jnp.where(head_lane == j, wide[:, 0:128] * inverse, together)
        mixed[:, b] = together.astype(bf16).reshape(2, 128, 128)
    rl.send()
    mixed.send()
    for half, res in ((1, sib), (0, own)):
        for k in range(8):
            res[:, k * 256 : (k + 1) * 256] = nn(
                mixed[half].reshape(256, 128), out_weights(me, w, k)
            ).astype(bf16)


def attend_back_kernel(
    me, w, al_own, al_sib, q, kv, rl, e0, e1, e2, e3, dq, dkv, band, far_out, d_ref, ds_ref, mg
):
    exps = (e0, e1, e2, e3)
    c = me.c
    for half, al in ((0, al_own), (1, al_sib)):
        acc = jnp.zeros((256, 128), f32)
        for k in range(8):
            acc = acc + nt(al[:, k * 256 : (k + 1) * 256], out_weights(me, w, k))
        mg[half] = acc.astype(bf16).reshape(2, 128, 128)
    tile_of, _ = key_places(c)
    head_lane = lax.broadcasted_iota(i32, (256, 128), 1) // HEAD
    ds_ref[:, D : D + 128] = jnp.zeros((256, 128), bf16)
    band[...] = jnp.zeros_like(band)
    far = [[jnp.zeros((1, D), f32) for _ in range(2)] for _ in range(2)]
    row16 = lax.broadcasted_iota(i32, (16, 256), 0)
    lane256 = lax.broadcasted_iota(i32, (16, 256), 1)
    marks = (row16 == lane256 // 128).astype(f32).astype(bf16)
    for b in range(2):
        keys = kv[:, b, :, 0:128].reshape(D, 128)
        values = kv[:, b, :, 128:256].reshape(D, 128)
        queries = q[:, b].reshape(256, 128)
        turned = queries.astype(f32).T.astype(bf16)
        grads = mg[:, b].reshape(256, 128).astype(f32)
        together = jnp.zeros((256, 128), f32)
        for j in range(2):
            inverse = rl[b * 2 + j]
            e = exps[b * 2 + j].ready()
            scaled = jnp.where(head_lane == j, grads * inverse, 0.0)
            mine = scaled.astype(bf16)
            d_ref[...] = nt(mine, values)

            def some_rows(i, carry, b=b, j=j, e=e):
                at = pl.ds(pl.multiple_of(i * 16, 16), 16)
                p = e[at, :].astype(f32)
                d = d_ref[at, :]
                inner = jnp.sum(p * d, axis=1, keepdims=True) * rl[b * 2 + j, at, :]
                ds_ref[at, 0:D] = (p * (d - inner)).astype(bf16)
                return carry

            lax.fori_loop(0, 16, some_rows, 0, unroll=16)
            score_grad = ds_ref[:, 0:D]
            together = jnp.where(head_lane == j, nn(score_grad, keys), together)
            left = jnp.concatenate([turned[j * HEAD : (j + 1) * HEAD, :], marks], axis=0)
            key_t = nn(left, score_grad)
            value_t = nn(scaled.T[j * HEAD : (j + 1) * HEAD, :].astype(bf16), e[...])
            for chip in range(8):
                lanes = slice(chip * 256, (chip + 1) * 256)
                at = chip * 256 + j * HEAD
                dkv[at : at + HEAD, b * 256 : (b + 1) * 256] = key_t[0:HEAD, lanes].astype(bf16)
                dkv[at + 128 : at + 128 + HEAD, b * 256 : (b + 1) * 256] = value_t[
                    :, lanes
                ].astype(bf16)
            for half in range(2):
                tile, lanes = band_tiles(me, half)
                rows = slice(half * 128, (half + 1) * 128)
                for t in range(3):
                    cols = slice(t * 128, (t + 1) * 128)
                    band[j, :, cols] = band[j, :, cols] + ds_ref[
                        rows, pl.ds(lanes[t], 128)
                    ].astype(f32)
                line = key_t[HEAD + half : HEAD + half + 1, :]
                far[j][0] = far[j][0] + jnp.where(tile_of < tile - 1, line, 0.0)
                far[j][1] = far[j][1] + jnp.where(tile_of > tile + 1, line, 0.0)
        dq[:, b] = together.astype(bf16).reshape(2, 128, 128)
        dkv.send_part((slice(None), pl.ds(b * 256, 256)))
    for j in range(2):
        for side in range(2):
            far_out[2 * j + side : 2 * j + side + 1, :] = far[j][side]


def table_kernel(me, band, far, tab):
    ids = band_buckets()
    lane = lax.broadcasted_iota(i32, (BUCKETS, 128), 1)
    bucket = lax.broadcasted_iota(i32, (BUCKETS, 1), 0)
    result = jnp.zeros((BUCKETS, 128), f32)
    for j in range(2):
        near = band[j]
        lines = [
            jnp.sum(jnp.where(ids == b, near, 0.0), axis=0, keepdims=True) for b in range(BUCKETS)
        ]
        column = jnp.sum(jnp.concatenate(lines, axis=0), axis=1, keepdims=True)
        sides = [jnp.sum(far[2 * j + k : 2 * j + k + 1, :], axis=1, keepdims=True) for k in (0, 1)]
        column = column + jnp.where(bucket == 15, sides[0], 0.0)
        column = column + jnp.where(bucket == 31, sides[1], 0.0)
        result = jnp.where(lane == j, column, result)
    tab[...] = result


def summed(parts, first, rows):
    total = parts[first : first + rows, :].astype(f32)
    for k in range(1, 8):
        total = total + parts[k * 32 + first : k * 32 + first + rows, :].astype(f32)
    return total


def spread_rows(res, first, rows, value):
    at = pl.ds(first, rows)
    res[at, :] = value.astype(bf16)
    size = res.ref.shape[0]
    for t in range(res.times):
        res.start(res.ref.at[at], res.there.at[pl.ds(t * size + first, rows)])


def norm_two_kernel(me, parts, x, gains, hid, normed):
    for first in (0, 16):
        rows = slice(first, first + 16)
        hidden_in = summed(parts, first, 16) + x[rows, :].astype(f32)
        rinv = lax.rsqrt(jnp.mean(hidden_in * hidden_in, axis=1, keepdims=True) + epsilon)
        spread_rows(normed, first, 16, hidden_in * rinv * gains[1:2, :])
        hid[rows, :] = hidden_in


def norm_back(value, grad, gain):
    rinv = lax.rsqrt(jnp.mean(value * value, axis=1, keepdims=True) + epsilon)
    u = grad * gain
    return rinv * u - (rinv * rinv * rinv) * value * jnp.mean(u * value, axis=1, keepdims=True)


def live_rows(me, half, b, first, count):
    c = me.c
    core = c if half == 0 else 1 - c
    place = (me.sc * 2 + core) * 128 + first + lax.broadcasted_iota(i32, (count, 1), 0)
    return place < me.lengths[b]


def norm_two_back_kernel(me, parts, hid, cot, gains, hig, low):
    b = me.h // 4
    for first in (0, 16):
        rows = slice(first, first + 16)
        place = (
            (me.sc * 2 + me.c) * 128
            + (me.h - b * 4) * 32
            + first
            + lax.broadcasted_iota(i32, (16, 1), 0)
        )
        total = summed(parts, first, 16)
        grad = norm_back(hid[rows, :], total, gains[1:2, :])
        grad = grad + jnp.where(place < jnp.where(b == 0, me.lengths[0], me.lengths[1]), cot[rows, :].astype(f32), 0.0)
        spread_rows(low, first, 16, grad)
        hig[rows, :] = grad


def norm_one_back_kernel(me, parts, x, gains, hig, res):
    for first in (0, 16):
        rows = slice(first, first + 16)
        total = summed(parts, first, 16)
        grad = norm_back(x[rows, :].astype(f32), total, gains[0:1, :]) + hig[rows, :]
        spread_rows(res, first, 16, grad)


def gelu_pair(g):
    k0, k1 = 0.7978845608028654, 0.044715
    g2 = g * g
    t = jnp.tanh(k0 * g * (1.0 + k1 * g2))
    value = 0.5 * g * (1.0 + t)
    slope = 0.5 * (1.0 + t) + 0.5 * g * (1.0 - t * t) * k0 * (1.0 + 3.0 * k1 * g2)
    return value, slope


def gate_up(w):
    wide = jnp.concatenate([w[320:576, :], w[576:832, :]], axis=1)
    rest = jnp.concatenate([w[832:960, 0:128], w[832:960, 128:256]], axis=0)
    return wide, rest


def live_cotangent(me, out_low, cot_own, cot_sib):
    for half, cot in ((0, cot_own), (1, cot_sib)):
        live = jnp.concatenate([live_rows(me, half, b, 0, 128) for b in range(2)], axis=0)
        out_low[rows_of(half), :] = jnp.where(live, cot[...], jnp.zeros((), bf16))


def weight_grad(me, k, res, hidden, grads, n_own, n_sib, gu_low):
    chip, c = me.idx[k], me.c
    res[0:320, :] = tn(hidden[...], grads).astype(bf16)
    v = jnp.concatenate(
        [chunk_p(n_own, slice(None), chip, c), chunk_p(n_sib, slice(None), chip, c)], axis=0
    )
    part = tn(v, gu_low[...]).astype(bf16)
    res[320:576, :] = part[:, 0:256]
    res[576:832, :] = part[:, 256:512]
    res[832:960, 0:128] = part[0:128, 512:640]
    res[832:960, 128:256] = part[128:256, 512:640]
    res.send()


def ffn_early_kernel(me, cot_own, cot_sib, *refs):
    blocks, (back, grads, out_low) = refs[:6], refs[6:]
    live_cotangent(me, out_low, cot_own, cot_sib)
    for k in (6, 7):
        grads[:, (k - 6) * 256 : (k - 5) * 256] = chunk_p(out_low, slice(None), me.idx[k], me.c)
    grads.send()
    total = jnp.zeros((512, FFC), f32)
    for k in range(6):
        total = total + nt(chunk_p(out_low, slice(None), me.idx[k], me.c), blocks[k][...])
    back[...] = total


def ffn_kernel(me, n_own, n_sib, *refs):
    blocks, (back, grads, gains), results = refs[:8], refs[8:11], refs[11:]
    hidden, gu_low, own, sib, out_own, out_sib, gain_sum, far_a, far_b = results
    c = me.c
    all_rows = slice(None)

    def tokens(chip):
        return jnp.concatenate(
            [chunk_p(n_own, all_rows, chip, c), chunk_p(n_sib, all_rows, chip, c)], axis=0
        )

    gu = jnp.zeros((512, 512), f32)
    rest = jnp.zeros((512, 128), f32)
    for k in range(8):
        if k == 2:
            for a in (*blocks[2:], back, grads, gains):
                a.ready()
        v = tokens(me.idx[k])
        wide, last = gate_up(blocks[k])
        gu = gu + nn(v, wide)
        rest = rest + nn(v, last)
    total = back[...]
    for k in (6, 7):
        total = total + nt(grads[:, (k - 6) * 256 : (k - 5) * 256], blocks[k][0:320, :])
    for gate, up, dh, at, size in (
        (gu[:, 0:256], gu[:, 256:512], total[:, 0:256], 0, 256),
        (rest[:, 0:64], rest[:, 64:128], total[:, 256:FFC], 256, 64),
    ):
        value, slope = gelu_pair(gate)
        hidden[:, at : at + size] = (value * up).astype(bf16)
        at = 2 * at
        gu_low[:, at : at + size] = (dh * up * slope).astype(bf16)
        gu_low[:, at + size : at + 2 * size] = (dh * value).astype(bf16)
    hidden.send()
    gu_low.send()
    for k, res in ((6, far_a), (7, far_b)):
        chunk = grads[:, (k - 6) * 256 : (k - 5) * 256]
        weight_grad(me, k, res, hidden, chunk, n_own, n_sib, gu_low)
    for k in range(8):
        chip = me.idx[k]
        wide, last = gate_up(blocks[k])
        part = nt(gu_low[:, 0:512], wide) + nt(gu_low[:, 512:640], last)
        made = nn(hidden[...], blocks[k][0:320, :])
        line = jnp.sum(part * tokens(chip).astype(f32), axis=0, keepdims=True)
        for p, core in ((0, c), (1, 1 - c)):
            lanes = pl.ds(lane_at(chip, core), 128)
            cols = slice(p * 128, (p + 1) * 128)
            gain_sum[0:1, lanes] = line[:, cols] / gains[1:2, lanes]
            for half, res, out in ((0, own, out_own), (1, sib, out_sib)):
                res[:, lanes] = part[rows_of(half), cols].astype(bf16)
                out[:, lanes] = made[rows_of(half), cols].astype(bf16)


def ffn_weights_kernel(me, cot_own, cot_sib, hidden, n_own, n_sib, gu_low, *results, ranks):
    *results, out_low = results
    live_cotangent(me, out_low, cot_own, cot_sib)
    for k, res in zip(ranks, results):
        grads = chunk_p(out_low, slice(None), me.idx[k], me.c)
        weight_grad(me, k, res, hidden, grads, n_own, n_sib, gu_low)


def layer_join_kernel(me, own, recv, hid, res):
    res[...] = (own[...].astype(f32) + recv[...].astype(f32)).astype(bf16)
    at = pl.ds(pl.multiple_of(me.h * 32, 32), 32)
    res[at, :] = (own[at, :].astype(f32) + recv[at, :].astype(f32) + hid[...]).astype(bf16)


def qkv_back_kernel(me, parts, q_low, w, n1, gains, kv_low, own, sib, gain_sum):
    c = me.c
    total = parts[0:256, :].astype(f32)
    for k in range(1, 8):
        total = total + parts[k * 256 : (k + 1) * 256, :].astype(f32)
    for b in range(2):
        for half in range(2):
            lanes = slice(b * 256 + half * 128, b * 256 + (half + 1) * 128)
            kv_low[half * 256 + b * 128 : half * 256 + (b + 1) * 128, :] = total[:, lanes].T.astype(
                bf16
            )
    for k in range(8):
        wk = jnp.concatenate(
            [
                w[k, rows_p(p), 0:384]
                for p in (c, 1 - c)
            ],
            axis=0,
        )
        lanes = slice(k * 256, (k + 1) * 256)
        line = jnp.zeros((1, 256), f32)
        for half, res in ((0, own), (1, sib)):
            rows = rows_of(half)
            part = nt(q_low[rows, :], wk[:, 0:128]) + nt(kv_low[rows, :], wk[:, 128:384])
            line = line + jnp.sum(part * n1[rows, lanes].astype(f32), axis=0, keepdims=True)
            res[:, lanes] = part.astype(bf16)
        gain_sum[0:1, lanes] = line / gains[0:1, lanes]


def early_weights_kernel(me, n1, q_low, mixed, al_own, al_sib, *results):
    c = me.c
    for k in range(8):
        chip = me.idx[k]
        res = results[k // 2].at[k % 2]
        al = jnp.concatenate(
            [chunk_p(al_own, slice(None), chip, c), chunk_p(al_sib, slice(None), chip, c)], axis=0
        )
        res[0:128, :] = tn(mixed[...], al).astype(bf16)
        part = tn(chunk_p(n1, slice(None), chip, c), q_low[...]).astype(bf16)
        res[128:256, 0:128] = part[0:128]
        res[128:256, 128:256] = part[128:256]
        if k % 2:
            results[k // 2].send()


def last_weights_kernel(me, n1, kv_low, g1, g2, tab, *results):
    c = me.c
    for k in (6, 7, 5, 2, 4, 3, 0, 1):
        chip = me.idx[k]
        res = results[k]
        part = tn(chunk_p(n1, slice(None), chip, c), kv_low[...]).astype(bf16)
        for p in range(2):
            rows, lanes = slice(p * 128, (p + 1) * 128), slice(p * 128, (p + 1) * 128)
            res[0:128, lanes] = part[rows, 0:128]
            res[128:256, lanes] = part[rows, 128:256]
        one = slice(0, 1)
        misc = jnp.concatenate(
            [
                chunk_p(g1, one, chip, c),
                chunk_p(g2, one, chip, c),
                tab[pl.ds(chip, 1), :],
                jnp.zeros((13, 256), f32),
            ],
            axis=0,
        )
        res[256:272, :] = misc.astype(bf16)
        res.send()


def unpack_kernel(me, rows, input_grad):
    for k in range(4):
        at = slice(k * 64, (k + 1) * 64)
        input_grad[at, :] = rows[at, :].astype(f32)
        input_grad.send_part(at)


def layer_place_kernel(me, *refs):
    parts, res = refs[:4], refs[4]
    x, y = me.h // 2, me.h % 2
    for part, step in zip(parts, (0, 1, 3, 2)):
        from_x = (x + 4 - step) % 4
        for k, from_y in ((0, y), (1, 1 - y)):
            at = pl.ds(pl.multiple_of((from_x * 2 + from_y) * 32, 32), 32)
            res[at, :] = part[k * 32 : (k + 1) * 32, :]


def layer_sum_kernel(me, parts, res):
    res[...] = summed(parts, 0, 32).astype(bf16)


def ffn_sum_kernel(me, *refs):
    parts, results = refs[:6], refs[6:]
    for y, res in enumerate(results):
        value = parts[y][...].astype(f32)
        for a in parts[2 + y :: 2]:
            value = value + a[...].astype(f32)
        res[...] = value.astype(res.ref.dtype)
        res.send()


def last_sum_kernel(me, *refs):
    early, late, (own, other) = refs[:4], refs[4:10], refs[10:]
    for y, res in ((1, other), (0, own)):
        value = early[0][y].astype(f32)
        for a in early[1:]:
            value = value + a[y].astype(f32)
        res[0:256, :] = value.astype(f32 if y == 0 else bf16)
        value = late[y][...].astype(f32)
        for a in late[2 + y :: 2]:
            value = value + a[...].astype(f32)
        res[256:528, :] = value.astype(f32 if y == 0 else bf16)


def last_split_kernel(me, own, recv, mine, theirs):
    total = own[...] + recv[...].astype(f32)
    for p, res in ((0, mine), (1, theirs)):
        cols = slice(p * 128, (p + 1) * 128)
        parts = [total[k * 128 : (k + 1) * 128, cols] for k in range(4)]
        value = jnp.concatenate(parts, axis=1)
        res[0:128, :] = value.astype(bf16 if p else f32)
        value = jnp.concatenate([total[512:528, cols]] * 4, axis=1)
        res[128:144, :] = value.astype(bf16 if p else f32)


def gain_kernel(me, mine, recv, res):
    a, b = mine[128:144, 0:128], recv[128:144, 0:128].astype(f32)
    res[...] = jnp.concatenate([a[0:2] + b[0:2], a[2:3], b[2:3], a[4:8]], axis=0)


def ffn_split_kernel(me, own, recv, mine, theirs):
    for p, res in ((1, theirs), (0, mine)):
        lanes = slice(p * 128, (p + 1) * 128)
        rows = [(0, 320, lanes)]
        for first in (320, 576):
            rows += [(first + p * 128, 128, slice(0, 128)), (first + p * 128, 128, slice(128, 256))]
        rows.append((832, 128, lanes))
        at = 0
        for first, size, cols in rows:
            value = own[first : first + size, cols] + recv[first : first + size, cols].astype(f32)
            res[at : at + size, :] = value.astype(bf16 if p else f32)
            at += size


def ffn_order_kernel(me, mine, recv, gate_grad, up_grad, down_grad):
    first = me.c == 0
    a, b = mine[0:320, :], recv[0:320, :].astype(f32)
    down_grad[0:320, :] = jnp.where(first, a, b)
    down_grad[320:640, :] = jnp.where(first, b, a)
    down_grad.send()
    for at, lane, res in ((320, 0, gate_grad), (576, 64, up_grad)):
        sides = []
        for ref in (mine, recv):
            rest = ref[832:960, lane : lane + 64]
            sides.append(
                jnp.concatenate([ref[at : at + 128, :], ref[at + 128 : at + 256, :], rest], axis=1)
            )
        a, b = sides[0], sides[1].astype(f32)
        res[...] = jnp.concatenate([jnp.where(first, a, b), jnp.where(first, b, a)], axis=1)
        res.send()


def last_order_kernel(me, mine, recv, out_grad, query_grad, key_grad, value_grad):
    a, b = mine[0:128, :], recv[0:128, :].astype(f32)
    low, high = jnp.where(me.c == 0, a, b), jnp.where(me.c == 0, b, a)
    out_grad[0:128, :] = low[:, 0:128]
    out_grad[128:256, :] = high[:, 0:128]
    for k, res in ((1, query_grad), (2, key_grad), (3, value_grad)):
        cols = slice(k * 128, (k + 1) * 128)
        res[:, 0:128] = low[:, cols]
        res[:, 128:256] = high[:, cols]


def to_sibling(a):
    return lax.ppermute(a, "seq", CORE)


def over_head(a):
    return lax.all_to_all(a, "head", 0, 0, tiled=True)


def over_chips(a):
    return lax.all_to_all(a, "seq", 0, 0, axis_index_groups=CHIP_GROUPS, tiled=True)


def body(
    inputs,
    cotangent,
    lengths,
    attn_gain,
    w_query,
    w_key,
    w_value,
    w_out,
    bias_table,
    ffn_gain,
    w_gate,
    w_up,
    w_down,
):
    s = lax.axis_index("seq")
    first = s % 2 == 0
    scalars = place_scalars(lengths)

    def halves(a, axis):
        low, high = jnp.split(a, 2, axis=axis)
        return jnp.where(first, low, high), jnp.where(first, high, low)

    def in_order(own, sib, axis):
        return jnp.where(
            first,
            jnp.concatenate([own, sib], axis=axis),
            jnp.concatenate([sib, own], axis=axis),
        )

    def on(kernel, outs, *args, **more):
        return call(kernel, outs, scalars, *args, **more)

    mine, theirs = on(
        pack_kernel,
        [((144, 512), bf16)] * 2,
        Far(w_query),
        Far(w_key),
        Far(w_value),
        Far(w_out),
        Far(attn_gain.reshape(1, 128)),
        Far(ffn_gain.reshape(1, 128)),
        Far(bias_table),
        scratch=[pltpu.VMEM((16, 512), f32)],
        name="pack",
    )
    recv = to_sibling(theirs)
    block = jnp.concatenate([mine[0:128], recv[0:128], mine[128:136], recv[128:136]], axis=0)
    w_attn = over_chips(jnp.broadcast_to(block[None], (8, 272, 512)).reshape(8 * 272, 512))
    w_attn = w_attn.reshape(8, 272, 512)

    x_own = inputs.reshape(256, D)
    x_sib = to_sibling(x_own)
    cot_own = cotangent.reshape(256, D)
    cot_sib = to_sibling(cot_own)

    down_mine, down_theirs = halves(w_down, 0)
    gate_mine, gate_theirs = halves(w_gate, 1)
    up_mine, up_theirs = halves(w_up, 1)

    def joined(gate, up):
        return jnp.concatenate(
            [gate[:, 0:256], up[:, 0:256], gate[:, 256:FFC], up[:, 256:FFC]], axis=1
        )

    gu_mine = joined(gate_mine, up_mine)
    down_recv = to_sibling(down_theirs)
    gu_recv = to_sibling(joined(gate_theirs, up_theirs))
    block = jnp.concatenate(
        [
            jnp.concatenate([down_mine, down_recv], axis=1),
            jnp.concatenate([gu_mine[:, 0:256], gu_recv[:, 0:256]], axis=0),
            jnp.concatenate([gu_mine[:, 256:512], gu_recv[:, 256:512]], axis=0),
            jnp.concatenate([gu_mine[:, 512:640], gu_recv[:, 512:640]], axis=1),
        ],
        axis=0,
    )

    def with_sibling(own, sib):
        return (own.astype(f32) + to_sibling(sib).astype(f32)).astype(bf16)

    def along_z(a, steps):
        return lax.ppermute(a, "seq", ALONG_Z[steps % 4])

    def other_y(a):
        return lax.ppermute(a, "seq", OTHER_Y)

    tie = lax.optimization_barrier
    half, part, line = ((256, D), bf16), ((256, D), bf16), ((1, D), f32)

    n1, q, kv, gains = on(
        qkv_kernel,
        [((512, D), bf16, 1), ((512, 128), bf16, 1), ((512, 256), bf16, 8), ((2, D), f32, 1)],
        x_own,
        Far(x_sib),
        Far(w_attn),
        vmem=16,
        name="qkv",
    )
    q = q.reshape(2, 2, 128, 128)
    rows = w_attn[:, 256:272, 0:4].reshape(8, 2, 8, 4)[:, :, 1:3].astype(f32)
    rows = jnp.where(first, rows, rows[:, ::-1]).reshape(BUCKETS, 4)
    table = jnp.where(first, rows[:, 0:2], rows[:, 2:4])
    (band,) = on(band_kernel, [((2, 128, 384), f32)], smem=(table,), name="band")
    kv, block, band = tie((over_chips(kv), block, band))
    kv = kv.reshape(16, 2, 128, 256)
    w_parts = Far(w_attn, (slice(None), pl.ds(0, 256), pl.ds(384, 128)))
    *exps, rl, mixed, own, sib = on(
        attend_kernel,
        [((256, D), bf16, 1)] * 4 + [((4, 256, 1), f32, 1), ((2, 2, 128, 128), bf16, 1), half, half],
        Far(q),
        Far(kv),
        band,
        w_parts,
        smem=(table,),
        scratch=[pltpu.VMEM((256, D + 128), f32)],
        vmem=24, name="attend",
    )
    mixed = mixed.reshape(512, 128)
    flipped = other_y(block)
    sib, flipped, up_a, down_a = tie((sib, flipped, along_z(block, 1), along_z(block, 3)))
    attn, flipped = tie((with_sibling(own, sib), flipped))
    attn = over_head(attn)
    up_b, down_b = along_z(flipped, 1), along_z(flipped, 3)
    hid, n2 = on(
        norm_two_kernel,
        [((32, D), f32, 1), ((32, D), bf16, 8)],
        attn,
        Rows(x_own),
        Far(gains),
        name="norm_two",
    )
    n2, up_a, up_b, down_b = tie((n2, up_a, up_b, down_b))
    blocks = [block, flipped, up_a, up_b, down_a, down_b]
    down_rows = (pl.ds(0, 320), slice(None))
    back, grads = on(
        ffn_early_kernel,
        [((512, FFC), f32, 1), ((512, 512), bf16, 1)],
        Far(cot_own),
        Far(cot_sib),
        *[Far(a, down_rows) for a in blocks],
        scratch=[pltpu.VMEM((512, D), bf16)],
        vmem=16,
        name="ffn_early",
    )
    n_own, far_a, far_b, back, grads = tie(
        (over_head(n2), along_z(up_a, 1), along_z(down_b, 3), back, grads)
    )
    blocks += [far_a, far_b]
    n_sib = to_sibling(n_own)

    hidden, gu_low, own, sib, out_own, out_sib, g2, far_a, far_b = on(
        ffn_kernel,
        [
            ((512, FFC), bf16, 1),
            ((512, 640), bf16, 1),
            part,
            part,
            part,
            part,
            line,
            ((960, 256), bf16, 1),
            ((960, 256), bf16, 1),
        ],
        n_own,
        n_sib,
        *[Far(a) for a in blocks],
        Far(back),
        Far(grads),
        Far(gains),
        vmem=28,
        name="ffn",
    )

    def weight_grads(name, ranks):
        return on(
            functools.partial(ffn_weights_kernel, ranks=ranks),
            [((960, 256), bf16, 1)] * len(ranks),
            Far(cot_own),
            Far(cot_sib),
            Far(hidden),
            Far(n_own),
            Far(n_sib),
            Far(gu_low),
            scratch=[pltpu.VMEM((512, D), bf16)],
            vmem=18,
            name=name,
        )

    fore_a, back_b, fore_b, back_a = weight_grads("ffn_weights_next", (4, 3, 5, 2))
    (out_own,) = on(
        layer_join_kernel, [part], out_own, to_sibling(out_sib), Far(hid), name="layer_join"
    )
    ffn_sum, fore_recv, back_recv, fore_a, back_b, fore_b, back_a = tie(
        (
            over_head(with_sibling(own, sib)),
            along_z(far_a, 1),
            along_z(far_b, 3),
            fore_a,
            back_b,
            fore_b,
            back_a,
        )
    )
    hig, low = on(
        norm_two_back_kernel,
        [((32, D), f32, 1), ((32, D), bf16, 8)],
        ffn_sum,
        Far(hid),
        Rows(cot_own),
        Far(gains),
        name="norm_two_back",
    )
    low, fore_recv, back_recv = tie((low, fore_recv, back_recv))
    fore_a = (fore_a.astype(f32) + fore_recv.astype(f32)).astype(bf16)
    back_b = (back_b.astype(f32) + back_recv.astype(f32)).astype(bf16)
    al_own, fore_a, back_b, fore_b, back_a, out_own = tie(
        (over_head(low), along_z(fore_a, 1), along_z(back_b, 3), fore_b, back_a, out_own)
    )
    al_sib = to_sibling(al_own)

    out_parts = over_head(out_own)
    q_low, dkv, near_sums, far_sums = on(
        attend_back_kernel,
        [
            ((2, 2, 128, 128), bf16, 1),
            ((8 * 256, 512), bf16, 1),
            ((2, 128, 384), f32),
            ((4, D), f32),
        ],
        w_parts,
        al_own,
        al_sib,
        Far(q),
        Far(kv),
        Far(rl),
        *[Far(e) for e in exps],
        scratch=[
            pltpu.VMEM((256, D), f32),
            pltpu.VMEM((256, D + 128), bf16),
            pltpu.VMEM((2, 2, 128, 128), bf16),
        ],
        vmem=28, name="attend_back",
    )
    dkv, out_parts, fore_b, back_a = tie(
        (dkv, out_parts, along_z(fore_b, 1), along_z(back_a, 3))
    )
    q_low = q_low.reshape(512, 128)

    (layer_out,) = on(layer_sum_kernel, [((32, D), bf16)], out_parts, name="layer_sum")
    (tab,) = on(table_kernel, [((BUCKETS, 128), f32)], near_sums, far_sums, name="table")
    early = on(
        early_weights_kernel,
        [((2, 256, 256), bf16, 1)] * 4,
        Far(n1),
        Far(q_low),
        Far(mixed),
        Far(al_own),
        Far(al_sib),
        vmem=14,
        name="early_weights",
    )
    near_a, near_b = weight_grads("ffn_weights_near", (0, 1))
    ffn_own, ffn_other = on(
        ffn_sum_kernel,
        [((960, 256), f32, 1), ((960, 256), bf16, 1)],
        *[Far(a) for a in (near_a, near_b, fore_a, fore_b, back_a, back_b)],
        vmem=12,
        name="ffn_sum",
    )
    kv_parts, tab, layer_out, ffn_own, ffn_other, *early = tie(
        (over_chips(dkv), tab, layer_out, ffn_own, ffn_other, *early)
    )
    kv_low, own, sib, g1 = on(
        qkv_back_kernel,
        [((512, 256), bf16, 1), part, part, line],
        kv_parts,
        Far(q_low),
        Far(w_attn),
        Far(n1),
        Far(gains),
        vmem=16,
        name="qkv_back",
    )

    rows = tab[:, 0:2].reshape(8, 2, 4)
    rows = jnp.where(first, rows, rows[:, ::-1])
    rows = jnp.pad(rows, ((0, 0), (0, 0), (0, 124))).reshape(8, 256)
    near_a, near_b, back_a, back_b, fore_a, fore_b, far_a, far_b = on(
        last_weights_kernel,
        [((272, 256), bf16, 1)] * 8,
        Far(n1),
        Far(kv_low),
        g1,
        g2,
        rows,
        vmem=14,
        name="last_weights",
    )

    def gathered(near, back, fore, far):
        return near, along_z(fore, 1), along_z(back, 3), along_z(far, 2)

    one_sum, ffn_recv, *early = tie(
        (
            over_head(with_sibling(own, sib)),
            other_y(ffn_other),
            *gathered(*early),
        )
    )
    (low,) = on(
        norm_one_back_kernel,
        [((32, D), bf16, 8)],
        one_sum,
        Rows(x_own),
        Far(gains),
        Far(hig),
        name="norm_one_back",
    )
    fore_recv, back_recv = along_z(far_a, 1), along_z(far_b, 3)
    low, fore_recv, back_recv, fore_b, back_a = tie(
        (low, fore_recv, back_recv, along_z(fore_b, 1), along_z(back_a, 3))
    )
    fore_a = (fore_a.astype(f32) + fore_recv.astype(f32)).astype(bf16)
    back_b = (back_b.astype(f32) + back_recv.astype(f32)).astype(bf16)
    fore_a, back_b = along_z(fore_a, 1), along_z(back_b, 3)
    low, layer_out = tie((low, layer_out))
    both = over_head(low)
    layer_recv = lax.ppermute(layer_out, "head", OTHER_HEAD_Y)
    layer_pair = jnp.concatenate([layer_out, layer_recv], axis=0)
    last_own, last_other = on(
        last_sum_kernel,
        [((528, 256), f32), ((528, 256), bf16)],
        *[Far(a) for a in (*early, near_a, near_b, fore_a, fore_b, back_a, back_b)],
        name="last_sum",
    )
    mine, theirs = on(
        last_split_kernel,
        [((144, 512), f32), ((144, 512), bf16)],
        last_own,
        other_y(last_other),
        name="last_split",
    )
    recv = to_sibling(theirs)
    (small,) = on(gain_kernel, [((8, 128), f32)], mine, recv, name="gain")
    both, small, *layer_pairs = tie(
        (both, small, *[lax.ppermute(layer_pair, "head", ALONG_X[d]) for d in (1, 3, 2)])
    )
    small_sums = over_head(jnp.broadcast_to(small[None], (8, 8, 128)).reshape(64, 128))
    (input_grad,) = on(unpack_kernel, [((256, D), f32, 1)], Far(both), name="unpack")
    (layer_out,) = on(
        layer_place_kernel,
        [((256, D), bf16, 1)],
        Far(layer_pair),
        *[Far(a) for a in layer_pairs],
        name="layer_place",
    )
    gain_sums = small_sums.reshape(8, 8, 128)[:, 0:2].sum(0)
    out_grad, query_grad, key_grad, value_grad = on(
        last_order_kernel,
        [((256, 128), f32, 1)] + [((128, 256), f32, 1)] * 3,
        mine,
        recv,
        name="last_order",
    )
    table_grad = in_order(small[2, 0:4].reshape(2, 2), small[3, 0:4].reshape(2, 2), 1)

    mine, theirs = on(
        ffn_split_kernel,
        [((960, 128), f32), ((960, 128), bf16)],
        Far(ffn_own),
        ffn_recv,
        name="ffn_split",
    )
    gate_grad, up_grad, down_grad = on(
        ffn_order_kernel,
        [((128, 640), f32, 1), ((128, 640), f32, 1), ((640, 128), f32, 1)],
        mine,
        to_sibling(theirs),
        name="ffn_order",
    )
    return (
        layer_out.reshape(2, 128, D),
        input_grad.reshape(2, 128, D),
        gain_sums[0],
        query_grad,
        key_grad,
        value_grad,
        out_grad,
        table_grad,
        gain_sums[1],
        gate_grad,
        up_grad,
        down_grad,
    )


def solution(mesh):
    seq_head, head_seq = P("seq", "head"), P("head", "seq")
    in_specs = (
        P(None, "seq", None),
        P(None, "seq", None),
        P(),
        P("seq"),
        seq_head,
        seq_head,
        seq_head,
        head_seq,
        seq_head,
        P("seq"),
        seq_head,
        seq_head,
        head_seq,
    )
    out_specs = (
        P(None, "seq", None),
        P(None, "seq", None),
        P("seq"),
        seq_head,
        seq_head,
        seq_head,
        head_seq,
        seq_head,
        P("seq"),
        seq_head,
        seq_head,
        head_seq,
    )
    return jax.shard_map(body, mesh=mesh, in_specs=in_specs, out_specs=out_specs, check_vma=False)
```

```python
import functools

import jax
import jax.numpy as jnp
from jax import lax
from jax.experimental import pallas as pl
from jax.experimental.pallas import tpu as pltpu
from jax.sharding import PartitionSpec as P


D = 2048
HEAD = 64
BUCKETS = 32
FFC = 320
epsilon = 1e-06
limits = (8, 12, 16, 23, 32, 46, 64, 91)
masked_score = -1000000000.0

f32, bf16, i32 = jnp.float32, jnp.bfloat16, jnp.int32
MIB = 1024 * 1024

CHIP_GROUPS = [[s for s in range(16) if s % 2 == c] for c in range(2)]
RELATIVE = ((0, 0), (0, 1), (1, 0), (1, 1), (3, 0), (3, 1), (2, 0), (2, 1))
def seq_perm(f):
    return [
        (z * 4 + y * 2 + c, (lambda t: t[0] * 4 + t[1] * 2 + t[2])(f(z, y, c)))
        for z in range(4)
        for y in range(2)
        for c in range(2)
    ]


def head_perm(f):
    return [
        (x * 2 + y, (lambda t: t[0] * 2 + t[1])(f(x, y))) for x in range(4) for y in range(2)
    ]


CORE = seq_perm(lambda z, y, c: (z, y, 1 - c))
OTHER_Y = seq_perm(lambda z, y, c: (z, 1 - y, c))
ALONG_Z = {d: seq_perm(lambda z, y, c, d=d: ((z + d) % 4, y, c)) for d in (1, 2, 3)}
OTHER_HEAD_Y = head_perm(lambda x, y: (x, 1 - y))
ALONG_X = {d: head_perm(lambda x, y, d=d: ((x + d) % 4, y)) for d in (1, 2, 3)}


def nn(a, b):
    return jnp.dot(a, b, preferred_element_type=f32)


def nt(a, b):
    return lax.dot_general(a, b, (((1,), (1,)), ((), ())), preferred_element_type=f32)


def tn(a, b):
    return lax.dot_general(a, b, (((0,), (0,)), ((), ())), preferred_element_type=f32)


class Loaded:
    def __init__(self, copy, ref, queue):
        self.copy, self.ref, self.queue, self.here = copy, ref, queue, False

    def ready(self):
        if not self.here:
            while self in self.queue:
                self.queue.pop(0).copy.start()
            self.copy.wait()
            self.here = True
            if self.queue:
                self.queue.pop(0).copy.start()
        return self.ref

    def __getitem__(self, at):
        return self.ready()[at]

    @property
    def at(self):
        return self.ready().at


class Stored:
    def __init__(self, ref, there, sems, times):
        self.ref, self.there, self.sems, self.times = ref, there, sems, times
        self.copies, self.whole = [], True

    def start(self, source, target):
        copy = pltpu.make_async_copy(source, target, self.sems.at[len(self.copies)])
        copy.start()
        self.copies.append(copy)

    def send(self):
        rows = self.ref.shape[0]
        for t in range(self.times):
            there = self.there if self.times == 1 else self.there.at[pl.ds(t * rows, rows)]
            self.start(self.ref, there)

    def send_part(self, at):
        self.start(self.ref.at[at], self.there.at[at])

    def __getitem__(self, at):
        return self.ref[at]

    def __setitem__(self, at, value):
        self.ref[at] = value

    @property
    def at(self):
        return self.ref.at


class Place:
    def __init__(self, scalars):
        self.c, self.sc, self.h = scalars[0], scalars[1], scalars[2]
        self.lengths = {0: scalars[3], 1: scalars[4]}
        self.idx = [scalars[5 + k] for k in range(8)]


def place_scalars(lengths):
    s, h = lax.axis_index("seq"), lax.axis_index("head")
    c, sc = s % 2, s // 2
    z, y = sc // 2, sc % 2
    idx = [((z + 4 - dz) % 4) * 2 + (y if dy == 0 else 1 - y) for dz, dy in RELATIVE]
    return jnp.stack([c, sc, h, lengths[0], lengths[1], *idx]).astype(i32)


class Far:
    def __init__(self, value, at=None):
        self.value, self.at = value, at

    def shape(self):
        return jax.eval_shape(lambda v: v if self.at is None else v[self.at], self.value).shape


class Rows(Far):
    def shape(self):
        return (32, self.value.shape[1])


def call(kernel, outs, lengths, *args, smem=(), scratch=(), vmem=8, ahead=16, name=None):
    n, m, fixed = len(args), len(outs), 1 + len(smem)
    far_in = [i for i, a in enumerate(args) if isinstance(a, Far)]
    far_out = [k for k, o in enumerate(outs) if len(o) == 3]

    def whole(*refs):
        lens, scalars, refs = refs[0], refs[1:fixed], refs[fixed:]
        inputs, outputs, refs = list(refs[:n]), list(refs[n : n + m]), list(refs[n + m :])
        queue = []
        for i in far_in:
            buf, sem = refs.pop(0), refs.pop(0)
            there = inputs[i]
            if isinstance(args[i], Rows):
                first = pl.multiple_of(lens[2] * 32, 32)
                there = there.at[pl.ds(first, 32)]
            elif args[i].at is not None:
                there = there.at[args[i].at]
            inputs[i] = Loaded(pltpu.make_async_copy(there, buf, sem), buf, queue)
            queue.append(inputs[i])
        for _ in range(min(ahead, len(queue))):
            queue.pop(0).copy.start()
        for k in far_out:
            buf, sems = refs.pop(0), refs.pop(0)
            outputs[k] = Stored(buf, outputs[k], sems, outs[k][2])
        kernel(Place(lens), *scalars, *inputs, *outputs, *refs)
        for i in far_in:
            inputs[i].ready()
        for k in far_out:
            if not outputs[k].copies:
                outputs[k].send()
        for k in far_out:
            for copy in outputs[k].copies:
                copy.wait()

    buffers = []
    for i in far_in:
        buffers += [pltpu.VMEM(args[i].shape(), args[i].value.dtype), pltpu.SemaphoreType.DMA]
    for k in far_out:
        shape, dtype, _ = outs[k]
        buffers += [pltpu.VMEM(shape, dtype), pltpu.SemaphoreType.DMA((24,))]
    placed = [
        pltpu.with_memory_space_constraint(a.value, pltpu.HBM)
        if isinstance(a, Far)
        else pltpu.with_memory_space_constraint(a, pltpu.VMEM)
        for a in args
    ]
    shapes = [
        pltpu.HBM((o[0][0] * o[2], *o[0][1:]), o[1])
        if len(o) == 3
        else pltpu.VMEM(o[0], o[1])
        for o in outs
    ]
    return pl.pallas_call(
        whole,
        out_shape=tuple(shapes),
        in_specs=[pl.BlockSpec(memory_space=pltpu.SMEM)] * fixed
        + [pl.BlockSpec(memory_space=pl.ANY if i in far_in else pltpu.VMEM) for i in range(n)],
        out_specs=tuple(
            pl.BlockSpec(memory_space=pl.ANY if k in far_out else pltpu.VMEM) for k in range(m)
        ),
        scratch_shapes=buffers + list(scratch),
        compiler_params=pltpu.CompilerParams(vmem_limit_bytes=vmem * MIB),
        cost_estimate=pl.CostEstimate(flops=1000, bytes_accessed=1000, transcendentals=0),
        name=name,
    )(lengths, *smem, *placed)


def lane_at(chip, core):
    return pl.multiple_of(chip * 256 + core * 128, 128)


def chunk_p(ref, rows, chip, c):
    return jnp.concatenate(
        [ref[rows, pl.ds(lane_at(chip, c), 128)], ref[rows, pl.ds(lane_at(chip, 1 - c), 128)]],
        axis=1,
    )


def rows_of(half):
    return slice(half * 256, (half + 1) * 256)


def pack_kernel(me, wq, wk, wv, wo, ga, gf, bias, mine, theirs, misc):
    misc[...] = jnp.zeros_like(misc)
    misc[0:1, 0:128] = ga[...].astype(f32)
    misc[0:1, 128:256] = gf[...].astype(f32)
    misc[1:3, 0:4] = bias[...].astype(f32)
    low = jnp.concatenate([wq[:, 0:128], wk[:, 0:128], wv[:, 0:128], wo[0:128, :]], axis=1)
    high = jnp.concatenate(
        [wq[:, 128:256], wk[:, 128:256], wv[:, 128:256], wo[128:256, :]], axis=1
    )
    theirs[0:128, :] = jnp.where(me.c == 0, high, low)
    mine[0:128, :] = jnp.where(me.c == 0, low, high)
    for res in (mine, theirs):
        res[128:144, :] = misc[...].astype(bf16)


def qkv_kernel(me, x_own, x_sib, w, n1, q, kv, gains):
    c = me.c
    rinvs = []
    for x in (x_own, x_sib):
        total = jnp.zeros((256, 1), f32)
        for k in range(8):
            v = x[:, k * 256 : (k + 1) * 256].astype(f32)
            total = total + jnp.sum(v * v, axis=1, keepdims=True)
        rinvs.append(lax.rsqrt(total * (1.0 / D) + epsilon))
    for k in range(8):
        for core, p in ((0, c), (1, 1 - c)):
            rows = w[k, 256:272, 0:256].astype(f32)
            row = jnp.where(p == 0, rows[0:1], rows[8:9])
            gains[0:1, k * 256 + core * 128 : k * 256 + core * 128 + 128] = row[:, 0:128]
            gains[1:2, k * 256 + core * 128 : k * 256 + core * 128 + 128] = row[:, 128:256]
    gains.send()
    for half, x, rinv in ((0, x_own, rinvs[0]), (1, x_sib, rinvs[1])):
        rows = rows_of(half)
        acc = jnp.zeros((256, 384), f32)
        for k in range(8):
            lanes = slice(k * 256, (k + 1) * 256)
            v = x[:, lanes].astype(f32)
            normed = (v * rinv * gains[0:1, lanes]).astype(bf16)
            n1[rows, lanes] = normed
            wk = jnp.concatenate(
                [w[k, rows_p(c), 0:384], w[k, rows_p(1 - c), 0:384]], axis=0
            )
            acc = acc + nn(normed, wk)
        q[rows, :] = acc[:, 0:128].astype(bf16)
        kv[rows, :] = acc[:, 128:384].astype(bf16)
        for chip in range(8):
            kv.start(kv.ref.at[rows], kv.there.at[pl.ds(chip * 512 + half * 256, 256)])
        n1.send_part(rows)


def rows_p(p):
    return pl.ds(pl.multiple_of(p * 128, 128), 128)


def out_weights(me, w, k):
    return jnp.concatenate([w[k, rows_p(p)] for p in (me.c, 1 - me.c)], axis=1)


def bucket_ids(offset):
    distance = jnp.abs(offset)
    coarse = 7 + sum(((distance >= threshold).astype(i32) for threshold in limits))
    within = jnp.where(distance < 8, distance, coarse)
    return within + jnp.where(offset > 0, 16, 0).astype(i32)


def band_buckets():
    return bucket_ids(
        lax.broadcasted_iota(i32, (128, 384), 1)
        - 128
        - lax.broadcasted_iota(i32, (128, 384), 0)
    )


def key_places(c):
    lane = lax.broadcasted_iota(i32, (1, D), 1)
    stored = lane // 128
    tile = (stored // 2) * 2 + jnp.where(stored % 2 == 1, 1 - c, c)
    return tile, tile * 128 + lane % 128


def band_tiles(me, half):
    c = me.c
    tile = me.sc * 2 + (c if half == 0 else 1 - c)
    lanes = []
    for step in (-1, 0, 1):
        near = tile + step
        stored = (near // 2) * 2 + jnp.where(near % 2 == 1, 1 - c, c)
        inside = jnp.logical_and(near >= 0, near < 16)
        lanes.append(pl.multiple_of(jnp.where(inside, stored, 16) * 128, 128))
    return tile, lanes


def band_kernel(me, table, band):
    ids = band_buckets()
    for j in range(2):
        value = jnp.zeros((128, 384), f32)
        for b in range(BUCKETS):
            value = jnp.where(ids == b, table[b, j], value)
        band[j] = value


def attend_kernel(me, table, q, kv, band, w, e0, e1, e2, e3, rl, mixed, own, sib, s_ref):
    exps = (e0, e1, e2, e3)
    c = me.c
    tile_of, place_of = key_places(c)
    head_lane = lax.broadcasted_iota(i32, (256, 128), 1) // HEAD
    for b in range(2):
        length = me.lengths[b]
        keys = kv[:, b, :, 0:128].reshape(D, 128)
        values = jnp.concatenate(
            [kv[:, b, :, 128:256].reshape(D, 128), jnp.ones((D, 128), bf16)], axis=1
        )
        queries = q[:, b].reshape(256, 128)
        together = jnp.zeros((256, 128), f32)
        for j in range(2):
            mine = jnp.where(head_lane == j, queries, jnp.zeros_like(queries))
            s_ref[:, 0:D] = nt(mine, keys)
            for half in range(2):
                tile, lanes = band_tiles(me, half)
                rows = slice(half * 128, (half + 1) * 128)
                for t in range(3):
                    at = pl.ds(lanes[t], 128)
                    s_ref[rows, at] = s_ref[rows, at] + band[j, :, t * 128 : (t + 1) * 128]
                added = jnp.where(place_of >= length, masked_score, 0.0) + jnp.where(
                    tile_of < tile - 1,
                    table[15, j],
                    jnp.where(tile_of > tile + 1, table[31, j], 0.0),
                )

                def some_rows(i, carry, half=half, added=added, b=b, j=j):
                    at = pl.ds(pl.multiple_of(half * 128 + i * 16, 16), 16)
                    s = s_ref[at, 0:D] + added
                    exps[b * 2 + j][at, :] = jnp.exp(
                        s - jnp.max(s, axis=1, keepdims=True)
                    ).astype(bf16)
                    return carry

                lax.fori_loop(0, 8, some_rows, 0, unroll=8)
            exps[b * 2 + j].send()
            wide = nn(exps[b * 2 + j][...], values)
            inverse = 1.0 / wide[:, 128:129]
            rl[b * 2 + j] = inverse
            together = jnp.where(head_lane == j, wide[:, 0:128] * inverse, together)
        mixed[:, b] = together.astype(bf16).reshape(2, 128, 128)
    rl.send()
    mixed.send()
    for half, res in ((1, sib), (0, own)):
        for k in range(8):
            res[:, k * 256 : (k + 1) * 256] = nn(
                mixed[half].reshape(256, 128), out_weights(me, w, k)
            ).astype(bf16)


def attend_back_kernel(
    me, w, al_own, al_sib, q, kv, rl, e0, e1, e2, e3, dq, dkv, band, far_out, d_ref, ds_ref, mg
):
    exps = (e0, e1, e2, e3)
    c = me.c
    for half, al in ((0, al_own), (1, al_sib)):
        acc = jnp.zeros((256, 128), f32)
        for k in range(8):
            acc = acc + nt(al[:, k * 256 : (k + 1) * 256], out_weights(me, w, k))
        mg[half] = acc.astype(bf16).reshape(2, 128, 128)
    tile_of, _ = key_places(c)
    head_lane = lax.broadcasted_iota(i32, (256, 128), 1) // HEAD
    ds_ref[:, D : D + 128] = jnp.zeros((256, 128), bf16)
    band[...] = jnp.zeros_like(band)
    far = [[jnp.zeros((1, D), f32) for _ in range(2)] for _ in range(2)]
    row16 = lax.broadcasted_iota(i32, (16, 256), 0)
    lane256 = lax.broadcasted_iota(i32, (16, 256), 1)
    marks = (row16 == lane256 // 128).astype(f32).astype(bf16)
    for b in range(2):
        keys = kv[:, b, :, 0:128].reshape(D, 128)
        values = kv[:, b, :, 128:256].reshape(D, 128)
        queries = q[:, b].reshape(256, 128)
        turned = queries.astype(f32).T.astype(bf16)
        grads = mg[:, b].reshape(256, 128).astype(f32)
        together = jnp.zeros((256, 128), f32)
        for j in range(2):
            inverse = rl[b * 2 + j]
            e = exps[b * 2 + j].ready()
            scaled = jnp.where(head_lane == j, grads * inverse, 0.0)
            mine = scaled.astype(bf16)
            d_ref[...] = nt(mine, values)

            def some_rows(i, carry, b=b, j=j, e=e):
                at = pl.ds(pl.multiple_of(i * 16, 16), 16)
                p = e[at, :].astype(f32)
                d = d_ref[at, :]
                inner = jnp.sum(p * d, axis=1, keepdims=True) * rl[b * 2 + j, at, :]
                ds_ref[at, 0:D] = (p * (d - inner)).astype(bf16)
                return carry

            lax.fori_loop(0, 16, some_rows, 0, unroll=16)
            score_grad = ds_ref[:, 0:D]
            together = jnp.where(head_lane == j, nn(score_grad, keys), together)
            left = jnp.concatenate([turned[j * HEAD : (j + 1) * HEAD, :], marks], axis=0)
            key_t = nn(left, score_grad)
            value_t = nn(scaled.T[j * HEAD : (j + 1) * HEAD, :].astype(bf16), e[...])
            for chip in range(8):
                lanes = slice(chip * 256, (chip + 1) * 256)
                at = chip * 256 + j * HEAD
                dkv[at : at + HEAD, b * 256 : (b + 1) * 256] = key_t[0:HEAD, lanes].astype(bf16)
                dkv[at + 128 : at + 128 + HEAD, b * 256 : (b + 1) * 256] = value_t[
                    :, lanes
                ].astype(bf16)
            for half in range(2):
                tile, lanes = band_tiles(me, half)
                rows = slice(half * 128, (half + 1) * 128)
                for t in range(3):
                    cols = slice(t * 128, (t + 1) * 128)
                    band[j, :, cols] = band[j, :, cols] + ds_ref[
                        rows, pl.ds(lanes[t], 128)
                    ].astype(f32)
                line = key_t[HEAD + half : HEAD + half + 1, :]
                far[j][0] = far[j][0] + jnp.where(tile_of < tile - 1, line, 0.0)
                far[j][1] = far[j][1] + jnp.where(tile_of > tile + 1, line, 0.0)
        dq[:, b] = together.astype(bf16).reshape(2, 128, 128)
        dkv.send_part((slice(None), pl.ds(b * 256, 256)))
    for j in range(2):
        for side in range(2):
            far_out[2 * j + side : 2 * j + side + 1, :] = far[j][side]


def table_kernel(me, band, far, tab):
    ids = band_buckets()
    lane = lax.broadcasted_iota(i32, (BUCKETS, 128), 1)
    bucket = lax.broadcasted_iota(i32, (BUCKETS, 1), 0)
    result = jnp.zeros((BUCKETS, 128), f32)
    for j in range(2):
        near = band[j]
        lines = [
            jnp.sum(jnp.where(ids == b, near, 0.0), axis=0, keepdims=True) for b in range(BUCKETS)
        ]
        column = jnp.sum(jnp.concatenate(lines, axis=0), axis=1, keepdims=True)
        sides = [jnp.sum(far[2 * j + k : 2 * j + k + 1, :], axis=1, keepdims=True) for k in (0, 1)]
        column = column + jnp.where(bucket == 15, sides[0], 0.0)
        column = column + jnp.where(bucket == 31, sides[1], 0.0)
        result = jnp.where(lane == j, column, result)
    tab[...] = result


def summed(parts, first, rows):
    total = parts[first : first + rows, :].astype(f32)
    for k in range(1, 8):
        total = total + parts[k * 32 + first : k * 32 + first + rows, :].astype(f32)
    return total


def spread_rows(res, first, rows, value):
    at = pl.ds(first, rows)
    res[at, :] = value.astype(bf16)
    size = res.ref.shape[0]
    for t in range(res.times):
        res.start(res.ref.at[at], res.there.at[pl.ds(t * size + first, rows)])


def norm_two_kernel(me, parts, x, gains, hid, normed):
    for first in (0, 16):
        rows = slice(first, first + 16)
        hidden_in = summed(parts, first, 16) + x[rows, :].astype(f32)
        rinv = lax.rsqrt(jnp.mean(hidden_in * hidden_in, axis=1, keepdims=True) + epsilon)
        spread_rows(normed, first, 16, hidden_in * rinv * gains[1:2, :])
        hid[rows, :] = hidden_in


def norm_back(value, grad, gain):
    rinv = lax.rsqrt(jnp.mean(value * value, axis=1, keepdims=True) + epsilon)
    u = grad * gain
    return rinv * u - (rinv * rinv * rinv) * value * jnp.mean(u * value, axis=1, keepdims=True)


def live_rows(me, half, b, first, count):
    c = me.c
    core = c if half == 0 else 1 - c
    place = (me.sc * 2 + core) * 128 + first + lax.broadcasted_iota(i32, (count, 1), 0)
    return place < me.lengths[b]


def norm_two_back_kernel(me, parts, hid, cot, gains, hig, low):
    b = me.h // 4
    for first in (0, 16):
        rows = slice(first, first + 16)
        place = (
            (me.sc * 2 + me.c) * 128
            + (me.h - b * 4) * 32
            + first
            + lax.broadcasted_iota(i32, (16, 1), 0)
        )
        total = summed(parts, first, 16)
        grad = norm_back(hid[rows, :], total, gains[1:2, :])
        grad = grad + jnp.where(place < jnp.where(b == 0, me.lengths[0], me.lengths[1]), cot[rows, :].astype(f32), 0.0)
        spread_rows(low, first, 16, grad)
        hig[rows, :] = grad


def norm_one_back_kernel(me, parts, x, gains, hig, res):
    for first in (0, 16):
        rows = slice(first, first + 16)
        total = summed(parts, first, 16)
        grad = norm_back(x[rows, :].astype(f32), total, gains[0:1, :]) + hig[rows, :]
        spread_rows(res, first, 16, grad)


def gelu_pair(g):
    k0, k1 = 0.7978845608028654, 0.044715
    g2 = g * g
    t = jnp.tanh(k0 * g * (1.0 + k1 * g2))
    value = 0.5 * g * (1.0 + t)
    slope = 0.5 * (1.0 + t) + 0.5 * g * (1.0 - t * t) * k0 * (1.0 + 3.0 * k1 * g2)
    return value, slope


def gate_up(w):
    wide = jnp.concatenate([w[320:576, :], w[576:832, :]], axis=1)
    rest = jnp.concatenate([w[832:960, 0:128], w[832:960, 128:256]], axis=0)
    return wide, rest


def live_cotangent(me, out_low, cot_own, cot_sib):
    for half, cot in ((0, cot_own), (1, cot_sib)):
        live = jnp.concatenate([live_rows(me, half, b, 0, 128) for b in range(2)], axis=0)
        out_low[rows_of(half), :] = jnp.where(live, cot[...], jnp.zeros((), bf16))


def weight_grad(me, k, res, hidden, grads, n_own, n_sib, gu_low):
    chip, c = me.idx[k], me.c
    res[0:320, :] = tn(hidden[...], grads).astype(bf16)
    v = jnp.concatenate(
        [chunk_p(n_own, slice(None), chip, c), chunk_p(n_sib, slice(None), chip, c)], axis=0
    )
    part = tn(v, gu_low[...]).astype(bf16)
    res[320:576, :] = part[:, 0:256]
    res[576:832, :] = part[:, 256:512]
    res[832:960, 0:128] = part[0:128, 512:640]
    res[832:960, 128:256] = part[128:256, 512:640]
    res.send()


def ffn_early_kernel(me, cot_own, cot_sib, *refs):
    blocks, (back, grads, out_low) = refs[:6], refs[6:]
    live_cotangent(me, out_low, cot_own, cot_sib)
    for k in (6, 7):
        grads[:, (k - 6) * 256 : (k - 5) * 256] = chunk_p(out_low, slice(None), me.idx[k], me.c)
    grads.send()
    total = jnp.zeros((512, FFC), f32)
    for k in range(6):
        total = total + nt(chunk_p(out_low, slice(None), me.idx[k], me.c), blocks[k][...])
    back[...] = total


def ffn_kernel(me, n_own, n_sib, *refs):
    blocks, (back, grads, gains), results = refs[:8], refs[8:11], refs[11:]
    hidden, gu_low, own, sib, out_own, out_sib, gain_sum, far_a, far_b = results
    c = me.c
    all_rows = slice(None)

    def tokens(chip):
        return jnp.concatenate(
            [chunk_p(n_own, all_rows, chip, c), chunk_p(n_sib, all_rows, chip, c)], axis=0
        )

    gu = jnp.zeros((512, 512), f32)
    rest = jnp.zeros((512, 128), f32)
    for k in range(8):
        if k == 2:
            for a in (*blocks[2:], back, grads, gains):
                a.ready()
        v = tokens(me.idx[k])
        wide, last = gate_up(blocks[k])
        gu = gu + nn(v, wide)
        rest = rest + nn(v, last)
    total = back[...]
    for k in (6, 7):
        total = total + nt(grads[:, (k - 6) * 256 : (k - 5) * 256], blocks[k][0:320, :])
    for gate, up, dh, at, size in (
        (gu[:, 0:256], gu[:, 256:512], total[:, 0:256], 0, 256),
        (rest[:, 0:64], rest[:, 64:128], total[:, 256:FFC], 256, 64),
    ):
        value, slope = gelu_pair(gate)
        hidden[:, at : at + size] = (value * up).astype(bf16)
        at = 2 * at
        gu_low[:, at : at + size] = (dh * up * slope).astype(bf16)
        gu_low[:, at + size : at + 2 * size] = (dh * value).astype(bf16)
    hidden.send()
    gu_low.send()
    for k, res in ((6, far_a), (7, far_b)):
        chunk = grads[:, (k - 6) * 256 : (k - 5) * 256]
        weight_grad(me, k, res, hidden, chunk, n_own, n_sib, gu_low)
    for k in range(8):
        chip = me.idx[k]
        wide, last = gate_up(blocks[k])
        part = nt(gu_low[:, 0:512], wide) + nt(gu_low[:, 512:640], last)
        made = nn(hidden[...], blocks[k][0:320, :])
        line = jnp.sum(part * tokens(chip).astype(f32), axis=0, keepdims=True)
        for p, core in ((0, c), (1, 1 - c)):
            lanes = pl.ds(lane_at(chip, core), 128)
            cols = slice(p * 128, (p + 1) * 128)
            gain_sum[0:1, lanes] = line[:, cols] / gains[1:2, lanes]
            for half, res, out in ((0, own, out_own), (1, sib, out_sib)):
                res[:, lanes] = part[rows_of(half), cols].astype(bf16)
                out[:, lanes] = made[rows_of(half), cols].astype(bf16)


def ffn_weights_kernel(me, cot_own, cot_sib, hidden, n_own, n_sib, gu_low, *results, ranks):
    *results, out_low = results
    live_cotangent(me, out_low, cot_own, cot_sib)
    for k, res in zip(ranks, results):
        grads = chunk_p(out_low, slice(None), me.idx[k], me.c)
        weight_grad(me, k, res, hidden, grads, n_own, n_sib, gu_low)


def layer_join_kernel(me, own, recv, hid, res):
    res[...] = (own[...].astype(f32) + recv[...].astype(f32)).astype(bf16)
    at = pl.ds(pl.multiple_of(me.h * 32, 32), 32)
    res[at, :] = (own[at, :].astype(f32) + recv[at, :].astype(f32) + hid[...]).astype(bf16)


def qkv_back_kernel(me, parts, q_low, w, n1, gains, kv_low, own, sib, gain_sum):
    c = me.c
    total = parts[0:256, :].astype(f32)
    for k in range(1, 8):
        total = total + parts[k * 256 : (k + 1) * 256, :].astype(f32)
    for b in range(2):
        for half in range(2):
            lanes = slice(b * 256 + half * 128, b * 256 + (half + 1) * 128)
            kv_low[half * 256 + b * 128 : half * 256 + (b + 1) * 128, :] = total[:, lanes].T.astype(
                bf16
            )
    for k in range(8):
        wk = jnp.concatenate(
            [
                w[k, rows_p(p), 0:384]
                for p in (c, 1 - c)
            ],
            axis=0,
        )
        lanes = slice(k * 256, (k + 1) * 256)
        line = jnp.zeros((1, 256), f32)
        for half, res in ((0, own), (1, sib)):
            rows = rows_of(half)
            part = nt(q_low[rows, :], wk[:, 0:128]) + nt(kv_low[rows, :], wk[:, 128:384])
            line = line + jnp.sum(part * n1[rows, lanes].astype(f32), axis=0, keepdims=True)
            res[:, lanes] = part.astype(bf16)
        gain_sum[0:1, lanes] = line / gains[0:1, lanes]


def early_weights_kernel(me, n1, q_low, mixed, al_own, al_sib, *results):
    c = me.c
    for k in range(8):
        chip = me.idx[k]
        res = results[k // 2].at[k % 2]
        al = jnp.concatenate(
            [chunk_p(al_own, slice(None), chip, c), chunk_p(al_sib, slice(None), chip, c)], axis=0
        )
        res[0:128, :] = tn(mixed[...], al).astype(bf16)
        part = tn(chunk_p(n1, slice(None), chip, c), q_low[...]).astype(bf16)
        res[128:256, 0:128] = part[0:128]
        res[128:256, 128:256] = part[128:256]
        if k % 2:
            results[k // 2].send()


def last_weights_kernel(me, n1, kv_low, g1, g2, tab, *results):
    c = me.c
    for k in (6, 7, 5, 2, 4, 3, 0, 1):
        chip = me.idx[k]
        res = results[k]
        part = tn(chunk_p(n1, slice(None), chip, c), kv_low[...]).astype(bf16)
        for p in range(2):
            rows, lanes = slice(p * 128, (p + 1) * 128), slice(p * 128, (p + 1) * 128)
            res[0:128, lanes] = part[rows, 0:128]
            res[128:256, lanes] = part[rows, 128:256]
        one = slice(0, 1)
        misc = jnp.concatenate(
            [
                chunk_p(g1, one, chip, c),
                chunk_p(g2, one, chip, c),
                tab[pl.ds(chip, 1), :],
                jnp.zeros((13, 256), f32),
            ],
            axis=0,
        )
        res[256:272, :] = misc.astype(bf16)
        res.send()


def unpack_kernel(me, rows, input_grad):
    for k in range(4):
        at = slice(k * 64, (k + 1) * 64)
        input_grad[at, :] = rows[at, :].astype(f32)
        input_grad.send_part(at)


def layer_place_kernel(me, *refs):
    parts, res = refs[:4], refs[4]
    x, y = me.h // 2, me.h % 2
    for part, step in zip(parts, (0, 1, 3, 2)):
        from_x = (x + 4 - step) % 4
        for k, from_y in ((0, y), (1, 1 - y)):
            at = pl.ds(pl.multiple_of((from_x * 2 + from_y) * 32, 32), 32)
            res[at, :] = part[k * 32 : (k + 1) * 32, :]


def layer_sum_kernel(me, parts, res):
    res[...] = summed(parts, 0, 32).astype(bf16)


def ffn_sum_kernel(me, *refs):
    parts, results = refs[:6], refs[6:]
    for y, res in enumerate(results):
        value = parts[y][...].astype(f32)
        for a in parts[2 + y :: 2]:
            value = value + a[...].astype(f32)
        res[...] = value.astype(res.ref.dtype)
        res.send()


def last_sum_kernel(me, *refs):
    early, late, (own, other) = refs[:4], refs[4:10], refs[10:]
    for y, res in ((1, other), (0, own)):
        value = early[0][y].astype(f32)
        for a in early[1:]:
            value = value + a[y].astype(f32)
        res[0:256, :] = value.astype(f32 if y == 0 else bf16)
        value = late[y][...].astype(f32)
        for a in late[2 + y :: 2]:
            value = value + a[...].astype(f32)
        res[256:528, :] = value.astype(f32 if y == 0 else bf16)


def last_split_kernel(me, own, recv, mine, theirs):
    total = own[...] + recv[...].astype(f32)
    for p, res in ((0, mine), (1, theirs)):
        cols = slice(p * 128, (p + 1) * 128)
        parts = [total[k * 128 : (k + 1) * 128, cols] for k in range(4)]
        value = jnp.concatenate(parts, axis=1)
        res[0:128, :] = value.astype(bf16 if p else f32)
        value = jnp.concatenate([total[512:528, cols]] * 4, axis=1)
        res[128:144, :] = value.astype(bf16 if p else f32)


def gain_kernel(me, mine, recv, res):
    a, b = mine[128:144, 0:128], recv[128:144, 0:128].astype(f32)
    res[...] = jnp.concatenate([a[0:2] + b[0:2], a[2:3], b[2:3], a[4:8]], axis=0)


def ffn_split_kernel(me, own, recv, mine, theirs):
    for p, res in ((1, theirs), (0, mine)):
        lanes = slice(p * 128, (p + 1) * 128)
        rows = [(0, 320, lanes)]
        for first in (320, 576):
            rows += [(first + p * 128, 128, slice(0, 128)), (first + p * 128, 128, slice(128, 256))]
        rows.append((832, 128, lanes))
        at = 0
        for first, size, cols in rows:
            value = own[first : first + size, cols] + recv[first : first + size, cols].astype(f32)
            res[at : at + size, :] = value.astype(bf16 if p else f32)
            at += size


def ffn_order_kernel(me, mine, recv, gate_grad, up_grad, down_grad):
    first = me.c == 0
    a, b = mine[0:320, :], recv[0:320, :].astype(f32)
    down_grad[0:320, :] = jnp.where(first, a, b)
    down_grad[320:640, :] = jnp.where(first, b, a)
    down_grad.send()
    for at, lane, res in ((320, 0, gate_grad), (576, 64, up_grad)):
        sides = []
        for ref in (mine, recv):
            rest = ref[832:960, lane : lane + 64]
            sides.append(
                jnp.concatenate([ref[at : at + 128, :], ref[at + 128 : at + 256, :], rest], axis=1)
            )
        a, b = sides[0], sides[1].astype(f32)
        res[...] = jnp.concatenate([jnp.where(first, a, b), jnp.where(first, b, a)], axis=1)
        res.send()


def last_order_kernel(me, mine, recv, out_grad, query_grad, key_grad, value_grad):
    a, b = mine[0:128, :], recv[0:128, :].astype(f32)
    low, high = jnp.where(me.c == 0, a, b), jnp.where(me.c == 0, b, a)
    out_grad[0:128, :] = low[:, 0:128]
    out_grad[128:256, :] = high[:, 0:128]
    for k, res in ((1, query_grad), (2, key_grad), (3, value_grad)):
        cols = slice(k * 128, (k + 1) * 128)
        res[:, 0:128] = low[:, cols]
        res[:, 128:256] = high[:, cols]


def to_sibling(a):
    return lax.ppermute(a, "seq", CORE)


def over_head(a):
    return lax.all_to_all(a, "head", 0, 0, tiled=True)


def over_chips(a):
    return lax.all_to_all(a, "seq", 0, 0, axis_index_groups=CHIP_GROUPS, tiled=True)


def body(
    inputs,
    cotangent,
    lengths,
    attn_gain,
    w_query,
    w_key,
    w_value,
    w_out,
    bias_table,
    ffn_gain,
    w_gate,
    w_up,
    w_down,
):
    s = lax.axis_index("seq")
    first = s % 2 == 0
    scalars = place_scalars(lengths)

    def halves(a, axis):
        low, high = jnp.split(a, 2, axis=axis)
        return jnp.where(first, low, high), jnp.where(first, high, low)

    def in_order(own, sib, axis):
        return jnp.where(
            first,
            jnp.concatenate([own, sib], axis=axis),
            jnp.concatenate([sib, own], axis=axis),
        )

    def on(kernel, outs, *args, **more):
        return call(kernel, outs, scalars, *args, **more)

    mine, theirs = on(
        pack_kernel,
        [((144, 512), bf16)] * 2,
        Far(w_query),
        Far(w_key),
        Far(w_value),
        Far(w_out),
        Far(attn_gain.reshape(1, 128)),
        Far(ffn_gain.reshape(1, 128)),
        Far(bias_table),
        scratch=[pltpu.VMEM((16, 512), f32)],
        name="pack",
    )
    recv = to_sibling(theirs)
    block = jnp.concatenate([mine[0:128], recv[0:128], mine[128:136], recv[128:136]], axis=0)
    w_attn = over_chips(jnp.broadcast_to(block[None], (8, 272, 512)).reshape(8 * 272, 512))
    w_attn = w_attn.reshape(8, 272, 512)

    x_own = inputs.reshape(256, D)
    x_sib = to_sibling(x_own)
    cot_own = cotangent.reshape(256, D)
    cot_sib = to_sibling(cot_own)

    down_mine, down_theirs = halves(w_down, 0)
    gate_mine, gate_theirs = halves(w_gate, 1)
    up_mine, up_theirs = halves(w_up, 1)

    def joined(gate, up):
        return jnp.concatenate(
            [gate[:, 0:256], up[:, 0:256], gate[:, 256:FFC], up[:, 256:FFC]], axis=1
        )

    gu_mine = joined(gate_mine, up_mine)
    down_recv = to_sibling(down_theirs)
    gu_recv = to_sibling(joined(gate_theirs, up_theirs))
    block = jnp.concatenate(
        [
            jnp.concatenate([down_mine, down_recv], axis=1),
            jnp.concatenate([gu_mine[:, 0:256], gu_recv[:, 0:256]], axis=0),
            jnp.concatenate([gu_mine[:, 256:512], gu_recv[:, 256:512]], axis=0),
            jnp.concatenate([gu_mine[:, 512:640], gu_recv[:, 512:640]], axis=1),
        ],
        axis=0,
    )

    def with_sibling(own, sib):
        return (own.astype(f32) + to_sibling(sib).astype(f32)).astype(bf16)

    def along_z(a, steps):
        return lax.ppermute(a, "seq", ALONG_Z[steps % 4])

    def other_y(a):
        return lax.ppermute(a, "seq", OTHER_Y)

    tie = lax.optimization_barrier
    half, part, line = ((256, D), bf16), ((256, D), bf16), ((1, D), f32)

    n1, q, kv, gains = on(
        qkv_kernel,
        [((512, D), bf16, 1), ((512, 128), bf16, 1), ((512, 256), bf16, 8), ((2, D), f32, 1)],
        x_own,
        Far(x_sib),
        Far(w_attn),
        vmem=16,
        name="qkv",
    )
    q = q.reshape(2, 2, 128, 128)
    rows = w_attn[:, 256:272, 0:4].reshape(8, 2, 8, 4)[:, :, 1:3].astype(f32)
    rows = jnp.where(first, rows, rows[:, ::-1]).reshape(BUCKETS, 4)
    table = jnp.where(first, rows[:, 0:2], rows[:, 2:4])
    (band,) = on(band_kernel, [((2, 128, 384), f32)], smem=(table,), name="band")
    kv, block, band = tie((over_chips(kv), block, band))
    kv = kv.reshape(16, 2, 128, 256)
    w_parts = Far(w_attn, (slice(None), pl.ds(0, 256), pl.ds(384, 128)))
    *exps, rl, mixed, own, sib = on(
        attend_kernel,
        [((256, D), bf16, 1)] * 4 + [((4, 256, 1), f32, 1), ((2, 2, 128, 128), bf16, 1), half, half],
        Far(q),
        Far(kv),
        band,
        w_parts,
        smem=(table,),
        scratch=[pltpu.VMEM((256, D + 128), f32)],
        vmem=24, name="attend",
    )
    mixed = mixed.reshape(512, 128)
    flipped = other_y(block)
    sib, flipped, up_a, down_a = tie((sib, flipped, along_z(block, 1), along_z(block, 3)))
    attn, flipped = tie((with_sibling(own, sib), flipped))
    attn = over_head(attn)
    up_b, down_b = along_z(flipped, 1), along_z(flipped, 3)
    hid, n2 = on(
        norm_two_kernel,
        [((32, D), f32, 1), ((32, D), bf16, 8)],
        attn,
        Rows(x_own),
        Far(gains),
        name="norm_two",
    )
    n2, up_a, up_b, down_b = tie((n2, up_a, up_b, down_b))
    blocks = [block, flipped, up_a, up_b, down_a, down_b]
    down_rows = (pl.ds(0, 320), slice(None))
    back, grads = on(
        ffn_early_kernel,
        [((512, FFC), f32, 1), ((512, 512), bf16, 1)],
        Far(cot_own),
        Far(cot_sib),
        *[Far(a, down_rows) for a in blocks],
        scratch=[pltpu.VMEM((512, D), bf16)],
        vmem=16,
        name="ffn_early",
    )
    n_own, far_a, far_b, back, grads = tie(
        (over_head(n2), along_z(up_a, 1), along_z(down_b, 3), back, grads)
    )
    blocks += [far_a, far_b]
    n_sib = to_sibling(n_own)

    hidden, gu_low, own, sib, out_own, out_sib, g2, far_a, far_b = on(
        ffn_kernel,
        [
            ((512, FFC), bf16, 1),
            ((512, 640), bf16, 1),
            part,
            part,
            part,
            part,
            line,
            ((960, 256), bf16, 1),
            ((960, 256), bf16, 1),
        ],
        n_own,
        n_sib,
        *[Far(a) for a in blocks],
        Far(back),
        Far(grads),
        Far(gains),
        vmem=28,
        name="ffn",
    )

    def weight_grads(name, ranks):
        return on(
            functools.partial(ffn_weights_kernel, ranks=ranks),
            [((960, 256), bf16, 1)] * len(ranks),
            Far(cot_own),
            Far(cot_sib),
            Far(hidden),
            Far(n_own),
            Far(n_sib),
            Far(gu_low),
            scratch=[pltpu.VMEM((512, D), bf16)],
            vmem=18,
            name=name,
        )

    fore_a, back_b, fore_b, back_a = weight_grads("ffn_weights_next", (4, 3, 5, 2))
    (out_own,) = on(
        layer_join_kernel, [part], out_own, to_sibling(out_sib), Far(hid), name="layer_join"
    )
    ffn_sum, fore_recv, back_recv, fore_a, back_b, fore_b, back_a = tie(
        (
            over_head(with_sibling(own, sib)),
            along_z(far_a, 1),
            along_z(far_b, 3),
            fore_a,
            back_b,
            fore_b,
            back_a,
        )
    )
    hig, low = on(
        norm_two_back_kernel,
        [((32, D), f32, 1), ((32, D), bf16, 8)],
        ffn_sum,
        Far(hid),
        Rows(cot_own),
        Far(gains),
        name="norm_two_back",
    )
    low, fore_recv, back_recv = tie((low, fore_recv, back_recv))
    fore_a = (fore_a.astype(f32) + fore_recv.astype(f32)).astype(bf16)
    back_b = (back_b.astype(f32) + back_recv.astype(f32)).astype(bf16)
    al_own, fore_a, back_b, fore_b, back_a, out_own = tie(
        (over_head(low), along_z(fore_a, 1), along_z(back_b, 3), fore_b, back_a, out_own)
    )
    al_sib = to_sibling(al_own)

    out_parts = over_head(out_own)
    q_low, dkv, near_sums, far_sums = on(
        attend_back_kernel,
        [
            ((2, 2, 128, 128), bf16, 1),
            ((8 * 256, 512), bf16, 1),
            ((2, 128, 384), f32),
            ((4, D), f32),
        ],
        w_parts,
        al_own,
        al_sib,
        Far(q),
        Far(kv),
        Far(rl),
        *[Far(e) for e in exps],
        scratch=[
            pltpu.VMEM((256, D), f32),
            pltpu.VMEM((256, D + 128), bf16),
            pltpu.VMEM((2, 2, 128, 128), bf16),
        ],
        vmem=28, name="attend_back",
    )
    dkv, out_parts, fore_b, back_a = tie(
        (dkv, out_parts, along_z(fore_b, 1), along_z(back_a, 3))
    )
    q_low = q_low.reshape(512, 128)

    (layer_out,) = on(layer_sum_kernel, [((32, D), bf16)], out_parts, name="layer_sum")
    (tab,) = on(table_kernel, [((BUCKETS, 128), f32)], near_sums, far_sums, name="table")
    early = on(
        early_weights_kernel,
        [((2, 256, 256), bf16, 1)] * 4,
        Far(n1),
        Far(q_low),
        Far(mixed),
        Far(al_own),
        Far(al_sib),
        vmem=14,
        name="early_weights",
    )
    near_a, near_b = weight_grads("ffn_weights_near", (0, 1))
    ffn_own, ffn_other = on(
        ffn_sum_kernel,
        [((960, 256), f32, 1), ((960, 256), bf16, 1)],
        *[Far(a) for a in (near_a, near_b, fore_a, fore_b, back_a, back_b)],
        vmem=12,
        name="ffn_sum",
    )
    kv_parts, tab, layer_out, ffn_own, ffn_other, *early = tie(
        (over_chips(dkv), tab, layer_out, ffn_own, ffn_other, *early)
    )
    kv_low, own, sib, g1 = on(
        qkv_back_kernel,
        [((512, 256), bf16, 1), part, part, line],
        kv_parts,
        Far(q_low),
        Far(w_attn),
        Far(n1),
        Far(gains),
        vmem=16,
        name="qkv_back",
    )

    rows = tab[:, 0:2].reshape(8, 2, 4)
    rows = jnp.where(first, rows, rows[:, ::-1])
    rows = jnp.pad(rows, ((0, 0), (0, 0), (0, 124))).reshape(8, 256)
    near_a, near_b, back_a, back_b, fore_a, fore_b, far_a, far_b = on(
        last_weights_kernel,
        [((272, 256), bf16, 1)] * 8,
        Far(n1),
        Far(kv_low),
        g1,
        g2,
        rows,
        vmem=14,
        name="last_weights",
    )

    def gathered(near, back, fore, far):
        return near, along_z(fore, 1), along_z(back, 3), along_z(far, 2)

    one_sum, *early = tie((over_head(with_sibling(own, sib)), *gathered(*early)))
    ffn_recv = other_y(ffn_other)
    (low,) = on(
        norm_one_back_kernel,
        [((32, D), bf16, 8)],
        one_sum,
        Rows(x_own),
        Far(gains),
        Far(hig),
        name="norm_one_back",
    )
    fore_recv, back_recv = along_z(far_a, 1), along_z(far_b, 3)
    low, fore_recv, back_recv, fore_b, back_a = tie(
        (low, fore_recv, back_recv, along_z(fore_b, 1), along_z(back_a, 3))
    )
    fore_a = (fore_a.astype(f32) + fore_recv.astype(f32)).astype(bf16)
    back_b = (back_b.astype(f32) + back_recv.astype(f32)).astype(bf16)
    fore_a, back_b = along_z(fore_a, 1), along_z(back_b, 3)
    low, layer_out, ffn_recv = tie((low, layer_out, ffn_recv))
    both = over_head(low)
    layer_recv = lax.ppermute(layer_out, "head", OTHER_HEAD_Y)
    layer_pair = jnp.concatenate([layer_out, layer_recv], axis=0)
    last_own, last_other = on(
        last_sum_kernel,
        [((528, 256), f32), ((528, 256), bf16)],
        *[Far(a) for a in (*early, near_a, near_b, fore_a, fore_b, back_a, back_b)],
        name="last_sum",
    )
    mine, theirs = on(
        last_split_kernel,
        [((144, 512), f32), ((144, 512), bf16)],
        last_own,
        other_y(last_other),
        name="last_split",
    )
    recv = to_sibling(theirs)
    (small,) = on(gain_kernel, [((8, 128), f32)], mine, recv, name="gain")
    both, small, *layer_pairs = tie(
        (both, small, *[lax.ppermute(layer_pair, "head", ALONG_X[d]) for d in (1, 3, 2)])
    )
    small_sums = over_head(jnp.broadcast_to(small[None], (8, 8, 128)).reshape(64, 128))
    (input_grad,) = on(unpack_kernel, [((256, D), f32, 1)], Far(both), name="unpack")
    (layer_out,) = on(
        layer_place_kernel,
        [((256, D), bf16, 1)],
        Far(layer_pair),
        *[Far(a) for a in layer_pairs],
        name="layer_place",
    )
    gain_sums = small_sums.reshape(8, 8, 128)[:, 0:2].sum(0)
    out_grad, query_grad, key_grad, value_grad = on(
        last_order_kernel,
        [((256, 128), f32, 1)] + [((128, 256), f32, 1)] * 3,
        mine,
        recv,
        name="last_order",
    )
    table_grad = in_order(small[2, 0:4].reshape(2, 2), small[3, 0:4].reshape(2, 2), 1)

    mine, theirs = on(
        ffn_split_kernel,
        [((960, 128), f32), ((960, 128), bf16)],
        Far(ffn_own),
        ffn_recv,
        name="ffn_split",
    )
    gate_grad, up_grad, down_grad = on(
        ffn_order_kernel,
        [((128, 640), f32, 1), ((128, 640), f32, 1), ((640, 128), f32, 1)],
        mine,
        to_sibling(theirs),
        name="ffn_order",
    )
    return (
        layer_out.reshape(2, 128, D),
        input_grad.reshape(2, 128, D),
        gain_sums[0],
        query_grad,
        key_grad,
        value_grad,
        out_grad,
        table_grad,
        gain_sums[1],
        gate_grad,
        up_grad,
        down_grad,
    )


def solution(mesh):
    seq_head, head_seq = P("seq", "head"), P("head", "seq")
    in_specs = (
        P(None, "seq", None),
        P(None, "seq", None),
        P(),
        P("seq"),
        seq_head,
        seq_head,
        seq_head,
        head_seq,
        seq_head,
        P("seq"),
        seq_head,
        seq_head,
        head_seq,
    )
    out_specs = (
        P(None, "seq", None),
        P(None, "seq", None),
        P("seq"),
        seq_head,
        seq_head,
        seq_head,
        head_seq,
        seq_head,
        P("seq"),
        seq_head,
        seq_head,
        head_seq,
    )
    return jax.shard_map(body, mesh=mesh, in_specs=in_specs, out_specs=out_specs, check_vma=False)
```

```python
import functools

import jax
import jax.numpy as jnp
from jax import lax
from jax.experimental import pallas as pl
from jax.experimental.pallas import tpu as pltpu
from jax.sharding import PartitionSpec as P


D = 2048
HEAD = 64
BUCKETS = 32
FFC = 320
epsilon = 1e-06
limits = (8, 12, 16, 23, 32, 46, 64, 91)
masked_score = -1000000000.0

f32, bf16, i32 = jnp.float32, jnp.bfloat16, jnp.int32
MIB = 1024 * 1024

CHIP_GROUPS = [[s for s in range(16) if s % 2 == c] for c in range(2)]
RELATIVE = ((0, 0), (0, 1), (1, 0), (1, 1), (3, 0), (3, 1), (2, 0), (2, 1))
def seq_perm(f):
    return [
        (z * 4 + y * 2 + c, (lambda t: t[0] * 4 + t[1] * 2 + t[2])(f(z, y, c)))
        for z in range(4)
        for y in range(2)
        for c in range(2)
    ]


def head_perm(f):
    return [
        (x * 2 + y, (lambda t: t[0] * 2 + t[1])(f(x, y))) for x in range(4) for y in range(2)
    ]


CORE = seq_perm(lambda z, y, c: (z, y, 1 - c))
OTHER_Y = seq_perm(lambda z, y, c: (z, 1 - y, c))
ALONG_Z = {d: seq_perm(lambda z, y, c, d=d: ((z + d) % 4, y, c)) for d in (1, 2, 3)}
OTHER_HEAD_Y = head_perm(lambda x, y: (x, 1 - y))
ALONG_X = {d: head_perm(lambda x, y, d=d: ((x + d) % 4, y)) for d in (1, 2, 3)}


def nn(a, b):
    return jnp.dot(a, b, preferred_element_type=f32)


def nt(a, b):
    return lax.dot_general(a, b, (((1,), (1,)), ((), ())), preferred_element_type=f32)


def tn(a, b):
    return lax.dot_general(a, b, (((0,), (0,)), ((), ())), preferred_element_type=f32)


class Loaded:
    def __init__(self, copy, ref, queue):
        self.copy, self.ref, self.queue, self.here = copy, ref, queue, False

    def ready(self):
        if not self.here:
            while self in self.queue:
                self.queue.pop(0).copy.start()
            self.copy.wait()
            self.here = True
            if self.queue:
                self.queue.pop(0).copy.start()
        return self.ref

    def __getitem__(self, at):
        return self.ready()[at]

    @property
    def at(self):
        return self.ready().at


class Stored:
    def __init__(self, ref, there, sems, times):
        self.ref, self.there, self.sems, self.times = ref, there, sems, times
        self.copies, self.whole = [], True

    def start(self, source, target):
        copy = pltpu.make_async_copy(source, target, self.sems.at[len(self.copies)])
        copy.start()
        self.copies.append(copy)

    def send(self):
        rows = self.ref.shape[0]
        for t in range(self.times):
            there = self.there if self.times == 1 else self.there.at[pl.ds(t * rows, rows)]
            self.start(self.ref, there)

    def send_part(self, at):
        self.start(self.ref.at[at], self.there.at[at])

    def __getitem__(self, at):
        return self.ref[at]

    def __setitem__(self, at, value):
        self.ref[at] = value

    @property
    def at(self):
        return self.ref.at


class Place:
    def __init__(self, scalars):
        self.c, self.sc, self.h = scalars[0], scalars[1], scalars[2]
        self.lengths = {0: scalars[3], 1: scalars[4]}
        self.idx = [scalars[5 + k] for k in range(8)]


def place_scalars(lengths):
    s, h = lax.axis_index("seq"), lax.axis_index("head")
    c, sc = s % 2, s // 2
    z, y = sc // 2, sc % 2
    idx = [((z + 4 - dz) % 4) * 2 + (y if dy == 0 else 1 - y) for dz, dy in RELATIVE]
    return jnp.stack([c, sc, h, lengths[0], lengths[1], *idx]).astype(i32)


class Far:
    def __init__(self, value, at=None):
        self.value, self.at = value, at

    def shape(self):
        return jax.eval_shape(lambda v: v if self.at is None else v[self.at], self.value).shape


class Rows(Far):
    def shape(self):
        return (32, self.value.shape[1])


def call(kernel, outs, lengths, *args, smem=(), scratch=(), vmem=8, ahead=16, name=None):
    n, m, fixed = len(args), len(outs), 1 + len(smem)
    far_in = [i for i, a in enumerate(args) if isinstance(a, Far)]
    far_out = [k for k, o in enumerate(outs) if len(o) == 3]

    def whole(*refs):
        lens, scalars, refs = refs[0], refs[1:fixed], refs[fixed:]
        inputs, outputs, refs = list(refs[:n]), list(refs[n : n + m]), list(refs[n + m :])
        queue = []
        for i in far_in:
            buf, sem = refs.pop(0), refs.pop(0)
            there = inputs[i]
            if isinstance(args[i], Rows):
                first = pl.multiple_of(lens[2] * 32, 32)
                there = there.at[pl.ds(first, 32)]
            elif args[i].at is not None:
                there = there.at[args[i].at]
            inputs[i] = Loaded(pltpu.make_async_copy(there, buf, sem), buf, queue)
            queue.append(inputs[i])
        for _ in range(min(ahead, len(queue))):
            queue.pop(0).copy.start()
        for k in far_out:
            buf, sems = refs.pop(0), refs.pop(0)
            outputs[k] = Stored(buf, outputs[k], sems, outs[k][2])
        kernel(Place(lens), *scalars, *inputs, *outputs, *refs)
        for i in far_in:
            inputs[i].ready()
        for k in far_out:
            if not outputs[k].copies:
                outputs[k].send()
        for k in far_out:
            for copy in outputs[k].copies:
                copy.wait()

    buffers = []
    for i in far_in:
        buffers += [pltpu.VMEM(args[i].shape(), args[i].value.dtype), pltpu.SemaphoreType.DMA]
    for k in far_out:
        shape, dtype, _ = outs[k]
        buffers += [pltpu.VMEM(shape, dtype), pltpu.SemaphoreType.DMA((24,))]
    placed = [
        pltpu.with_memory_space_constraint(a.value, pltpu.HBM)
        if isinstance(a, Far)
        else pltpu.with_memory_space_constraint(a, pltpu.VMEM)
        for a in args
    ]
    shapes = [
        pltpu.HBM((o[0][0] * o[2], *o[0][1:]), o[1])
        if len(o) == 3
        else pltpu.VMEM(o[0], o[1])
        for o in outs
    ]
    return pl.pallas_call(
        whole,
        out_shape=tuple(shapes),
        in_specs=[pl.BlockSpec(memory_space=pltpu.SMEM)] * fixed
        + [pl.BlockSpec(memory_space=pl.ANY if i in far_in else pltpu.VMEM) for i in range(n)],
        out_specs=tuple(
            pl.BlockSpec(memory_space=pl.ANY if k in far_out else pltpu.VMEM) for k in range(m)
        ),
        scratch_shapes=buffers + list(scratch),
        compiler_params=pltpu.CompilerParams(vmem_limit_bytes=vmem * MIB),
        cost_estimate=pl.CostEstimate(flops=1000, bytes_accessed=1000, transcendentals=0),
        name=name,
    )(lengths, *smem, *placed)


def lane_at(chip, core):
    return pl.multiple_of(chip * 256 + core * 128, 128)


def chunk_p(ref, rows, chip, c):
    return jnp.concatenate(
        [ref[rows, pl.ds(lane_at(chip, c), 128)], ref[rows, pl.ds(lane_at(chip, 1 - c), 128)]],
        axis=1,
    )


def rows_of(half):
    return slice(half * 256, (half + 1) * 256)


def pack_kernel(me, wq, wk, wv, wo, ga, gf, bias, mine, theirs, misc):
    misc[...] = jnp.zeros_like(misc)
    misc[0:1, 0:128] = ga[...].astype(f32)
    misc[0:1, 128:256] = gf[...].astype(f32)
    misc[1:3, 0:4] = bias[...].astype(f32)
    low = jnp.concatenate([wq[:, 0:128], wk[:, 0:128], wv[:, 0:128], wo[0:128, :]], axis=1)
    high = jnp.concatenate(
        [wq[:, 128:256], wk[:, 128:256], wv[:, 128:256], wo[128:256, :]], axis=1
    )
    theirs[0:128, :] = jnp.where(me.c == 0, high, low)
    mine[0:128, :] = jnp.where(me.c == 0, low, high)
    for res in (mine, theirs):
        res[128:144, :] = misc[...].astype(bf16)


def qkv_kernel(me, x_own, x_sib, rows_gain, w_first, w_rest, n1, q, kv, gains):
    c = me.c
    rinvs = []
    for x in (x_own, x_sib):
        total = jnp.zeros((256, 1), f32)
        for k in range(8):
            v = x[:, k * 256 : (k + 1) * 256].astype(f32)
            total = total + jnp.sum(v * v, axis=1, keepdims=True)
        rinvs.append(lax.rsqrt(total * (1.0 / D) + epsilon))
    for k in range(8):
        for core, p in ((0, c), (1, 1 - c)):
            rows = rows_gain[k].astype(f32)
            row = jnp.where(p == 0, rows[0:1], rows[8:9])
            gains[0:1, k * 256 + core * 128 : k * 256 + core * 128 + 128] = row[:, 0:128]
            gains[1:2, k * 256 + core * 128 : k * 256 + core * 128 + 128] = row[:, 128:256]
    gains.send()
    for half, x, rinv in ((0, x_own, rinvs[0]), (1, x_sib, rinvs[1])):
        rows = rows_of(half)
        acc = jnp.zeros((256, 384), f32)
        for k in range(8):
            lanes = slice(k * 256, (k + 1) * 256)
            v = x[:, lanes].astype(f32)
            normed = (v * rinv * gains[0:1, lanes]).astype(bf16)
            n1[rows, lanes] = normed
            w, at = (w_first, k) if k < 2 else (w_rest, k - 2)
            wk = jnp.concatenate(
                [w[at, rows_p(c), :], w[at, rows_p(1 - c), :]], axis=0
            )
            acc = acc + nn(normed, wk)
        q[rows, :] = acc[:, 0:128].astype(bf16)
        kv[rows, :] = acc[:, 128:384].astype(bf16)
        for chip in range(8):
            kv.start(kv.ref.at[rows], kv.there.at[pl.ds(chip * 512 + half * 256, 256)])
        n1.send_part(rows)


def rows_p(p):
    return pl.ds(pl.multiple_of(p * 128, 128), 128)


def out_weights(me, w, k):
    return jnp.concatenate([w[k, rows_p(p)] for p in (me.c, 1 - me.c)], axis=1)


def bucket_ids(offset):
    distance = jnp.abs(offset)
    coarse = 7 + sum(((distance >= threshold).astype(i32) for threshold in limits))
    within = jnp.where(distance < 8, distance, coarse)
    return within + jnp.where(offset > 0, 16, 0).astype(i32)


def band_buckets():
    return bucket_ids(
        lax.broadcasted_iota(i32, (128, 384), 1)
        - 128
        - lax.broadcasted_iota(i32, (128, 384), 0)
    )


def key_places(c):
    lane = lax.broadcasted_iota(i32, (1, D), 1)
    stored = lane // 128
    tile = (stored // 2) * 2 + jnp.where(stored % 2 == 1, 1 - c, c)
    return tile, tile * 128 + lane % 128


def band_tiles(me, half):
    c = me.c
    tile = me.sc * 2 + (c if half == 0 else 1 - c)
    lanes = []
    for step in (-1, 0, 1):
        near = tile + step
        stored = (near // 2) * 2 + jnp.where(near % 2 == 1, 1 - c, c)
        inside = jnp.logical_and(near >= 0, near < 16)
        lanes.append(pl.multiple_of(jnp.where(inside, stored, 16) * 128, 128))
    return tile, lanes


def band_kernel(me, table, band):
    ids = band_buckets()
    for j in range(2):
        value = jnp.zeros((128, 384), f32)
        for b in range(BUCKETS):
            value = jnp.where(ids == b, table[b, j], value)
        band[j] = value


def attend_kernel(me, table, q, kv, band, w, e0, e1, e2, e3, rl, mixed, own, sib, s_ref):
    exps = (e0, e1, e2, e3)
    c = me.c
    tile_of, place_of = key_places(c)
    head_lane = lax.broadcasted_iota(i32, (256, 128), 1) // HEAD
    for b in range(2):
        length = me.lengths[b]
        keys = kv[:, b, :, 0:128].reshape(D, 128)
        values = jnp.concatenate(
            [kv[:, b, :, 128:256].reshape(D, 128), jnp.ones((D, 128), bf16)], axis=1
        )
        queries = q[:, b].reshape(256, 128)
        together = jnp.zeros((256, 128), f32)
        for j in range(2):
            mine = jnp.where(head_lane == j, queries, jnp.zeros_like(queries))
            s_ref[:, 0:D] = nt(mine, keys)
            for half in range(2):
                tile, lanes = band_tiles(me, half)
                rows = slice(half * 128, (half + 1) * 128)
                for t in range(3):
                    at = pl.ds(lanes[t], 128)
                    s_ref[rows, at] = s_ref[rows, at] + band[j, :, t * 128 : (t + 1) * 128]
                added = jnp.where(place_of >= length, masked_score, 0.0) + jnp.where(
                    tile_of < tile - 1,
                    table[15, j],
                    jnp.where(tile_of > tile + 1, table[31, j], 0.0),
                )

                def some_rows(i, carry, half=half, added=added, b=b, j=j):
                    at = pl.ds(pl.multiple_of(half * 128 + i * 16, 16), 16)
                    s = s_ref[at, 0:D] + added
                    exps[b * 2 + j][at, :] = jnp.exp(
                        s - jnp.max(s, axis=1, keepdims=True)
                    ).astype(bf16)
                    return carry

                lax.fori_loop(0, 8, some_rows, 0, unroll=8)
            exps[b * 2 + j].send()
            wide = nn(exps[b * 2 + j][...], values)
            inverse = 1.0 / wide[:, 128:129]
            rl[b * 2 + j] = inverse
            together = jnp.where(head_lane == j, wide[:, 0:128] * inverse, together)
        mixed[:, b] = together.astype(bf16).reshape(2, 128, 128)
    rl.send()
    mixed.send()
    for half, res in ((1, sib), (0, own)):
        for k in range(8):
            res[:, k * 256 : (k + 1) * 256] = nn(
                mixed[half].reshape(256, 128), out_weights(me, w, k)
            ).astype(bf16)


def attend_back_kernel(
    me, w, al_own, al_sib, q, kv, rl, e0, e1, e2, e3, dq, dkv, band, far_out, d_ref, ds_ref, mg
):
    exps = (e0, e1, e2, e3)
    c = me.c
    for half, al in ((0, al_own), (1, al_sib)):
        acc = jnp.zeros((256, 128), f32)
        for k in range(8):
            acc = acc + nt(al[:, k * 256 : (k + 1) * 256], out_weights(me, w, k))
        mg[half] = acc.astype(bf16).reshape(2, 128, 128)
    tile_of, _ = key_places(c)
    head_lane = lax.broadcasted_iota(i32, (256, 128), 1) // HEAD
    ds_ref[:, D : D + 128] = jnp.zeros((256, 128), bf16)
    band[...] = jnp.zeros_like(band)
    far = [[jnp.zeros((1, D), f32) for _ in range(2)] for _ in range(2)]
    row16 = lax.broadcasted_iota(i32, (16, 256), 0)
    lane256 = lax.broadcasted_iota(i32, (16, 256), 1)
    marks = (row16 == lane256 // 128).astype(f32).astype(bf16)
    for b in range(2):
        keys = kv[:, b, :, 0:128].reshape(D, 128)
        values = kv[:, b, :, 128:256].reshape(D, 128)
        queries = q[:, b].reshape(256, 128)
        turned = queries.astype(f32).T.astype(bf16)
        grads = mg[:, b].reshape(256, 128).astype(f32)
        together = jnp.zeros((256, 128), f32)
        for j in range(2):
            inverse = rl[b * 2 + j]
            e = exps[b * 2 + j].ready()
            scaled = jnp.where(head_lane == j, grads * inverse, 0.0)
            mine = scaled.astype(bf16)
            d_ref[...] = nt(mine, values)

            def some_rows(i, carry, b=b, j=j, e=e):
                at = pl.ds(pl.multiple_of(i * 16, 16), 16)
                p = e[at, :].astype(f32)
                d = d_ref[at, :]
                inner = jnp.sum(p * d, axis=1, keepdims=True) * rl[b * 2 + j, at, :]
                ds_ref[at, 0:D] = (p * (d - inner)).astype(bf16)
                return carry

            lax.fori_loop(0, 16, some_rows, 0, unroll=16)
            score_grad = ds_ref[:, 0:D]
            together = jnp.where(head_lane == j, nn(score_grad, keys), together)
            left = jnp.concatenate([turned[j * HEAD : (j + 1) * HEAD, :], marks], axis=0)
            key_t = nn(left, score_grad)
            value_t = nn(scaled.T[j * HEAD : (j + 1) * HEAD, :].astype(bf16), e[...])
            for chip in range(8):
                lanes = slice(chip * 256, (chip + 1) * 256)
                at = chip * 256 + j * HEAD
                dkv[at : at + HEAD, b * 256 : (b + 1) * 256] = key_t[0:HEAD, lanes].astype(bf16)
                dkv[at + 128 : at + 128 + HEAD, b * 256 : (b + 1) * 256] = value_t[
                    :, lanes
                ].astype(bf16)
            for half in range(2):
                tile, lanes = band_tiles(me, half)
                rows = slice(half * 128, (half + 1) * 128)
                for t in range(3):
                    cols = slice(t * 128, (t + 1) * 128)
                    band[j, :, cols] = band[j, :, cols] + ds_ref[
                        rows, pl.ds(lanes[t], 128)
                    ].astype(f32)
                line = key_t[HEAD + half : HEAD + half + 1, :]
                far[j][0] = far[j][0] + jnp.where(tile_of < tile - 1, line, 0.0)
                far[j][1] = far[j][1] + jnp.where(tile_of > tile + 1, line, 0.0)
        dq[:, b] = together.astype(bf16).reshape(2, 128, 128)
        dkv.send_part((slice(None), pl.ds(b * 256, 256)))
    for j in range(2):
        for side in range(2):
            far_out[2 * j + side : 2 * j + side + 1, :] = far[j][side]


def table_kernel(me, band, far, tab):
    ids = band_buckets()
    lane = lax.broadcasted_iota(i32, (BUCKETS, 128), 1)
    bucket = lax.broadcasted_iota(i32, (BUCKETS, 1), 0)
    result = jnp.zeros((BUCKETS, 128), f32)
    for j in range(2):
        near = band[j]
        lines = [
            jnp.sum(jnp.where(ids == b, near, 0.0), axis=0, keepdims=True) for b in range(BUCKETS)
        ]
        column = jnp.sum(jnp.concatenate(lines, axis=0), axis=1, keepdims=True)
        sides = [jnp.sum(far[2 * j + k : 2 * j + k + 1, :], axis=1, keepdims=True) for k in (0, 1)]
        column = column + jnp.where(bucket == 15, sides[0], 0.0)
        column = column + jnp.where(bucket == 31, sides[1], 0.0)
        result = jnp.where(lane == j, column, result)
    tab[...] = result


def summed(parts, first, rows):
    total = parts[first : first + rows, :].astype(f32)
    for k in range(1, 8):
        total = total + parts[k * 32 + first : k * 32 + first + rows, :].astype(f32)
    return total


def spread_rows(res, first, rows, value):
    at = pl.ds(first, rows)
    res[at, :] = value.astype(bf16)
    size = res.ref.shape[0]
    for t in range(res.times):
        res.start(res.ref.at[at], res.there.at[pl.ds(t * size + first, rows)])


def norm_two_kernel(me, parts, x, gains, hid, normed):
    for first in (0, 16):
        rows = slice(first, first + 16)
        hidden_in = summed(parts, first, 16) + x[rows, :].astype(f32)
        rinv = lax.rsqrt(jnp.mean(hidden_in * hidden_in, axis=1, keepdims=True) + epsilon)
        spread_rows(normed, first, 16, hidden_in * rinv * gains[1:2, :])
        hid[rows, :] = hidden_in


def norm_back(value, grad, gain):
    rinv = lax.rsqrt(jnp.mean(value * value, axis=1, keepdims=True) + epsilon)
    u = grad * gain
    return rinv * u - (rinv * rinv * rinv) * value * jnp.mean(u * value, axis=1, keepdims=True)


def live_rows(me, half, b, first, count):
    c = me.c
    core = c if half == 0 else 1 - c
    place = (me.sc * 2 + core) * 128 + first + lax.broadcasted_iota(i32, (count, 1), 0)
    return place < me.lengths[b]


def norm_two_back_kernel(me, parts, hid, cot, gains, hig, low):
    b = me.h // 4
    for first in (0, 16):
        rows = slice(first, first + 16)
        place = (
            (me.sc * 2 + me.c) * 128
            + (me.h - b * 4) * 32
            + first
            + lax.broadcasted_iota(i32, (16, 1), 0)
        )
        total = summed(parts, first, 16)
        grad = norm_back(hid[rows, :], total, gains[1:2, :])
        grad = grad + jnp.where(place < jnp.where(b == 0, me.lengths[0], me.lengths[1]), cot[rows, :].astype(f32), 0.0)
        spread_rows(low, first, 16, grad)
        hig[rows, :] = grad


def norm_one_back_kernel(me, parts, x, gains, hig, res):
    for first in (0, 16):
        rows = slice(first, first + 16)
        total = summed(parts, first, 16)
        grad = norm_back(x[rows, :].astype(f32), total, gains[0:1, :]) + hig[rows, :]
        spread_rows(res, first, 16, grad)


def gelu_pair(g):
    k0, k1 = 0.7978845608028654, 0.044715
    g2 = g * g
    t = jnp.tanh(k0 * g * (1.0 + k1 * g2))
    value = 0.5 * g * (1.0 + t)
    slope = 0.5 * (1.0 + t) + 0.5 * g * (1.0 - t * t) * k0 * (1.0 + 3.0 * k1 * g2)
    return value, slope


def gate_up(w):
    wide = jnp.concatenate([w[320:576, :], w[576:832, :]], axis=1)
    rest = jnp.concatenate([w[832:960, 0:128], w[832:960, 128:256]], axis=0)
    return wide, rest


def live_cotangent(me, out_low, cot_own, cot_sib):
    for half, cot in ((0, cot_own), (1, cot_sib)):
        live = jnp.concatenate([live_rows(me, half, b, 0, 128) for b in range(2)], axis=0)
        out_low[rows_of(half), :] = jnp.where(live, cot[...], jnp.zeros((), bf16))


def weight_grad(me, k, res, hidden, grads, n_own, n_sib, gu_low):
    chip, c = me.idx[k], me.c
    res[0:320, :] = tn(hidden[...], grads).astype(bf16)
    v = jnp.concatenate(
        [chunk_p(n_own, slice(None), chip, c), chunk_p(n_sib, slice(None), chip, c)], axis=0
    )
    part = tn(v, gu_low[...]).astype(bf16)
    res[320:576, :] = part[:, 0:256]
    res[576:832, :] = part[:, 256:512]
    res[832:960, 0:128] = part[0:128, 512:640]
    res[832:960, 128:256] = part[128:256, 512:640]
    res.send()


def ffn_early_kernel(me, cot_own, cot_sib, *refs):
    blocks, (back, grads, out_low) = refs[:6], refs[6:]
    live_cotangent(me, out_low, cot_own, cot_sib)
    for k in (6, 7):
        grads[:, (k - 6) * 256 : (k - 5) * 256] = chunk_p(out_low, slice(None), me.idx[k], me.c)
    grads.send()
    total = jnp.zeros((512, FFC), f32)
    for k in range(6):
        total = total + nt(chunk_p(out_low, slice(None), me.idx[k], me.c), blocks[k][...])
    back[...] = total


def ffn_kernel(me, n_own, n_sib, *refs):
    blocks, (back, grads, gains), results = refs[:8], refs[8:11], refs[11:]
    hidden, gu_low, own, sib, out_own, out_sib, gain_sum, far_a, far_b = results
    c = me.c
    all_rows = slice(None)

    def tokens(chip):
        return jnp.concatenate(
            [chunk_p(n_own, all_rows, chip, c), chunk_p(n_sib, all_rows, chip, c)], axis=0
        )

    gu = jnp.zeros((512, 512), f32)
    rest = jnp.zeros((512, 128), f32)
    for k in range(8):
        if k == 2:
            for a in (*blocks[2:], back, grads, gains):
                a.ready()
        v = tokens(me.idx[k])
        wide, last = gate_up(blocks[k])
        gu = gu + nn(v, wide)
        rest = rest + nn(v, last)
    total = back[...]
    for k in (6, 7):
        total = total + nt(grads[:, (k - 6) * 256 : (k - 5) * 256], blocks[k][0:320, :])
    for gate, up, dh, at, size in (
        (gu[:, 0:256], gu[:, 256:512], total[:, 0:256], 0, 256),
        (rest[:, 0:64], rest[:, 64:128], total[:, 256:FFC], 256, 64),
    ):
        value, slope = gelu_pair(gate)
        hidden[:, at : at + size] = (value * up).astype(bf16)
        at = 2 * at
        gu_low[:, at : at + size] = (dh * up * slope).astype(bf16)
        gu_low[:, at + size : at + 2 * size] = (dh * value).astype(bf16)
    hidden.send()
    gu_low.send()
    for k, res in ((6, far_a), (7, far_b)):
        chunk = grads[:, (k - 6) * 256 : (k - 5) * 256]
        weight_grad(me, k, res, hidden, chunk, n_own, n_sib, gu_low)
    for k in range(8):
        chip = me.idx[k]
        wide, last = gate_up(blocks[k])
        part = nt(gu_low[:, 0:512], wide) + nt(gu_low[:, 512:640], last)
        made = nn(hidden[...], blocks[k][0:320, :])
        line = jnp.sum(part * tokens(chip).astype(f32), axis=0, keepdims=True)
        for p, core in ((0, c), (1, 1 - c)):
            lanes = pl.ds(lane_at(chip, core), 128)
            cols = slice(p * 128, (p + 1) * 128)
            gain_sum[0:1, lanes] = line[:, cols] / gains[1:2, lanes]
            for half, res, out in ((0, own, out_own), (1, sib, out_sib)):
                res[:, lanes] = part[rows_of(half), cols].astype(bf16)
                out[:, lanes] = made[rows_of(half), cols].astype(bf16)


def ffn_weights_kernel(me, cot_own, cot_sib, hidden, n_own, n_sib, gu_low, *results, ranks):
    *results, out_low = results
    live_cotangent(me, out_low, cot_own, cot_sib)
    for k, res in zip(ranks, results):
        grads = chunk_p(out_low, slice(None), me.idx[k], me.c)
        weight_grad(me, k, res, hidden, grads, n_own, n_sib, gu_low)


def layer_join_kernel(me, own, recv, hid, res):
    res[...] = (own[...].astype(f32) + recv[...].astype(f32)).astype(bf16)
    at = pl.ds(pl.multiple_of(me.h * 32, 32), 32)
    res[at, :] = (own[at, :].astype(f32) + recv[at, :].astype(f32) + hid[...]).astype(bf16)


def qkv_back_kernel(me, parts, q_low, w, n1, gains, kv_low, own, sib, gain_sum):
    c = me.c
    total = parts[0:256, :].astype(f32)
    for k in range(1, 8):
        total = total + parts[k * 256 : (k + 1) * 256, :].astype(f32)
    for b in range(2):
        for half in range(2):
            lanes = slice(b * 256 + half * 128, b * 256 + (half + 1) * 128)
            kv_low[half * 256 + b * 128 : half * 256 + (b + 1) * 128, :] = total[:, lanes].T.astype(
                bf16
            )
    for k in range(8):
        wk = jnp.concatenate(
            [
                w[k, rows_p(p), 0:384]
                for p in (c, 1 - c)
            ],
            axis=0,
        )
        lanes = slice(k * 256, (k + 1) * 256)
        line = jnp.zeros((1, 256), f32)
        for half, res in ((0, own), (1, sib)):
            rows = rows_of(half)
            part = nt(q_low[rows, :], wk[:, 0:128]) + nt(kv_low[rows, :], wk[:, 128:384])
            line = line + jnp.sum(part * n1[rows, lanes].astype(f32), axis=0, keepdims=True)
            res[:, lanes] = part.astype(bf16)
        gain_sum[0:1, lanes] = line / gains[0:1, lanes]


def early_weights_kernel(me, n1, q_low, mixed, al_own, al_sib, *results):
    c = me.c
    for k in range(8):
        chip = me.idx[k]
        res = results[k // 2].at[k % 2]
        al = jnp.concatenate(
            [chunk_p(al_own, slice(None), chip, c), chunk_p(al_sib, slice(None), chip, c)], axis=0
        )
        res[0:128, :] = tn(mixed[...], al).astype(bf16)
        part = tn(chunk_p(n1, slice(None), chip, c), q_low[...]).astype(bf16)
        res[128:256, 0:128] = part[0:128]
        res[128:256, 128:256] = part[128:256]
        if k % 2:
            results[k // 2].send()


def last_weights_kernel(me, n1, kv_low, g1, g2, tab, *results):
    c = me.c
    for k in (6, 7, 5, 2, 4, 3, 0, 1):
        chip = me.idx[k]
        res = results[k]
        part = tn(chunk_p(n1, slice(None), chip, c), kv_low[...]).astype(bf16)
        for p in range(2):
            rows, lanes = slice(p * 128, (p + 1) * 128), slice(p * 128, (p + 1) * 128)
            res[0:128, lanes] = part[rows, 0:128]
            res[128:256, lanes] = part[rows, 128:256]
        one = slice(0, 1)
        misc = jnp.concatenate(
            [
                chunk_p(g1, one, chip, c),
                chunk_p(g2, one, chip, c),
                tab[pl.ds(chip, 1), :],
                jnp.zeros((13, 256), f32),
            ],
            axis=0,
        )
        res[256:272, :] = misc.astype(bf16)
        res.send()


def unpack_kernel(me, rows, input_grad):
    for k in range(4):
        at = slice(k * 64, (k + 1) * 64)
        input_grad[at, :] = rows[at, :].astype(f32)
        input_grad.send_part(at)


def layer_place_kernel(me, *refs):
    parts, res = refs[:4], refs[4]
    x, y = me.h // 2, me.h % 2
    for part, step in zip(parts, (0, 1, 3, 2)):
        from_x = (x + 4 - step) % 4
        for k, from_y in ((0, y), (1, 1 - y)):
            at = pl.ds(pl.multiple_of((from_x * 2 + from_y) * 32, 32), 32)
            res[at, :] = part[k * 32 : (k + 1) * 32, :]


def layer_sum_kernel(me, parts, res):
    res[...] = summed(parts, 0, 32).astype(bf16)


def ffn_sum_kernel(me, *refs):
    parts, results = refs[:6], refs[6:]
    for y, res in enumerate(results):
        value = parts[y][...].astype(f32)
        for a in parts[2 + y :: 2]:
            value = value + a[...].astype(f32)
        res[...] = value.astype(res.ref.dtype)
        res.send()


def last_sum_kernel(me, *refs):
    early, late, (own, other) = refs[:4], refs[4:10], refs[10:]
    for y, res in ((1, other), (0, own)):
        value = early[0][y].astype(f32)
        for a in early[1:]:
            value = value + a[y].astype(f32)
        res[0:256, :] = value.astype(f32 if y == 0 else bf16)
        value = late[y][...].astype(f32)
        for a in late[2 + y :: 2]:
            value = value + a[...].astype(f32)
        res[256:528, :] = value.astype(f32 if y == 0 else bf16)


def last_split_kernel(me, own, recv, mine, theirs):
    total = own[...] + recv[...].astype(f32)
    for p, res in ((0, mine), (1, theirs)):
        cols = slice(p * 128, (p + 1) * 128)
        parts = [total[k * 128 : (k + 1) * 128, cols] for k in range(4)]
        value = jnp.concatenate(parts, axis=1)
        res[0:128, :] = value.astype(bf16 if p else f32)
        value = jnp.concatenate([total[512:528, cols]] * 4, axis=1)
        res[128:144, :] = value.astype(bf16 if p else f32)


def gain_kernel(me, mine, recv, res):
    a, b = mine[128:144, 0:128], recv[128:144, 0:128].astype(f32)
    res[...] = jnp.concatenate([a[0:2] + b[0:2], a[2:3], b[2:3], a[4:8]], axis=0)


def ffn_split_kernel(me, own, recv, mine, theirs):
    for p, res in ((1, theirs), (0, mine)):
        lanes = slice(p * 128, (p + 1) * 128)
        rows = [(0, 320, lanes)]
        for first in (320, 576):
            rows += [(first + p * 128, 128, slice(0, 128)), (first + p * 128, 128, slice(128, 256))]
        rows.append((832, 128, lanes))
        at = 0
        for first, size, cols in rows:
            value = own[first : first + size, cols] + recv[first : first + size, cols].astype(f32)
            res[at : at + size, :] = value.astype(bf16 if p else f32)
            at += size


def ffn_order_kernel(me, mine, recv, gate_grad, up_grad, down_grad):
    first = me.c == 0
    a, b = mine[0:320, :], recv[0:320, :].astype(f32)
    down_grad[0:320, :] = jnp.where(first, a, b)
    down_grad[320:640, :] = jnp.where(first, b, a)
    down_grad.send()
    for at, lane, res in ((320, 0, gate_grad), (576, 64, up_grad)):
        sides = []
        for ref in (mine, recv):
            rest = ref[832:960, lane : lane + 64]
            sides.append(
                jnp.concatenate([ref[at : at + 128, :], ref[at + 128 : at + 256, :], rest], axis=1)
            )
        a, b = sides[0], sides[1].astype(f32)
        res[...] = jnp.concatenate([jnp.where(first, a, b), jnp.where(first, b, a)], axis=1)
        res.send()


def last_order_kernel(me, mine, recv, out_grad, query_grad, key_grad, value_grad):
    a, b = mine[0:128, :], recv[0:128, :].astype(f32)
    low, high = jnp.where(me.c == 0, a, b), jnp.where(me.c == 0, b, a)
    out_grad[0:128, :] = low[:, 0:128]
    out_grad[128:256, :] = high[:, 0:128]
    for k, res in ((1, query_grad), (2, key_grad), (3, value_grad)):
        cols = slice(k * 128, (k + 1) * 128)
        res[:, 0:128] = low[:, cols]
        res[:, 128:256] = high[:, cols]


def to_sibling(a):
    return lax.ppermute(a, "seq", CORE)


def over_head(a):
    return lax.all_to_all(a, "head", 0, 0, tiled=True)


def over_chips(a):
    return lax.all_to_all(a, "seq", 0, 0, axis_index_groups=CHIP_GROUPS, tiled=True)


def body(
    inputs,
    cotangent,
    lengths,
    attn_gain,
    w_query,
    w_key,
    w_value,
    w_out,
    bias_table,
    ffn_gain,
    w_gate,
    w_up,
    w_down,
):
    s = lax.axis_index("seq")
    first = s % 2 == 0
    scalars = place_scalars(lengths)

    def halves(a, axis):
        low, high = jnp.split(a, 2, axis=axis)
        return jnp.where(first, low, high), jnp.where(first, high, low)

    def in_order(own, sib, axis):
        return jnp.where(
            first,
            jnp.concatenate([own, sib], axis=axis),
            jnp.concatenate([sib, own], axis=axis),
        )

    def on(kernel, outs, *args, **more):
        return call(kernel, outs, scalars, *args, **more)

    mine, theirs = on(
        pack_kernel,
        [((144, 512), bf16)] * 2,
        Far(w_query),
        Far(w_key),
        Far(w_value),
        Far(w_out),
        Far(attn_gain.reshape(1, 128)),
        Far(ffn_gain.reshape(1, 128)),
        Far(bias_table),
        scratch=[pltpu.VMEM((16, 512), f32)],
        name="pack",
    )
    recv = to_sibling(theirs)
    block = jnp.concatenate([mine[0:128], recv[0:128], mine[128:136], recv[128:136]], axis=0)
    w_attn = over_chips(jnp.broadcast_to(block[None], (8, 272, 512)).reshape(8 * 272, 512))
    w_attn = w_attn.reshape(8, 272, 512)

    x_own = inputs.reshape(256, D)
    x_sib = to_sibling(x_own)
    cot_own = cotangent.reshape(256, D)
    cot_sib = to_sibling(cot_own)

    down_mine, down_theirs = halves(w_down, 0)
    gate_mine, gate_theirs = halves(w_gate, 1)
    up_mine, up_theirs = halves(w_up, 1)

    def joined(gate, up):
        return jnp.concatenate(
            [gate[:, 0:256], up[:, 0:256], gate[:, 256:FFC], up[:, 256:FFC]], axis=1
        )

    gu_mine = joined(gate_mine, up_mine)
    down_recv = to_sibling(down_theirs)
    gu_recv = to_sibling(joined(gate_theirs, up_theirs))
    block = jnp.concatenate(
        [
            jnp.concatenate([down_mine, down_recv], axis=1),
            jnp.concatenate([gu_mine[:, 0:256], gu_recv[:, 0:256]], axis=0),
            jnp.concatenate([gu_mine[:, 256:512], gu_recv[:, 256:512]], axis=0),
            jnp.concatenate([gu_mine[:, 512:640], gu_recv[:, 512:640]], axis=1),
        ],
        axis=0,
    )

    def with_sibling(own, sib):
        return (own.astype(f32) + to_sibling(sib).astype(f32)).astype(bf16)

    def along_z(a, steps):
        return lax.ppermute(a, "seq", ALONG_Z[steps % 4])

    def other_y(a):
        return lax.ppermute(a, "seq", OTHER_Y)

    tie = lax.optimization_barrier
    half, part, line = ((256, D), bf16), ((256, D), bf16), ((1, D), f32)

    n1, q, kv, gains = on(
        qkv_kernel,
        [((512, D), bf16, 1), ((512, 128), bf16, 1), ((512, 256), bf16, 8), ((2, D), f32, 1)],
        x_own,
        Far(x_sib),
        Far(w_attn, (slice(None), pl.ds(256, 16), pl.ds(0, 256))),
        Far(w_attn, (pl.ds(0, 2), pl.ds(0, 256), pl.ds(0, 384))),
        Far(w_attn, (pl.ds(2, 6), pl.ds(0, 256), pl.ds(0, 384))),
        vmem=16,
        name="qkv",
    )
    q = q.reshape(2, 2, 128, 128)
    rows = w_attn[:, 256:272, 0:4].reshape(8, 2, 8, 4)[:, :, 1:3].astype(f32)
    rows = jnp.where(first, rows, rows[:, ::-1]).reshape(BUCKETS, 4)
    table = jnp.where(first, rows[:, 0:2], rows[:, 2:4])
    (band,) = on(band_kernel, [((2, 128, 384), f32)], smem=(table,), name="band")
    kv, block, band = tie((over_chips(kv), block, band))
    kv = kv.reshape(16, 2, 128, 256)
    w_parts = Far(w_attn, (slice(None), pl.ds(0, 256), pl.ds(384, 128)))
    *exps, rl, mixed, own, sib = on(
        attend_kernel,
        [((256, D), bf16, 1)] * 4 + [((4, 256, 1), f32, 1), ((2, 2, 128, 128), bf16, 1), half, half],
        Far(q),
        Far(kv),
        band,
        w_parts,
        smem=(table,),
        scratch=[pltpu.VMEM((256, D + 128), f32)],
        vmem=24, name="attend",
    )
    mixed = mixed.reshape(512, 128)
    flipped = other_y(block)
    sib, flipped, up_a, down_a = tie((sib, flipped, along_z(block, 1), along_z(block, 3)))
    attn, flipped = tie((with_sibling(own, sib), flipped))
    attn = over_head(attn)
    up_b, down_b = along_z(flipped, 1), along_z(flipped, 3)
    hid, n2 = on(
        norm_two_kernel,
        [((32, D), f32, 1), ((32, D), bf16, 8)],
        attn,
        Rows(x_own),
        Far(gains),
        name="norm_two",
    )
    n2, up_a, up_b, down_b = tie((n2, up_a, up_b, down_b))
    blocks = [block, flipped, up_a, up_b, down_a, down_b]
    down_rows = (pl.ds(0, 320), slice(None))
    back, grads = on(
        ffn_early_kernel,
        [((512, FFC), f32, 1), ((512, 512), bf16, 1)],
        Far(cot_own),
        Far(cot_sib),
        *[Far(a, down_rows) for a in blocks],
        scratch=[pltpu.VMEM((512, D), bf16)],
        vmem=16,
        name="ffn_early",
    )
    n_own, far_a, far_b, back, grads = tie(
        (over_head(n2), along_z(up_a, 1), along_z(down_b, 3), back, grads)
    )
    blocks += [far_a, far_b]
    n_sib = to_sibling(n_own)

    hidden, gu_low, own, sib, out_own, out_sib, g2, far_a, far_b = on(
        ffn_kernel,
        [
            ((512, FFC), bf16, 1),
            ((512, 640), bf16, 1),
            part,
            part,
            part,
            part,
            line,
            ((960, 256), bf16, 1),
            ((960, 256), bf16, 1),
        ],
        n_own,
        n_sib,
        *[Far(a) for a in blocks],
        Far(back),
        Far(grads),
        Far(gains),
        vmem=28,
        name="ffn",
    )

    def weight_grads(name, ranks):
        return on(
            functools.partial(ffn_weights_kernel, ranks=ranks),
            [((960, 256), bf16, 1)] * len(ranks),
            Far(cot_own),
            Far(cot_sib),
            Far(hidden),
            Far(n_own),
            Far(n_sib),
            Far(gu_low),
            scratch=[pltpu.VMEM((512, D), bf16)],
            vmem=18,
            name=name,
        )

    fore_a, back_b, fore_b, back_a = weight_grads("ffn_weights_next", (4, 3, 5, 2))
    (out_own,) = on(
        layer_join_kernel, [part], out_own, to_sibling(out_sib), Far(hid), name="layer_join"
    )
    ffn_sum, fore_recv, back_recv, fore_a, back_b, fore_b, back_a = tie(
        (
            over_head(with_sibling(own, sib)),
            along_z(far_a, 1),
            along_z(far_b, 3),
            fore_a,
            back_b,
            fore_b,
            back_a,
        )
    )
    hig, low = on(
        norm_two_back_kernel,
        [((32, D), f32, 1), ((32, D), bf16, 8)],
        ffn_sum,
        Far(hid),
        Rows(cot_own),
        Far(gains),
        name="norm_two_back",
    )
    low, fore_recv, back_recv = tie((low, fore_recv, back_recv))
    fore_a = (fore_a.astype(f32) + fore_recv.astype(f32)).astype(bf16)
    back_b = (back_b.astype(f32) + back_recv.astype(f32)).astype(bf16)
    al_own, fore_a, back_b, fore_b, back_a, out_own = tie(
        (over_head(low), along_z(fore_a, 1), along_z(back_b, 3), fore_b, back_a, out_own)
    )
    al_sib = to_sibling(al_own)

    out_parts = over_head(out_own)
    q_low, dkv, near_sums, far_sums = on(
        attend_back_kernel,
        [
            ((2, 2, 128, 128), bf16, 1),
            ((8 * 256, 512), bf16, 1),
            ((2, 128, 384), f32),
            ((4, D), f32),
        ],
        w_parts,
        al_own,
        al_sib,
        Far(q),
        Far(kv),
        Far(rl),
        *[Far(e) for e in exps],
        scratch=[
            pltpu.VMEM((256, D), f32),
            pltpu.VMEM((256, D + 128), bf16),
            pltpu.VMEM((2, 2, 128, 128), bf16),
        ],
        vmem=28, name="attend_back",
    )
    dkv, out_parts, fore_b, back_a = tie(
        (dkv, out_parts, along_z(fore_b, 1), along_z(back_a, 3))
    )
    q_low = q_low.reshape(512, 128)

    (layer_out,) = on(layer_sum_kernel, [((32, D), bf16)], out_parts, name="layer_sum")
    (tab,) = on(table_kernel, [((BUCKETS, 128), f32)], near_sums, far_sums, name="table")
    early = on(
        early_weights_kernel,
        [((2, 256, 256), bf16, 1)] * 4,
        Far(n1),
        Far(q_low),
        Far(mixed),
        Far(al_own),
        Far(al_sib),
        vmem=14,
        name="early_weights",
    )
    near_a, near_b = weight_grads("ffn_weights_near", (0, 1))
    ffn_own, ffn_other = on(
        ffn_sum_kernel,
        [((960, 256), f32, 1), ((960, 256), bf16, 1)],
        *[Far(a) for a in (near_a, near_b, fore_a, fore_b, back_a, back_b)],
        vmem=12,
        name="ffn_sum",
    )
    kv_parts, tab, layer_out, ffn_own, ffn_other, *early = tie(
        (over_chips(dkv), tab, layer_out, ffn_own, ffn_other, *early)
    )
    kv_low, own, sib, g1 = on(
        qkv_back_kernel,
        [((512, 256), bf16, 1), part, part, line],
        kv_parts,
        Far(q_low),
        Far(w_attn),
        Far(n1),
        Far(gains),
        vmem=16,
        name="qkv_back",
    )

    rows = tab[:, 0:2].reshape(8, 2, 4)
    rows = jnp.where(first, rows, rows[:, ::-1])
    rows = jnp.pad(rows, ((0, 0), (0, 0), (0, 124))).reshape(8, 256)
    near_a, near_b, back_a, back_b, fore_a, fore_b, far_a, far_b = on(
        last_weights_kernel,
        [((272, 256), bf16, 1)] * 8,
        Far(n1),
        Far(kv_low),
        g1,
        g2,
        rows,
        vmem=14,
        name="last_weights",
    )

    def gathered(near, back, fore, far):
        return near, along_z(fore, 1), along_z(back, 3), along_z(far, 2)

    one_sum, *early = tie((over_head(with_sibling(own, sib)), *gathered(*early)))
    ffn_recv = other_y(ffn_other)
    (low,) = on(
        norm_one_back_kernel,
        [((32, D), bf16, 8)],
        one_sum,
        Rows(x_own),
        Far(gains),
        Far(hig),
        name="norm_one_back",
    )
    fore_recv, back_recv = along_z(far_a, 1), along_z(far_b, 3)
    low, fore_recv, back_recv, fore_b, back_a = tie(
        (low, fore_recv, back_recv, along_z(fore_b, 1), along_z(back_a, 3))
    )
    fore_a = (fore_a.astype(f32) + fore_recv.astype(f32)).astype(bf16)
    back_b = (back_b.astype(f32) + back_recv.astype(f32)).astype(bf16)
    fore_a, back_b = along_z(fore_a, 1), along_z(back_b, 3)
    low, layer_out, ffn_recv = tie((low, layer_out, ffn_recv))
    both = over_head(low)
    layer_recv = lax.ppermute(layer_out, "head", OTHER_HEAD_Y)
    layer_pair = jnp.concatenate([layer_out, layer_recv], axis=0)
    last_own, last_other = on(
        last_sum_kernel,
        [((528, 256), f32), ((528, 256), bf16)],
        *[Far(a) for a in (*early, near_a, near_b, fore_a, fore_b, back_a, back_b)],
        name="last_sum",
    )
    mine, theirs = on(
        last_split_kernel,
        [((144, 512), f32), ((144, 512), bf16)],
        last_own,
        other_y(last_other),
        name="last_split",
    )
    recv = to_sibling(theirs)
    (small,) = on(gain_kernel, [((8, 128), f32)], mine, recv, name="gain")
    both, small, *layer_pairs = tie(
        (both, small, *[lax.ppermute(layer_pair, "head", ALONG_X[d]) for d in (1, 3, 2)])
    )
    small_sums = over_head(jnp.broadcast_to(small[None], (8, 8, 128)).reshape(64, 128))
    (input_grad,) = on(unpack_kernel, [((256, D), f32, 1)], Far(both), name="unpack")
    (layer_out,) = on(
        layer_place_kernel,
        [((256, D), bf16, 1)],
        Far(layer_pair),
        *[Far(a) for a in layer_pairs],
        name="layer_place",
    )
    gain_sums = small_sums.reshape(8, 8, 128)[:, 0:2].sum(0)
    out_grad, query_grad, key_grad, value_grad = on(
        last_order_kernel,
        [((256, 128), f32, 1)] + [((128, 256), f32, 1)] * 3,
        mine,
        recv,
        name="last_order",
    )
    table_grad = in_order(small[2, 0:4].reshape(2, 2), small[3, 0:4].reshape(2, 2), 1)

    mine, theirs = on(
        ffn_split_kernel,
        [((960, 128), f32), ((960, 128), bf16)],
        Far(ffn_own),
        ffn_recv,
        name="ffn_split",
    )
    gate_grad, up_grad, down_grad = on(
        ffn_order_kernel,
        [((128, 640), f32, 1), ((128, 640), f32, 1), ((640, 128), f32, 1)],
        mine,
        to_sibling(theirs),
        name="ffn_order",
    )
    return (
        layer_out.reshape(2, 128, D),
        input_grad.reshape(2, 128, D),
        gain_sums[0],
        query_grad,
        key_grad,
        value_grad,
        out_grad,
        table_grad,
        gain_sums[1],
        gate_grad,
        up_grad,
        down_grad,
    )


def solution(mesh):
    seq_head, head_seq = P("seq", "head"), P("head", "seq")
    in_specs = (
        P(None, "seq", None),
        P(None, "seq", None),
        P(),
        P("seq"),
        seq_head,
        seq_head,
        seq_head,
        head_seq,
        seq_head,
        P("seq"),
        seq_head,
        seq_head,
        head_seq,
    )
    out_specs = (
        P(None, "seq", None),
        P(None, "seq", None),
        P("seq"),
        seq_head,
        seq_head,
        seq_head,
        head_seq,
        seq_head,
        P("seq"),
        seq_head,
        seq_head,
        head_seq,
    )
    return jax.shard_map(body, mesh=mesh, in_specs=in_specs, out_specs=out_specs, check_vma=False)
```
